32 devices in a mesh: band: 4 (over x, core), pw: 8 (over z, y).
Axes of the slice: x: 2, y: 2, z: 4, core: 2. Of those that a mesh axis runs over, the one named last changes fastest.
Arguments:
- coeffs: bfloat16 [2, 64, 256, 256], P(None, None, ('band', 'pw')), may hold values from -6 to 6
- rotation_matrix: bfloat16 [2, 64, 8], replicated, may hold values from -0.5 to 0.5
- stick_length: int32 [256], replicated, may hold values from 64 to 256
- stick_column: int32 [256], replicated, may hold values from 0 to 65535, as said below
- plane_index: int32 [16], replicated, may hold values from 0 to 255, as said below
- occupation: int32 [8], P('band'), may hold values from 0 to 2
Outputs:
- density: float32 [16, 256, 256], P('pw')
The draws below stay inside these ranges and needn't reach their ends.
Inputs may be any that keep to these rules, and one draw needn't show every extreme that they name: `stick_column`: distinct column numbers. `plane_index`: distinct plane numbers.
All inputs are finite; a program needn't handle non-finite values.
Results may differ from the reference program's by a relative error of at most 0.003.
Values may be sent and summed in bfloat16 or wider, within the bound.
No kernel may reach another device: no remote copies, remote signals or barrier semaphores. Data moves between devices by JAX's collectives and lax.ppermute only.
A program may use at most 64 MiB of HBM per device.

```python
import math
import jax
import jax.numpy as jnp
from jax import lax

GRID = 256
IN_BANDS = 64
OUT_BANDS = 8
STICKS = 256
Z_WIN = 16
N_BAND = 4


def draw_stick_column(key, part):
    seeded = jax.random.fold_in(key, 11)
    return jax.random.permutation(seeded, GRID * GRID)[:STICKS].astype(jnp.int32)


def draw_plane_index(key, part):
    seeded = jax.random.fold_in(key, 23)
    return jax.random.permutation(seeded, GRID)[:Z_WIN].astype(jnp.int32)


def set_ends(drawn, rng, low, high):
    longest = drawn.shape.index(max(drawn.shape))
    spots = []
    for shift in (0, 1):
        where = [jax.random.randint(jax.random.fold_in(rng, axis), (), 0, length) for axis, length in enumerate(drawn.shape)]
        where[longest] = (where[longest] + shift) % drawn.shape[longest]
        spots.append(tuple(where))
    return drawn.at[spots[0]].set(low).at[spots[1]].set(high)


def levels(rng, extent, pieces, low, high):
    level, own = 1.0, jax.random.fold_in(rng, 6)
    for axis_at, blocks in pieces:
        heights = jnp.exp(jax.random.uniform(jax.random.fold_in(own, axis_at), (blocks,), jnp.float32, low / len(pieces), high / len(pieces)))
        level = level * jnp.repeat(heights, extent[axis_at] // blocks).reshape([-1 if axis == axis_at else 1 for axis in range(len(extent))])
    return level


def scatter_about(rng, dims, width, bound, cuts=(), kind=jnp.bfloat16):
    values = width * jax.random.normal(rng, dims, jnp.float32)
    if cuts:
        values = values * levels(rng, dims, cuts, -0.22, 0.18)
    return jnp.clip(values, -bound, bound).astype(kind)


def setup_inputs(seed: int = 0) -> dict:
    streams_of = jax.random.split(jax.random.key(seed), 7)
    return {
        "coeffs": scatter_about(streams_of[0], (2, IN_BANDS, STICKS, GRID), 1.0, 6.0, ((2, 32),)),
        "rotation_matrix": scatter_about(streams_of[1], (2, IN_BANDS, OUT_BANDS), (2 * IN_BANDS) ** -0.5, 0.5),
        "stick_length": set_ends(jax.random.randint(streams_of[2], (STICKS,), GRID // 4, GRID + 1), jax.random.fold_in(streams_of[2], 1), GRID // 4, GRID).astype(jnp.int32),
        "stick_column": draw_stick_column(jax.random.fold_in(streams_of[6], 71), 0),
        "plane_index": draw_plane_index(jax.random.fold_in(streams_of[6], 71), 0),
        "occupation": set_ends(jax.random.randint(streams_of[5], (OUT_BANDS,), 0, 3), jax.random.fold_in(streams_of[5], 1), 0, 2).astype(jnp.int32),
    }


def tables(grid_len, indices):
    product = (jnp.arange(grid_len, dtype=jnp.int32)[:, None] * indices[None, :]) % grid_len
    angles = (2.0 * math.pi / grid_len) * product.astype(jnp.float32)
    return jnp.cos(angles).astype(jnp.bfloat16), jnp.sin(angles).astype(jnp.bfloat16)


def contract(form, left, right):
    return jnp.einsum(form, left.astype(jnp.float32), right.astype(jnp.float32), precision=lax.Precision.HIGHEST)


def rotate(coeff_part, rotation_matrix):
    in_count = rotation_matrix.shape[1]
    out_count = rotation_matrix.shape[2]
    rotation = jnp.concatenate([jnp.concatenate([rotation_matrix[0], rotation_matrix[1]], 1), jnp.concatenate([-rotation_matrix[1], rotation_matrix[0]], 1)], 0)
    flattened = coeff_part.reshape(2 * in_count, -1)
    result = jnp.dot(rotation.T, flattened, preferred_element_type=jnp.float32)
    return result.reshape((2, out_count) + coeff_part.shape[2:]).astype(jnp.bfloat16)


def z_transform(rotated, lengths, plane_index):
    grid_len = rotated.shape[3]
    count = plane_index.shape[0]
    live_mask = (jnp.arange(grid_len, dtype=jnp.int32)[None, :] < lengths[:, None]).astype(jnp.bfloat16)
    masked = rotated * live_mask
    cos_table, sin_table = tables(grid_len, plane_index)
    weight = jnp.concatenate([jnp.concatenate([cos_table, sin_table], 1), jnp.concatenate([-sin_table, cos_table], 1)], 0)
    stacked = jnp.concatenate([masked[0], masked[1]], axis=-1)
    amplitude = contract('bsj,jk->bsk', stacked, weight)
    amp_real = amplitude[..., :count]
    amp_imag = amplitude[..., count:]
    shift = ((lengths // 2)[:, None] * plane_index[None, :]) % grid_len
    phase = (-2.0 * math.pi / grid_len) * shift.astype(jnp.float32)
    phase_cos = jnp.cos(phase)
    phase_sin = jnp.sin(phase)
    out_real = amp_real * phase_cos - amp_imag * phase_sin
    out_imag = amp_real * phase_sin + amp_imag * phase_cos
    result = jnp.stack([out_real, out_imag])
    return jnp.swapaxes(result, 2, 3).astype(jnp.bfloat16)


def plane_power(values, columns, grid_len):
    shape = values.shape
    flattened = jnp.zeros(shape[:3] + (grid_len * grid_len,), jnp.bfloat16).at[..., columns].set(values)
    planes = flattened.reshape(shape[:3] + (grid_len, grid_len))
    cos_table, sin_table = tables(grid_len, jnp.arange(grid_len, dtype=jnp.int32))
    half_real = (contract('bzxy,yk->bzxk', planes[0], cos_table) - contract('bzxy,yk->bzxk', planes[1], sin_table)).astype(jnp.bfloat16)
    half_imag = (contract('bzxy,yk->bzxk', planes[0], sin_table) + contract('bzxy,yk->bzxk', planes[1], cos_table)).astype(jnp.bfloat16)
    wave_real = contract('xq,bzxk->bzqk', cos_table, half_real) - contract('xq,bzxk->bzqk', sin_table, half_imag)
    wave_imag = contract('xq,bzxk->bzqk', sin_table, half_real) + contract('xq,bzxk->bzqk', cos_table, half_imag)
    return wave_real * wave_real + wave_imag * wave_imag


def reference(coeffs, rotation_matrix, stick_length, stick_column, plane_index, occupation):
    block_len = STICKS // N_BAND

    def one_group(group):
        first_row = (group * block_len).astype(jnp.int32)
        coeff_part = lax.dynamic_slice_in_dim(coeffs, first_row, block_len, 2)
        lengths = lax.dynamic_slice_in_dim(stick_length, first_row, block_len, 0)
        return z_transform(rotate(coeff_part, rotation_matrix), lengths, plane_index)

    grouped = lax.map(one_group, jnp.arange(N_BAND, dtype=jnp.int32))
    z_values = jnp.transpose(grouped, (1, 2, 3, 0, 4)).reshape(2, OUT_BANDS, Z_WIN, STICKS)
    by_plane = jnp.moveaxis(z_values, 2, 0)
    weights = occupation.astype(jnp.float32)

    def one_plane(values):
        power = plane_power(values[:, :, None, :], stick_column, GRID)[:, 0]
        return jnp.einsum('b,bxy->xy', weights, power)

    total = lax.map(one_plane, by_plane)
    return total / jnp.float32(OUT_BANDS * STICKS * GRID)
```

```python
import functools
import math

import jax
import jax.numpy as jnp
from jax import lax
from jax.experimental import pallas as pl
from jax.experimental.pallas import tpu as pltpu
from jax.sharding import PartitionSpec as P

LANES = 128


def wrap(value, period):
    if period & (period - 1) == 0:
        return value & (period - 1)
    return lax.rem(value, period)


def cut(value, size):
    if size & (size - 1) == 0:
        return value >> (size.bit_length() - 1)
    return lax.div(value, size)


def cosine(index, period):
    fold = jnp.abs(wrap(index, period) - period // 2) - period // 4
    angle = fold.astype(jnp.float32) * (2.0 * math.pi / period)
    square = angle * angle
    series = -2.39e-08
    for factor in (2.7526e-06, -1.984090e-04, 8.3333315e-03, -1.666666664e-01, 1.0):
        series = series * square + factor
    return angle * series


def sine(index, period):
    return cosine(index + (period - period // 4), period)


def iota(shape, dim):
    return lax.broadcasted_iota(jnp.int32, shape, dim)


def dot_last(left, right):
    return lax.dot_general(
        left, right, (((1,), (1,)), ((), ())), preferred_element_type=jnp.float32
    )


def dot(left, right):
    return jnp.dot(left, right, preferred_element_type=jnp.float32)


def spread(scalars, index, shape):
    result = jnp.full(shape, scalars[0])
    for place, scalar in enumerate(scalars[1:], 1):
        result = jnp.where(index == place, scalar, result)
    return result


def stick_kernel(
    pw_count, length_ref, plane_ref, occupation_ref, rotation_ref, coeff_ref, out_ref, held, sem
):
    in_count, out_count = rotation_ref.shape[1:]
    grid_len = coeff_ref.shape[1]
    sticks = coeff_ref.shape[0] // (2 * in_count)
    plane_count = plane_ref.shape[0]
    own_planes = plane_count // pw_count
    own_bands = occupation_ref.shape[0]
    row_count = 2 * out_count * sticks
    band_index = lax.axis_index("band")
    first_stick = (band_index * pw_count + lax.axis_index("pw")) * sticks
    copy = pltpu.make_async_copy(coeff_ref, held, sem)
    copy.start()

    lengths = [length_ref[first_stick + place] for place in range(sticks)]
    planes = [plane_ref[place] for place in range(plane_count)]

    pick = (
        wrap(cut(iota((row_count, out_count), 0), sticks), out_count)
        == iota((row_count, out_count), 1)
    ).astype(jnp.bfloat16)
    from_real = dot_last(pick, rotation_ref[0])
    from_imag = dot_last(pick, rotation_ref[1])
    is_real = iota((row_count, in_count), 0) < out_count * sticks
    widen = (
        cut(iota((in_count, in_count * sticks), 1), sticks)
        == iota((in_count, in_count * sticks), 0)
    ).astype(jnp.bfloat16)
    shape = (row_count, in_count * sticks)
    same = wrap(iota(shape, 0), sticks) == wrap(iota(shape, 1), sticks)
    mixed = []
    for block in (
        jnp.where(is_real, from_real, from_imag),
        jnp.where(is_real, -from_imag, from_real),
    ):
        wide = dot(block.astype(jnp.bfloat16), widen)
        mixed.append(jnp.where(same, wide, 0.0).astype(jnp.bfloat16))
    rotation = jnp.concatenate(mixed, 1)

    plane_rows = spread(planes, iota((plane_count, grid_len), 0), (plane_count, grid_len))
    product = iota((plane_count, grid_len), 1) * plane_rows
    table = jnp.concatenate([cosine(product, grid_len), sine(product, grid_len)], 0).astype(
        jnp.bfloat16
    )

    shape = (plane_count, row_count)
    lane_lengths = spread(lengths, wrap(iota(shape, 1), sticks), shape)
    shift = (lane_lengths >> 1) * spread(planes, iota(shape, 0), shape)
    phase_cos = cosine(shift, grid_len)
    phase_sin = sine(shift, grid_len)
    real_lane = iota(shape, 1) < row_count // 2

    row_lengths = spread(lengths, iota((sticks, grid_len), 0), (sticks, grid_len))
    live = iota((sticks, grid_len), 1) < row_lengths

    copy.wait()
    rotated = dot(rotation, held[...])
    rotated = rotated.reshape(row_count // sticks, sticks, grid_len)
    rotated = jnp.where(live[None], rotated, 0.0).reshape(row_count, grid_len)
    sums = dot_last(table, rotated.astype(jnp.bfloat16))
    with_cos, with_sin = sums[:plane_count], sums[plane_count:]
    turned = pltpu.roll(with_sin, row_count // 2, 1)
    amplitude = with_cos + jnp.where(real_lane, -turned, turned)
    turned = pltpu.roll(amplitude, row_count // 2, 1) * phase_sin
    values = amplitude * phase_cos + jnp.where(real_lane, turned, -turned)

    lanes = out_ref.shape[2]
    spots = 2 * out_count
    tall = jnp.broadcast_to(values[:, None, :], (plane_count, sticks, row_count))
    own = iota((sticks, row_count), 0) == wrap(iota((sticks, row_count), 1), sticks)
    tall = jnp.where(own[None], tall, 0.0).reshape(plane_count * sticks, row_count)
    shape = (row_count, lanes)
    place = (
        (cut(iota(shape, 0), sticks) == lax.rem(iota(shape, 1), spots))
        & (iota(shape, 1) < own_planes * spots)
    ).astype(jnp.bfloat16)
    laid = dot(tall.astype(jnp.bfloat16), place).reshape(pw_count, own_planes, sticks, lanes)
    mine = cut(iota((own_planes, sticks, lanes), 2), spots) == iota((own_planes, sticks, lanes), 0)
    message = jnp.sum(jnp.where(mine[None], laid, 0.0), 1)
    occupied = jnp.zeros((sticks, lanes), jnp.int32)
    for own_band in range(own_bands):
        lane = own_planes * spots + band_index * own_bands + own_band
        occupied = jnp.where(
            iota((sticks, lanes), 1) == lane, occupation_ref[own_band], occupied
        )
    message = (message + occupied.astype(jnp.float32)[None]).astype(out_ref.dtype)
    for band in range(out_ref.shape[0] // pw_count):
        out_ref[band * pw_count : (band + 1) * pw_count] = message


def table_kernel(grid_len, column_ref, left_ref, right_ref):
    count = column_ref.shape[1]
    columns = column_ref[...]
    freq = iota((grid_len, count), 0)
    turns = freq * cut(columns, grid_len)
    left_ref[0] = cosine(turns, grid_len).astype(jnp.bfloat16)
    left_ref[1] = sine(turns, grid_len).astype(jnp.bfloat16)
    turns = freq * wrap(columns, grid_len)
    cos_table = cosine(turns, grid_len).astype(jnp.bfloat16)
    sin_table = sine(turns, grid_len).astype(jnp.bfloat16)
    right_ref[0, :grid_len] = cos_table
    right_ref[0, grid_len:] = sin_table
    right_ref[1, :grid_len] = -sin_table
    right_ref[1, grid_len:] = cos_table


def plane_kernel(
    bands, own_planes, norm_factor, message_ref, left_ref, right_ref, out_ref, value_ref
):
    chunks = value_ref.shape[0]
    chunk = value_ref.shape[2]
    grid_len = out_ref.shape[1]
    lanes = message_ref.shape[1]
    rows = value_ref.shape[1]
    spots = 2 * bands
    select = (iota((rows + bands, lanes), 0) == iota((rows + bands, lanes), 1)).astype(
        jnp.bfloat16
    )

    def turn(index, peak):
        first = index * chunk
        picked = dot_last(select, message_ref[pl.ds(first, chunk), :])
        value_ref[index] = picked[:rows]
        return jnp.maximum(peak, jnp.max(picked[rows:], 1, keepdims=True))

    peak = jnp.zeros((bands, 1), jnp.float32)
    if chunks == 1:
        peak = turn(0, peak)
    else:
        peak = lax.fori_loop(0, chunks, turn, peak)
    scale = jnp.sqrt(peak)
    for group in range(rows // bands):
        where = slice(group * bands, (group + 1) * bands)
        value_ref[:, where] = value_ref[:, where] * scale[None]

    def partial_wave(index, plane, band):
        lane = pl.ds(index * chunk, chunk) if chunks > 1 else slice(None)
        real = value_ref[index, pl.ds(plane * spots + band, 1), :]
        imag = value_ref[index, pl.ds(plane * spots + bands + band, 1), :]
        cos_table = left_ref[0, :, lane].astype(jnp.float32)
        sin_table = left_ref[1, :, lane].astype(jnp.float32)
        part_real = (cos_table * real - sin_table * imag).astype(jnp.bfloat16)
        part_imag = (sin_table * real + cos_table * imag).astype(jnp.bfloat16)
        return dot_last(part_real, right_ref[0, :, lane]) + dot_last(
            part_imag, right_ref[1, :, lane]
        )

    for plane in range(own_planes):

        def add_band(band, total):
            if chunks == 1:
                wave = partial_wave(0, plane, band)
            else:
                wave = lax.fori_loop(
                    0,
                    chunks,
                    lambda index, so_far: so_far + partial_wave(index, plane, band),
                    jnp.zeros((grid_len, 2 * grid_len), jnp.float32),
                )
            real, imag = wave[:, :grid_len], wave[:, grid_len:]
            out_ref[plane] += real * real + imag * imag
            return total

        out_ref[plane] = jnp.zeros((grid_len, grid_len), jnp.float32)
        lax.fori_loop(0, bands, add_band, 0)
        out_ref[plane] = out_ref[plane] * norm_factor


def shards(coeffs, rotation_matrix, stick_length, stick_column, plane_index, occupation):
    band_count = lax.axis_size("band")
    pw_count = lax.axis_size("pw")
    devices = band_count * pw_count
    in_count, sticks, grid_len = coeffs.shape[1:]
    bands = rotation_matrix.shape[2]
    stick_count = stick_column.shape[0]
    own_planes = plane_index.shape[0] // pw_count
    spots = 2 * bands
    rows = own_planes * spots
    lanes = -(-(rows + bands) // LANES) * LANES
    smem = pl.BlockSpec(memory_space=pltpu.SMEM)
    vmem = pl.BlockSpec(memory_space=pltpu.VMEM)
    room = pltpu.CompilerParams(vmem_limit_bytes=56 * 1024 * 1024)

    messages = pl.pallas_call(
        functools.partial(stick_kernel, pw_count),
        out_shape=jax.ShapeDtypeStruct((devices, sticks, lanes), jnp.bfloat16),
        in_specs=[smem, smem, smem, vmem, pl.BlockSpec(memory_space=pl.ANY)],
        out_specs=vmem,
        scratch_shapes=[
            pltpu.VMEM((2 * in_count * sticks, grid_len), jnp.bfloat16),
            pltpu.SemaphoreType.DMA,
        ],
        compiler_params=room,
        name="stick_values",
    )(
        stick_length,
        plane_index,
        occupation,
        rotation_matrix,
        coeffs.reshape(2 * in_count * sticks, grid_len),
    )
    left, right = pl.pallas_call(
        functools.partial(table_kernel, grid_len),
        out_shape=(
            jax.ShapeDtypeStruct((2, grid_len, stick_count), jnp.bfloat16),
            jax.ShapeDtypeStruct((2, 2 * grid_len, stick_count), jnp.bfloat16),
        ),
        in_specs=[vmem],
        out_specs=(vmem, vmem),
        compiler_params=room,
        cost_estimate=pl.CostEstimate(
            flops=80 * grid_len * stick_count,
            bytes_accessed=12 * grid_len * stick_count,
            transcendentals=0,
        ),
        name="stick_tables",
    )(stick_column.reshape(1, stick_count))
    arrived = lax.all_to_all(messages, ("band", "pw"), split_axis=0, concat_axis=0, tiled=True)
    chunk = min(grid_len, stick_count)
    norm_factor = 1.0 / float(bands * stick_count * grid_len)
    return pl.pallas_call(
        functools.partial(plane_kernel, bands, own_planes, norm_factor),
        out_shape=jax.ShapeDtypeStruct((own_planes, grid_len, grid_len), jnp.float32),
        in_specs=[vmem] * 3,
        out_specs=vmem,
        scratch_shapes=[pltpu.VMEM((stick_count // chunk, rows, chunk), jnp.float32)],
        compiler_params=room,
        name="plane_density",
    )(arrived.reshape(stick_count, lanes), left, right)


def solution(mesh):
    return jax.shard_map(
        shards,
        mesh=mesh,
        in_specs=(P(None, None, ("band", "pw"), None), P(), P(), P(), P(), P("band")),
        out_specs=P("pw", None, None),
        check_vma=False,
    )
```

```python
import functools
import math

import jax
import jax.numpy as jnp
from jax import lax
from jax.experimental import pallas as pl
from jax.experimental.pallas import tpu as pltpu
from jax.sharding import PartitionSpec as P

LANES = 128
PACK = 16
P_BLOCK = 64
BAND_GROUP = 8
MIB = 1024 * 1024


def wrap(value, period):
    if period & (period - 1) == 0:
        return value & (period - 1)
    return lax.rem(value, period)


def cut(value, size):
    if size & (size - 1) == 0:
        return value >> (size.bit_length() - 1)
    return lax.div(value, size)


def cosine(index, period):
    fold = jnp.abs(wrap(index, period) - period // 2) - period // 4
    angle = fold.astype(jnp.float32) * (2.0 * math.pi / period)
    square = angle * angle
    series = -2.39e-08
    for factor in (2.7526e-06, -1.984090e-04, 8.3333315e-03, -1.666666664e-01, 1.0):
        series = series * square + factor
    return angle * series


def sine(index, period):
    return cosine(index + (period - period // 4), period)


def iota(shape, dim):
    return lax.broadcasted_iota(jnp.int32, shape, dim)


def dot_last(left, right):
    return lax.dot_general(
        left, right, (((1,), (1,)), ((), ())), preferred_element_type=jnp.float32
    )


def dot(left, right):
    return jnp.dot(left, right, preferred_element_type=jnp.float32)


def loop(count, body, carry):
    if count > 16:
        return lax.fori_loop(0, count, body, carry)
    for index in range(count):
        carry = body(index, carry)
    return carry


def room(*sizes):
    return pltpu.CompilerParams(vmem_limit_bytes=min(56 * MIB, 16 * MIB + 2 * sum(sizes)))


def spread(scalars, index, shape):
    result = jnp.full(shape, scalars[0])
    for place, scalar in enumerate(scalars[1:], 1):
        result = jnp.where(index == place, scalar, result)
    return result


def stick_kernel(
    pw_count, length_ref, plane_ref, occupation_ref, rotation_ref, coeff_ref, out_ref, held, sem
):
    out_count, in_count = rotation_ref.shape[1:]
    grid_len = coeff_ref.shape[1]
    sticks = coeff_ref.shape[0] // (2 * in_count)
    plane_count = plane_ref.shape[0]
    own_planes = plane_count // pw_count
    own_bands = occupation_ref.shape[0]
    row_count = 2 * out_count * sticks
    band_index = lax.axis_index("band")
    first_stick = (band_index * pw_count + lax.axis_index("pw")) * sticks
    copy = pltpu.make_async_copy(coeff_ref, held, sem)
    copy.start()

    lengths = [length_ref[first_stick + place] for place in range(sticks)]
    planes = [plane_ref[place] for place in range(plane_count)]

    pick = (
        wrap(cut(iota((row_count, out_count), 0), sticks), out_count)
        == iota((row_count, out_count), 1)
    ).astype(jnp.bfloat16)
    from_real = dot(pick, rotation_ref[0])
    from_imag = dot(pick, rotation_ref[1])
    is_real = iota((row_count, in_count), 0) < out_count * sticks
    widen = (
        cut(iota((in_count, in_count * sticks), 1), sticks)
        == iota((in_count, in_count * sticks), 0)
    ).astype(jnp.bfloat16)
    shape = (row_count, in_count * sticks)
    same = wrap(iota(shape, 0), sticks) == wrap(iota(shape, 1), sticks)
    mixed = []
    for block in (
        jnp.where(is_real, from_real, from_imag),
        jnp.where(is_real, -from_imag, from_real),
    ):
        wide = dot(block.astype(jnp.bfloat16), widen)
        mixed.append(jnp.where(same, wide, 0.0).astype(jnp.bfloat16))
    rotation = jnp.concatenate(mixed, 1)

    plane_rows = spread(planes, iota((plane_count, grid_len), 0), (plane_count, grid_len))
    product = iota((plane_count, grid_len), 1) * plane_rows
    table = jnp.concatenate([cosine(product, grid_len), sine(product, grid_len)], 0).astype(
        jnp.bfloat16
    )

    shape = (plane_count, row_count)
    lane_lengths = spread(lengths, wrap(iota(shape, 1), sticks), shape)
    shift = (lane_lengths >> 1) * spread(planes, iota(shape, 0), shape)
    phase_cos = cosine(shift, grid_len)
    phase_sin = sine(shift, grid_len)
    real_lane = iota(shape, 1) < row_count // 2

    row_lengths = spread(lengths, iota((sticks, grid_len), 0), (sticks, grid_len))
    live = iota((sticks, grid_len), 1) < row_lengths

    copy.wait()
    rotated = dot(rotation, held[...])
    rotated = rotated.reshape(row_count // sticks, sticks, grid_len)
    rotated = jnp.where(live[None], rotated, 0.0).reshape(row_count, grid_len)
    sums = dot_last(table, rotated.astype(jnp.bfloat16))
    with_cos, with_sin = sums[:plane_count], sums[plane_count:]
    turned = pltpu.roll(with_sin, row_count // 2, 1)
    amplitude = with_cos + jnp.where(real_lane, -turned, turned)
    turned = pltpu.roll(amplitude, row_count // 2, 1) * phase_sin
    values = amplitude * phase_cos + jnp.where(real_lane, turned, -turned)

    lanes = out_ref.shape[2]
    spots = 2 * out_count
    tall = jnp.broadcast_to(values[:, None, :], (plane_count, sticks, row_count))
    own = iota((sticks, row_count), 0) == wrap(iota((sticks, row_count), 1), sticks)
    tall = jnp.where(own[None], tall, 0.0).reshape(plane_count * sticks, row_count)
    shape = (row_count, lanes)
    place = (
        (cut(iota(shape, 0), sticks) == lax.rem(iota(shape, 1), spots))
        & (iota(shape, 1) < own_planes * spots)
    ).astype(jnp.bfloat16)
    laid = dot(tall.astype(jnp.bfloat16), place).reshape(pw_count, own_planes, sticks, lanes)
    mine = cut(iota((own_planes, sticks, lanes), 2), spots) == iota((own_planes, sticks, lanes), 0)
    message = jnp.sum(jnp.where(mine[None], laid, 0.0), 1)
    occupied = jnp.zeros((sticks, lanes), jnp.int32)
    for own_band in range(own_bands):
        lane = own_planes * spots + band_index * own_bands + own_band
        occupied = jnp.where(
            iota((sticks, lanes), 1) == lane, occupation_ref[own_band], occupied
        )
    message = (message + occupied.astype(jnp.float32)[None]).astype(out_ref.dtype)
    for band in range(out_ref.shape[0] // pw_count):
        out_ref[band * pw_count : (band + 1) * pw_count] = message


def table_kernel(grid_len, column_ref, left_ref, right_ref):
    count = column_ref.shape[1]
    half = grid_len // 2
    columns = column_ref[...]
    turns = iota((grid_len, count), 0) * cut(columns, grid_len)
    left_ref[0] = cosine(turns, grid_len).astype(jnp.bfloat16)
    left_ref[1] = sine(turns, grid_len).astype(jnp.bfloat16)
    tall = jnp.transpose(jnp.broadcast_to(wrap(columns, grid_len), (half, count)))
    freq = iota((count, half), 1)
    right_ref[:, :half] = cosine(tall * freq, grid_len).astype(jnp.bfloat16)
    turns = jnp.where(freq == 0, tall * half, tall * freq + (grid_len - grid_len // 4))
    right_ref[:, half:] = cosine(turns, grid_len).astype(jnp.bfloat16)


def plane_kernel(
    bands,
    own_planes,
    norm_factor,
    message_ref,
    left_ref,
    right_ref,
    out_ref,
    value_ref,
    weight_ref,
    held_ref,
    sem,
):
    chunks, rows, chunk = value_ref.shape
    grid_len = out_ref.shape[1]
    half = grid_len // 2
    lanes = message_ref.shape[1]
    spots = 2 * bands
    height = math.gcd(grid_len, P_BLOCK)
    blocks = grid_len // height
    group = math.gcd(bands, BAND_GROUP)
    select = (iota((rows + bands, lanes), 0) == iota((rows + bands, lanes), 1)).astype(
        jnp.bfloat16
    )

    def turn(index, peak):
        first = index * chunk
        picked = dot_last(select, message_ref[pl.ds(first, chunk), :])
        value_ref[index] = picked[:rows]
        return jnp.maximum(peak, jnp.max(picked[rows:], 1, keepdims=True))

    peak = loop(chunks, turn, jnp.zeros((bands, 1), jnp.float32))
    weight_ref[...] = jnp.broadcast_to(peak * norm_factor, weight_ref.shape)

    def stick_sums(index, plane, block, first_band):
        lane = pl.ds(index * chunk, chunk)
        row = pl.ds(block * height, height)
        cos_table = left_ref[0, row, lane].reshape(height // PACK, PACK, chunk)
        sin_table = left_ref[1, row, lane].reshape(height // PACK, PACK, chunk)
        parts = []
        for band in range(group):
            at = plane * spots + first_band + band
            real, imag = (
                jnp.broadcast_to(value_ref[index, pl.ds(spot, 1), :], (PACK, chunk)).astype(
                    jnp.bfloat16
                )[None]
                for spot in (at, at + bands)
            )
            parts.append((cos_table * real - sin_table * imag).reshape(height, chunk))
            parts.append((sin_table * real + cos_table * imag).reshape(height, chunk))
        return dot(jnp.concatenate(parts, 0), right_ref[pl.ds(index * chunk, chunk), :])

    def one_block(step, carry):
        plane, block = step // blocks, step % blocks

        def one_group(index, sums):
            first_band = index * group
            if chunks == 1:
                found = stick_sums(0, plane, block, first_band)
            else:
                found = lax.fori_loop(
                    0,
                    chunks,
                    lambda at, so_far: so_far + stick_sums(at, plane, block, first_band),
                    jnp.zeros((2 * group * height, grid_len), jnp.float32),
                )
            with_cos, with_sin, mixed = sums
            for band in range(group):
                top = 2 * band * height
                a, d = found[top : top + height, :half], found[top : top + height, half:]
                top += height
                c, b = found[top : top + height, :half], found[top : top + height, half:]
                weight = weight_ref[pl.ds(first_band + band, 1), :half]
                with_cos += weight * (a * a + c * c)
                with_sin += weight * (b * b + d * d)
                mixed += weight * (c * d - a * b)
            return with_cos, with_sin, mixed

        zero = jnp.zeros((height, half), jnp.float32)
        with_cos, with_sin, mixed = loop(bands // group, one_group, (zero, zero, zero))
        lane = iota((height, half), 1)
        both, mixed = with_cos + with_sin, mixed + mixed
        ahead = jnp.where(lane == 0, with_cos, both + mixed)
        back = jnp.where(lane == 0, with_sin, both - mixed)
        row = pl.ds(block * height, height)
        held_ref[plane, row, :half] = ahead
        held_ref[plane, row, half:] = jnp.take_along_axis(
            back, jnp.where(lane == 0, 0, half - lane), axis=1
        )
        pltpu.make_async_copy(
            held_ref.at[plane, row], out_ref.at[plane, row], sem.at[step]
        ).start()
        return carry

    loop(own_planes * blocks, one_block, 0)
    for step in range(own_planes * blocks):
        where = (step // blocks, pl.ds(step % blocks * height, height))
        pltpu.make_async_copy(held_ref.at[where], out_ref.at[where], sem.at[step]).wait()


def shards(coeffs, rotation_matrix, stick_length, stick_column, plane_index, occupation):
    band_count = lax.axis_size("band")
    pw_count = lax.axis_size("pw")
    devices = band_count * pw_count
    in_count, sticks, grid_len = coeffs.shape[1:]
    bands = rotation_matrix.shape[2]
    stick_count = stick_column.shape[0]
    own_planes = plane_index.shape[0] // pw_count
    spots = 2 * bands
    rows = own_planes * spots
    lanes = -(-(rows + bands) // LANES) * LANES
    smem = pl.BlockSpec(memory_space=pltpu.SMEM)
    vmem = pl.BlockSpec(memory_space=pltpu.VMEM)
    table_bytes = 6 * grid_len * stick_count

    messages = pl.pallas_call(
        functools.partial(stick_kernel, pw_count),
        out_shape=jax.ShapeDtypeStruct((devices, sticks, lanes), jnp.bfloat16),
        in_specs=[smem, smem, smem, vmem, pl.BlockSpec(memory_space=pl.ANY)],
        out_specs=vmem,
        scratch_shapes=[
            pltpu.VMEM((2 * in_count * sticks, grid_len), jnp.bfloat16),
            pltpu.SemaphoreType.DMA,
        ],
        compiler_params=pltpu.CompilerParams(vmem_limit_bytes=56 * MIB),
        name="stick_values",
    )(
        stick_length,
        plane_index,
        occupation,
        jnp.swapaxes(rotation_matrix, 1, 2),
        coeffs.reshape(2 * in_count * sticks, grid_len),
    )
    left, right = pl.pallas_call(
        functools.partial(table_kernel, grid_len),
        out_shape=(
            jax.ShapeDtypeStruct((2, grid_len, stick_count), jnp.bfloat16),
            jax.ShapeDtypeStruct((stick_count, grid_len), jnp.bfloat16),
        ),
        in_specs=[vmem],
        out_specs=(vmem, vmem),
        compiler_params=room(table_bytes),
        cost_estimate=pl.CostEstimate(
            flops=80 * grid_len * stick_count,
            bytes_accessed=12 * grid_len * stick_count,
            transcendentals=0,
        ),
        name="stick_tables",
    )(stick_column.reshape(1, stick_count))
    arrived = lax.all_to_all(messages, ("band", "pw"), split_axis=0, concat_axis=0, tiled=True)
    chunk = min(grid_len, stick_count)
    norm_factor = 1.0 / float(bands * stick_count * grid_len)
    blocks = own_planes * (grid_len // math.gcd(grid_len, P_BLOCK))
    return pl.pallas_call(
        functools.partial(plane_kernel, bands, own_planes, norm_factor),
        out_shape=jax.ShapeDtypeStruct((own_planes, grid_len, grid_len), jnp.float32),
        in_specs=[vmem] * 3,
        out_specs=pl.BlockSpec(memory_space=pl.ANY),
        scratch_shapes=[
            pltpu.VMEM((stick_count // chunk, rows, chunk), jnp.float32),
            pltpu.VMEM((bands, LANES), jnp.float32),
            pltpu.VMEM((own_planes, grid_len, grid_len), jnp.float32),
            pltpu.SemaphoreType.DMA((blocks,)),
        ],
        compiler_params=room(table_bytes, 2 * stick_count * lanes),
        name="plane_density",
    )(arrived.reshape(stick_count, lanes), left, right)


def solution(mesh):
    return jax.shard_map(
        shards,
        mesh=mesh,
        in_specs=(P(None, None, ("band", "pw"), None), P(), P(), P(), P(), P("band")),
        out_specs=P("pw", None, None),
        check_vma=False,
    )
```

```python
import functools
import math

import jax
import jax.numpy as jnp
from jax import lax
from jax.experimental import pallas as pl
from jax.experimental.pallas import tpu as pltpu
from jax.sharding import PartitionSpec as P

LANES = 128
PACK = 16
P_BLOCK = 64
BAND_GROUP = 8
MIB = 1024 * 1024


def wrap(value, period):
    if period & (period - 1) == 0:
        return value & (period - 1)
    return lax.rem(value, period)


def cut(value, size):
    if size & (size - 1) == 0:
        return value >> (size.bit_length() - 1)
    return lax.div(value, size)


def cosine(index, period):
    fold = jnp.abs(wrap(index, period) - period // 2) - period // 4
    angle = fold.astype(jnp.float32) * (2.0 * math.pi / period)
    square = angle * angle
    series = -2.39e-08
    for factor in (2.7526e-06, -1.984090e-04, 8.3333315e-03, -1.666666664e-01, 1.0):
        series = series * square + factor
    return angle * series


def sine(index, period):
    return cosine(index + (period - period // 4), period)


def iota(shape, dim):
    return lax.broadcasted_iota(jnp.int32, shape, dim)


def dot_last(left, right):
    return lax.dot_general(
        left, right, (((1,), (1,)), ((), ())), preferred_element_type=jnp.float32
    )


def dot(left, right):
    return jnp.dot(left, right, preferred_element_type=jnp.float32)


def loop(count, body, carry):
    if count > 16:
        return lax.fori_loop(0, count, body, carry)
    for index in range(count):
        carry = body(index, carry)
    return carry


def room(*sizes):
    return pltpu.CompilerParams(vmem_limit_bytes=min(56 * MIB, 16 * MIB + 2 * sum(sizes)))


def spread(scalars, index, shape):
    result = jnp.full(shape, scalars[0])
    for place, scalar in enumerate(scalars[1:], 1):
        result = jnp.where(index == place, scalar, result)
    return result


def stick_kernel(
    length_hbm,
    plane_hbm,
    occupation_hbm,
    rotation_hbm,
    coeff_hbm,
    out_ref,
    length_ref,
    plane_ref,
    occupation_ref,
    rotation_ref,
    coeff_ref,
    sems,
):
    copies = [
        pltpu.make_async_copy(source, target, sems.at[index])
        for index, (source, target) in enumerate(
            (
                (rotation_hbm, rotation_ref),
                (coeff_hbm, coeff_ref),
                (plane_hbm, plane_ref),
                (length_hbm, length_ref),
                (occupation_hbm, occupation_ref),
            )
        )
    ]
    for copy in copies:
        copy.start()
    out_count, in_count = rotation_ref.shape[1:]
    grid_len = coeff_ref.shape[1]
    sticks = coeff_ref.shape[0] // (2 * in_count)
    plane_count = plane_ref.shape[0]
    pw_count = out_ref.shape[0]
    own_planes = plane_count // pw_count
    own_bands = occupation_ref.shape[0]
    row_count = 2 * out_count * sticks
    band_index = lax.axis_index("band")
    first_stick = (band_index * pw_count + lax.axis_index("pw")) * sticks

    pick = (
        wrap(cut(iota((row_count, out_count), 0), sticks), out_count)
        == iota((row_count, out_count), 1)
    ).astype(jnp.bfloat16)
    copies[0].wait()
    from_real = dot(pick, rotation_ref[0])
    from_imag = dot(pick, rotation_ref[1])
    is_real = iota((row_count, in_count), 0) < out_count * sticks
    widen = (
        cut(iota((in_count, in_count * sticks), 1), sticks)
        == iota((in_count, in_count * sticks), 0)
    ).astype(jnp.bfloat16)
    shape = (row_count, in_count * sticks)
    same = wrap(iota(shape, 0), sticks) == wrap(iota(shape, 1), sticks)
    mixed = []
    for block in (
        jnp.where(is_real, from_real, from_imag),
        jnp.where(is_real, -from_imag, from_real),
    ):
        wide = dot(block.astype(jnp.bfloat16), widen)
        mixed.append(jnp.where(same, wide, 0.0).astype(jnp.bfloat16))
    rotation = jnp.concatenate(mixed, 1)

    for copy in copies[2:]:
        copy.wait()
    lengths = [length_ref[first_stick + place] for place in range(sticks)]
    planes = [plane_ref[place] for place in range(plane_count)]
    plane_rows = spread(planes, iota((plane_count, grid_len), 0), (plane_count, grid_len))
    product = iota((plane_count, grid_len), 1) * plane_rows
    table = jnp.concatenate([cosine(product, grid_len), sine(product, grid_len)], 0).astype(
        jnp.bfloat16
    )

    shape = (plane_count, row_count)
    lane_lengths = spread(lengths, wrap(iota(shape, 1), sticks), shape)
    shift = (lane_lengths >> 1) * spread(planes, iota(shape, 0), shape)
    phase_cos = cosine(shift, grid_len)
    phase_sin = sine(shift, grid_len)
    real_lane = iota(shape, 1) < row_count // 2

    row_lengths = spread(lengths, iota((sticks, grid_len), 0), (sticks, grid_len))
    live = iota((sticks, grid_len), 1) < row_lengths

    copies[1].wait()
    rotated = dot(rotation, coeff_ref[...])
    rotated = rotated.reshape(row_count // sticks, sticks, grid_len)
    rotated = jnp.where(live[None], rotated, 0.0).reshape(row_count, grid_len)
    sums = dot_last(table, rotated.astype(jnp.bfloat16))
    with_cos, with_sin = sums[:plane_count], sums[plane_count:]
    turned = pltpu.roll(with_sin, row_count // 2, 1)
    amplitude = with_cos + jnp.where(real_lane, -turned, turned)
    turned = pltpu.roll(amplitude, row_count // 2, 1) * phase_sin
    values = amplitude * phase_cos + jnp.where(real_lane, turned, -turned)

    lanes = out_ref.shape[2]
    spots = 2 * out_count
    tall = jnp.broadcast_to(values[:, None, :], (plane_count, sticks, row_count))
    own = iota((sticks, row_count), 0) == wrap(iota((sticks, row_count), 1), sticks)
    tall = jnp.where(own[None], tall, 0.0).reshape(plane_count * sticks, row_count)
    shape = (row_count, lanes)
    place = (
        (cut(iota(shape, 0), sticks) == lax.rem(iota(shape, 1), spots))
        & (iota(shape, 1) < own_planes * spots)
    ).astype(jnp.bfloat16)
    laid = dot(tall.astype(jnp.bfloat16), place).reshape(pw_count, own_planes, sticks, lanes)
    mine = cut(iota((own_planes, sticks, lanes), 2), spots) == iota((own_planes, sticks, lanes), 0)
    message = jnp.sum(jnp.where(mine[None], laid, 0.0), 1)
    occupied = jnp.zeros((sticks, lanes), jnp.int32)
    for own_band in range(own_bands):
        lane = own_planes * spots + band_index * own_bands + own_band
        occupied = jnp.where(
            iota((sticks, lanes), 1) == lane, occupation_ref[own_band], occupied
        )
    out_ref[...] = (message + occupied.astype(jnp.float32)[None]).astype(out_ref.dtype)


def regroup_kernel(*refs):
    band_count = refs[-1].shape[0]
    pw_index = lax.axis_index("pw")
    for offset, out_ref in enumerate(refs[band_count:]):
        for place, gathered_ref in enumerate(refs[:band_count]):
            out_ref[place] = gathered_ref[pw_index ^ offset]


def table_kernel(grid_len, sticks, column_hbm, left_ref, right_ref, column_ref, sem):
    copy = pltpu.make_async_copy(column_hbm, column_ref, sem)
    copy.start()
    copy.wait()
    count = column_ref.shape[1]
    half = grid_len // 2
    me = lax.axis_index("band") * lax.axis_size("pw") + lax.axis_index("pw")
    columns = jnp.broadcast_to(column_ref[...], (8, count))
    stride = sticks
    while stride < count:
        high = cut(iota((8, count), 1), stride) & 1
        exchanged = jnp.where(
            high == 1, pltpu.roll(columns, stride, 1), pltpu.roll(columns, count - stride, 1)
        )
        columns = jnp.where(cut(me * sticks, stride) & 1 == 1, exchanged, columns)
        stride *= 2
    columns = columns[:1]
    turns = iota((grid_len, count), 0) * cut(columns, grid_len)
    left_ref[0] = cosine(turns, grid_len).astype(jnp.bfloat16)
    left_ref[1] = sine(turns, grid_len).astype(jnp.bfloat16)
    tall = jnp.transpose(jnp.broadcast_to(wrap(columns, grid_len), (half, count)))
    freq = iota((count, half), 1)
    right_ref[:, :half] = cosine(tall * freq, grid_len).astype(jnp.bfloat16)
    turns = jnp.where(freq == 0, tall * half, tall * freq + (grid_len - grid_len // 4))
    right_ref[:, half:] = cosine(turns, grid_len).astype(jnp.bfloat16)


def plane_kernel(
    bands,
    own_planes,
    norm_factor,
    *refs,
):
    *arrived, left_ref, right_ref, out_ref, message_ref, value_ref, weight_ref, held_ref, sem = refs
    chunks, rows, chunk = value_ref.shape
    grid_len = out_ref.shape[1]
    half = grid_len // 2
    sticks, lanes = message_ref.shape[1:]
    spots = 2 * bands
    height = math.gcd(grid_len, P_BLOCK)
    blocks = grid_len // height
    group = math.gcd(bands, BAND_GROUP)
    select = (iota((rows + bands, lanes), 0) == iota((rows + bands, lanes), 1)).astype(
        jnp.bfloat16
    )

    for offset, arrived_ref in enumerate(arrived):
        for place in range(arrived_ref.shape[0]):
            message_ref[place * len(arrived) + offset] = arrived_ref[place]

    def turn(index, peak):
        pieces = chunk // sticks
        picked = dot_last(
            select, message_ref[pl.ds(index * pieces, pieces)].reshape(chunk, lanes)
        )
        value_ref[index] = picked[:rows]
        return jnp.maximum(peak, jnp.max(picked[rows:], 1, keepdims=True))

    peak = loop(chunks, turn, jnp.zeros((bands, 1), jnp.float32))
    weight_ref[...] = jnp.broadcast_to(peak * norm_factor, weight_ref.shape)

    def stick_sums(index, plane, block, first_band):
        lane = pl.ds(index * chunk, chunk)
        row = pl.ds(block * height, height)
        cos_table = left_ref[0, row, lane].reshape(height // PACK, PACK, chunk)
        sin_table = left_ref[1, row, lane].reshape(height // PACK, PACK, chunk)
        parts = []
        for band in range(group):
            at = plane * spots + first_band + band
            real, imag = (
                jnp.broadcast_to(value_ref[index, pl.ds(spot, 1), :], (PACK, chunk)).astype(
                    jnp.bfloat16
                )[None]
                for spot in (at, at + bands)
            )
            parts.append((cos_table * real - sin_table * imag).reshape(height, chunk))
            parts.append((sin_table * real + cos_table * imag).reshape(height, chunk))
        return dot(jnp.concatenate(parts, 0), right_ref[pl.ds(index * chunk, chunk), :])

    def one_block(step, carry):
        plane, block = step // blocks, step % blocks

        def one_group(index, sums):
            first_band = index * group
            if chunks == 1:
                found = stick_sums(0, plane, block, first_band)
            else:
                found = lax.fori_loop(
                    0,
                    chunks,
                    lambda at, so_far: so_far + stick_sums(at, plane, block, first_band),
                    jnp.zeros((2 * group * height, grid_len), jnp.float32),
                )
            with_cos, with_sin, mixed = sums
            for band in range(group):
                top = 2 * band * height
                a, d = found[top : top + height, :half], found[top : top + height, half:]
                top += height
                c, b = found[top : top + height, :half], found[top : top + height, half:]
                weight = weight_ref[pl.ds(first_band + band, 1), :half]
                with_cos += weight * (a * a + c * c)
                with_sin += weight * (b * b + d * d)
                mixed += weight * (c * d - a * b)
            return with_cos, with_sin, mixed

        zero = jnp.zeros((height, half), jnp.float32)
        with_cos, with_sin, mixed = loop(bands // group, one_group, (zero, zero, zero))
        lane = iota((height, half), 1)
        both, mixed = with_cos + with_sin, mixed + mixed
        ahead = jnp.where(lane == 0, with_cos, both + mixed)
        back = jnp.where(lane == 0, with_sin, both - mixed)
        row = pl.ds(block * height, height)
        held_ref[plane, row, :half] = ahead
        held_ref[plane, row, half:] = jnp.take_along_axis(
            back, jnp.where(lane == 0, 0, half - lane), axis=1
        )
        pltpu.make_async_copy(
            held_ref.at[plane, row], out_ref.at[plane, row], sem.at[step]
        ).start()
        return carry

    loop(own_planes * blocks, one_block, 0)
    for step in range(own_planes * blocks):
        where = (step // blocks, pl.ds(step % blocks * height, height))
        pltpu.make_async_copy(held_ref.at[where], out_ref.at[where], sem.at[step]).wait()


def shards(coeffs, rotation_matrix, stick_length, stick_column, plane_index, occupation):
    band_count = lax.axis_size("band")
    pw_count = lax.axis_size("pw")
    in_count, sticks, grid_len = coeffs.shape[1:]
    bands = rotation_matrix.shape[2]
    stick_count = stick_column.shape[0]
    own_planes = plane_index.shape[0] // pw_count
    spots = 2 * bands
    rows = own_planes * spots
    lanes = -(-(rows + bands) // LANES) * LANES
    vmem = pl.BlockSpec(memory_space=pltpu.VMEM)
    hbm = pl.BlockSpec(memory_space=pltpu.HBM)
    table_bytes = 6 * grid_len * stick_count
    message_bytes = 2 * stick_count * lanes

    def exchange(array, axis, offset):
        count = lax.axis_size(axis)
        return lax.ppermute(array, axis, [(place, place ^ offset) for place in range(count)])

    messages = pl.pallas_call(
        stick_kernel,
        out_shape=jax.ShapeDtypeStruct((pw_count, sticks, lanes), jnp.bfloat16),
        in_specs=[hbm] * 5,
        out_specs=vmem,
        scratch_shapes=[
            pltpu.SMEM(stick_length.shape, jnp.int32),
            pltpu.SMEM(plane_index.shape, jnp.int32),
            pltpu.SMEM(occupation.shape, jnp.int32),
            pltpu.VMEM((2, bands, in_count), jnp.bfloat16),
            pltpu.VMEM((2 * in_count * sticks, grid_len), jnp.bfloat16),
            pltpu.SemaphoreType.DMA((5,)),
        ],
        compiler_params=room(),
        name="stick_values",
    )(
        *(
            pltpu.with_memory_space_constraint(array, pltpu.HBM)
            for array in (
                stick_length,
                plane_index,
                occupation,
                jnp.swapaxes(rotation_matrix, 1, 2),
                coeffs.reshape(2 * in_count * sticks, grid_len),
            )
        )
    )
    gathered = [messages] + [exchange(messages, "band", place) for place in range(1, band_count)]
    parcel = jax.ShapeDtypeStruct((band_count, sticks, lanes), jnp.bfloat16)
    parcels = pl.pallas_call(
        regroup_kernel,
        out_shape=(parcel,) * pw_count,
        in_specs=[vmem] * band_count,
        out_specs=(vmem,) * pw_count,
        compiler_params=room(message_bytes),
        name="regroup",
    )(*gathered)
    arrived = [parcels[0]] + [
        exchange(parcels[offset], "pw", offset) for offset in range(pw_count - 1, 0, -1)
    ][::-1]
    column_row, own = lax.optimization_barrier(
        (stick_column.reshape(1, stick_count), parcels[0])
    )
    arrived[0] = own
    left, right = pl.pallas_call(
        functools.partial(table_kernel, grid_len, sticks),
        out_shape=(
            jax.ShapeDtypeStruct((2, grid_len, stick_count), jnp.bfloat16),
            jax.ShapeDtypeStruct((stick_count, grid_len), jnp.bfloat16),
        ),
        in_specs=[hbm],
        out_specs=(vmem, vmem),
        scratch_shapes=[pltpu.VMEM((1, stick_count), jnp.int32), pltpu.SemaphoreType.DMA],
        compiler_params=room(table_bytes),
        cost_estimate=pl.CostEstimate(
            flops=80 * grid_len * stick_count,
            bytes_accessed=12 * grid_len * stick_count,
            transcendentals=0,
        ),
        name="stick_tables",
    )(pltpu.with_memory_space_constraint(column_row, pltpu.HBM))
    chunk = min(grid_len, stick_count)
    norm_factor = 1.0 / float(bands * stick_count * grid_len)
    blocks = own_planes * (grid_len // math.gcd(grid_len, P_BLOCK))
    return pl.pallas_call(
        functools.partial(plane_kernel, bands, own_planes, norm_factor),
        out_shape=jax.ShapeDtypeStruct((own_planes, grid_len, grid_len), jnp.float32),
        in_specs=[vmem] * (pw_count + 2),
        out_specs=hbm,
        scratch_shapes=[
            pltpu.VMEM((band_count * pw_count, sticks, lanes), jnp.bfloat16),
            pltpu.VMEM((stick_count // chunk, rows, chunk), jnp.float32),
            pltpu.VMEM((bands, LANES), jnp.float32),
            pltpu.VMEM((own_planes, grid_len, grid_len), jnp.float32),
            pltpu.SemaphoreType.DMA((blocks,)),
        ],
        compiler_params=room(table_bytes, message_bytes),
        name="plane_density",
    )(*arrived, left, right)


def solution(mesh):
    return jax.shard_map(
        shards,
        mesh=mesh,
        in_specs=(P(None, None, ("band", "pw"), None), P(), P(), P(), P(), P("band")),
        out_specs=P("pw", None, None),
        check_vma=False,
    )
```

```python
import functools
import math

import jax
import jax.numpy as jnp
from jax import lax
from jax.experimental import pallas as pl
from jax.experimental.pallas import tpu as pltpu
from jax.sharding import PartitionSpec as P

LANES = 128
PACK = 16
P_BLOCK = 64
BAND_GROUP = 8
MIB = 1024 * 1024


def wrap(value, period):
    if period & (period - 1) == 0:
        return value & (period - 1)
    return lax.rem(value, period)


def cut(value, size):
    if size & (size - 1) == 0:
        return value >> (size.bit_length() - 1)
    return lax.div(value, size)


def cosine(index, period):
    fold = jnp.abs(wrap(index, period) - period // 2) - period // 4
    angle = fold.astype(jnp.float32) * (2.0 * math.pi / period)
    square = angle * angle
    series = -2.39e-08
    for factor in (2.7526e-06, -1.984090e-04, 8.3333315e-03, -1.666666664e-01, 1.0):
        series = series * square + factor
    return angle * series


def sine(index, period):
    return cosine(index + (period - period // 4), period)


def iota(shape, dim):
    return lax.broadcasted_iota(jnp.int32, shape, dim)


def dot_last(left, right):
    return lax.dot_general(
        left, right, (((1,), (1,)), ((), ())), preferred_element_type=jnp.float32
    )


def dot(left, right):
    return jnp.dot(left, right, preferred_element_type=jnp.float32)


def loop(count, body, carry):
    if count > 16:
        return lax.fori_loop(0, count, body, carry)
    for index in range(count):
        carry = body(index, carry)
    return carry


def room(*sizes):
    return pltpu.CompilerParams(vmem_limit_bytes=min(56 * MIB, 16 * MIB + 2 * sum(sizes)))


def spread(scalars, index, shape):
    result = jnp.full(shape, scalars[0])
    for place, scalar in enumerate(scalars[1:], 1):
        result = jnp.where(index == place, scalar, result)
    return result


def stick_kernel(
    length_hbm,
    plane_hbm,
    occupation_hbm,
    rotation_hbm,
    coeff_hbm,
    out_ref,
    length_ref,
    plane_ref,
    occupation_ref,
    rotation_ref,
    coeff_ref,
    sems,
):
    copies = [
        pltpu.make_async_copy(source, target, sems.at[index])
        for index, (source, target) in enumerate(
            (
                (rotation_hbm, rotation_ref),
                (coeff_hbm, coeff_ref),
                (plane_hbm, plane_ref),
                (length_hbm, length_ref),
                (occupation_hbm, occupation_ref),
            )
        )
    ]
    for copy in copies:
        copy.start()
    out_count, in_count = rotation_ref.shape[1:]
    grid_len = coeff_ref.shape[1]
    sticks = coeff_ref.shape[0] // (2 * in_count)
    plane_count = plane_ref.shape[0]
    pw_count = lax.axis_size("pw")
    own_planes = plane_count // pw_count
    own_bands = occupation_ref.shape[0]
    row_count = 2 * out_count * sticks
    band_index = lax.axis_index("band")
    first_stick = (band_index * pw_count + lax.axis_index("pw")) * sticks

    pick = (
        wrap(cut(iota((row_count, out_count), 0), sticks), out_count)
        == iota((row_count, out_count), 1)
    ).astype(jnp.bfloat16)
    copies[0].wait()
    from_real = dot(pick, rotation_ref[0])
    from_imag = dot(pick, rotation_ref[1])
    is_real = iota((row_count, in_count), 0) < out_count * sticks
    widen = (
        cut(iota((in_count, in_count * sticks), 1), sticks)
        == iota((in_count, in_count * sticks), 0)
    ).astype(jnp.bfloat16)
    shape = (row_count, in_count * sticks)
    same = wrap(iota(shape, 0), sticks) == wrap(iota(shape, 1), sticks)
    mixed = []
    for block in (
        jnp.where(is_real, from_real, from_imag),
        jnp.where(is_real, -from_imag, from_real),
    ):
        wide = dot(block.astype(jnp.bfloat16), widen)
        mixed.append(jnp.where(same, wide, 0.0).astype(jnp.bfloat16))
    rotation = jnp.concatenate(mixed, 1)

    for copy in copies[2:]:
        copy.wait()
    lengths = [length_ref[first_stick + place] for place in range(sticks)]
    planes = [plane_ref[place] for place in range(plane_count)]
    plane_rows = spread(planes, iota((plane_count, grid_len), 0), (plane_count, grid_len))
    product = iota((plane_count, grid_len), 1) * plane_rows
    table = jnp.concatenate([cosine(product, grid_len), sine(product, grid_len)], 0).astype(
        jnp.bfloat16
    )

    shape = (plane_count, row_count)
    lane_lengths = spread(lengths, wrap(iota(shape, 1), sticks), shape)
    shift = (lane_lengths >> 1) * spread(planes, iota(shape, 0), shape)
    phase_cos = cosine(shift, grid_len)
    phase_sin = sine(shift, grid_len)
    real_lane = iota(shape, 1) < row_count // 2

    row_lengths = spread(lengths, iota((sticks, grid_len), 0), (sticks, grid_len))
    live = iota((sticks, grid_len), 1) < row_lengths

    copies[1].wait()
    rotated = dot(rotation, coeff_ref[...])
    rotated = rotated.reshape(row_count // sticks, sticks, grid_len)
    rotated = jnp.where(live[None], rotated, 0.0).reshape(row_count, grid_len)
    sums = dot_last(table, rotated.astype(jnp.bfloat16))
    with_cos, with_sin = sums[:plane_count], sums[plane_count:]
    turned = pltpu.roll(with_sin, row_count // 2, 1)
    amplitude = with_cos + jnp.where(real_lane, -turned, turned)
    turned = pltpu.roll(amplitude, row_count // 2, 1) * phase_sin
    values = amplitude * phase_cos + jnp.where(real_lane, turned, -turned)

    lanes = out_ref.shape[2]
    spots = 2 * out_count
    tall = jnp.broadcast_to(values[:, None, :], (plane_count, sticks, row_count))
    own = iota((sticks, row_count), 0) == wrap(iota((sticks, row_count), 1), sticks)
    tall = jnp.where(own[None], tall, 0.0).reshape(plane_count * sticks, row_count)
    shape = (row_count, lanes)
    place = (
        (cut(iota(shape, 0), sticks) == lax.rem(iota(shape, 1), spots))
        & (iota(shape, 1) < own_planes * spots)
    ).astype(jnp.bfloat16)
    laid = dot(tall.astype(jnp.bfloat16), place).reshape(pw_count, own_planes, sticks, lanes)
    mine = cut(iota((own_planes, sticks, lanes), 2), spots) == iota((own_planes, sticks, lanes), 0)
    message = jnp.sum(jnp.where(mine[None], laid, 0.0), 1)
    occupied = jnp.zeros((sticks, lanes), jnp.int32)
    for own_band in range(own_bands):
        lane = own_planes * spots + band_index * own_bands + own_band
        occupied = jnp.where(
            iota((sticks, lanes), 1) == lane, occupation_ref[own_band], occupied
        )
    message = (message + occupied.astype(jnp.float32)[None]).astype(out_ref.dtype)
    for band in range(out_ref.shape[0] // pw_count):
        out_ref[band * pw_count : (band + 1) * pw_count] = message


def table_kernel(grid_len, column_hbm, left_ref, right_ref, column_ref, sem):
    copy = pltpu.make_async_copy(column_hbm, column_ref, sem)
    copy.start()
    copy.wait()
    count = column_ref.shape[1]
    half = grid_len // 2
    columns = column_ref[...]
    turns = iota((grid_len, count), 0) * cut(columns, grid_len)
    left_ref[0] = cosine(turns, grid_len).astype(jnp.bfloat16)
    left_ref[1] = sine(turns, grid_len).astype(jnp.bfloat16)
    tall = jnp.transpose(jnp.broadcast_to(wrap(columns, grid_len), (half, count)))
    freq = iota((count, half), 1)
    right_ref[:, :half] = cosine(tall * freq, grid_len).astype(jnp.bfloat16)
    turns = jnp.where(freq == 0, tall * half, tall * freq + (grid_len - grid_len // 4))
    right_ref[:, half:] = cosine(turns, grid_len).astype(jnp.bfloat16)


def plane_kernel(
    bands,
    own_planes,
    norm_factor,
    message_ref,
    left_ref,
    right_ref,
    out_ref,
    value_ref,
    weight_ref,
    held_ref,
    sem,
):
    chunks, rows, chunk = value_ref.shape
    grid_len = out_ref.shape[1]
    half = grid_len // 2
    sticks, lanes = message_ref.shape[1:]
    spots = 2 * bands
    height = math.gcd(grid_len, P_BLOCK)
    blocks = grid_len // height
    group = math.gcd(bands, BAND_GROUP)
    select = (iota((rows + bands, lanes), 0) == iota((rows + bands, lanes), 1)).astype(
        jnp.bfloat16
    )

    def turn(index, peak):
        pieces = chunk // sticks
        picked = dot_last(
            select, message_ref[pl.ds(index * pieces, pieces)].reshape(chunk, lanes)
        )
        value_ref[index] = picked[:rows]
        return jnp.maximum(peak, jnp.max(picked[rows:], 1, keepdims=True))

    peak = loop(chunks, turn, jnp.zeros((bands, 1), jnp.float32))
    weight_ref[...] = jnp.broadcast_to(peak * norm_factor, weight_ref.shape)

    def stick_sums(index, plane, block, first_band):
        lane = pl.ds(index * chunk, chunk)
        row = pl.ds(block * height, height)
        cos_table = left_ref[0, row, lane].reshape(height // PACK, PACK, chunk)
        sin_table = left_ref[1, row, lane].reshape(height // PACK, PACK, chunk)
        parts = []
        for band in range(group):
            at = plane * spots + first_band + band
            real, imag = (
                jnp.broadcast_to(value_ref[index, pl.ds(spot, 1), :], (PACK, chunk)).astype(
                    jnp.bfloat16
                )[None]
                for spot in (at, at + bands)
            )
            parts.append((cos_table * real - sin_table * imag).reshape(height, chunk))
            parts.append((sin_table * real + cos_table * imag).reshape(height, chunk))
        return dot(jnp.concatenate(parts, 0), right_ref[pl.ds(index * chunk, chunk), :])

    def one_block(step, carry):
        plane, block = step // blocks, step % blocks

        def one_group(index, sums):
            first_band = index * group
            if chunks == 1:
                found = stick_sums(0, plane, block, first_band)
            else:
                found = lax.fori_loop(
                    0,
                    chunks,
                    lambda at, so_far: so_far + stick_sums(at, plane, block, first_band),
                    jnp.zeros((2 * group * height, grid_len), jnp.float32),
                )
            with_cos, with_sin, mixed = sums
            for band in range(group):
                top = 2 * band * height
                a, d = found[top : top + height, :half], found[top : top + height, half:]
                top += height
                c, b = found[top : top + height, :half], found[top : top + height, half:]
                weight = weight_ref[pl.ds(first_band + band, 1), :half]
                with_cos += weight * (a * a + c * c)
                with_sin += weight * (b * b + d * d)
                mixed += weight * (c * d - a * b)
            return with_cos, with_sin, mixed

        zero = jnp.zeros((height, half), jnp.float32)
        with_cos, with_sin, mixed = loop(bands // group, one_group, (zero, zero, zero))
        lane = iota((height, half), 1)
        both, mixed = with_cos + with_sin, mixed + mixed
        ahead = jnp.where(lane == 0, with_cos, both + mixed)
        back = jnp.where(lane == 0, with_sin, both - mixed)
        row = pl.ds(block * height, height)
        held_ref[plane, row, :half] = ahead
        held_ref[plane, row, half:] = jnp.take_along_axis(
            back, jnp.where(lane == 0, 0, half - lane), axis=1
        )
        pltpu.make_async_copy(
            held_ref.at[plane, row], out_ref.at[plane, row], sem.at[step]
        ).start()
        return carry

    loop(own_planes * blocks, one_block, 0)
    for step in range(own_planes * blocks):
        where = (step // blocks, pl.ds(step % blocks * height, height))
        pltpu.make_async_copy(held_ref.at[where], out_ref.at[where], sem.at[step]).wait()


def shards(coeffs, rotation_matrix, stick_length, stick_column, plane_index, occupation):
    band_count = lax.axis_size("band")
    pw_count = lax.axis_size("pw")
    devices = band_count * pw_count
    in_count, sticks, grid_len = coeffs.shape[1:]
    bands = rotation_matrix.shape[2]
    stick_count = stick_column.shape[0]
    own_planes = plane_index.shape[0] // pw_count
    spots = 2 * bands
    rows = own_planes * spots
    lanes = -(-(rows + bands) // LANES) * LANES
    vmem = pl.BlockSpec(memory_space=pltpu.VMEM)
    hbm = pl.BlockSpec(memory_space=pltpu.HBM)
    table_bytes = 6 * grid_len * stick_count
    message_bytes = 2 * stick_count * lanes

    messages = pl.pallas_call(
        stick_kernel,
        out_shape=jax.ShapeDtypeStruct((devices, sticks, lanes), jnp.bfloat16),
        in_specs=[hbm] * 5,
        out_specs=vmem,
        scratch_shapes=[
            pltpu.SMEM(stick_length.shape, jnp.int32),
            pltpu.SMEM(plane_index.shape, jnp.int32),
            pltpu.SMEM(occupation.shape, jnp.int32),
            pltpu.VMEM((2, bands, in_count), jnp.bfloat16),
            pltpu.VMEM((2 * in_count * sticks, grid_len), jnp.bfloat16),
            pltpu.SemaphoreType.DMA((5,)),
        ],
        compiler_params=room(2 * message_bytes),
        name="stick_values",
    )(
        *(
            pltpu.with_memory_space_constraint(array, pltpu.HBM)
            for array in (
                stick_length,
                plane_index,
                occupation,
                jnp.swapaxes(rotation_matrix, 1, 2),
                coeffs.reshape(2 * in_count * sticks, grid_len),
            )
        )
    )
    arrived = lax.all_to_all(messages, ("band", "pw"), split_axis=0, concat_axis=0, tiled=True)
    left, right = pl.pallas_call(
        functools.partial(table_kernel, grid_len),
        out_shape=(
            jax.ShapeDtypeStruct((2, grid_len, stick_count), jnp.bfloat16),
            jax.ShapeDtypeStruct((stick_count, grid_len), jnp.bfloat16),
        ),
        in_specs=[hbm],
        out_specs=(vmem, vmem),
        scratch_shapes=[pltpu.VMEM((1, stick_count), jnp.int32), pltpu.SemaphoreType.DMA],
        compiler_params=room(table_bytes),
        cost_estimate=pl.CostEstimate(
            flops=80 * grid_len * stick_count,
            bytes_accessed=12 * grid_len * stick_count,
            transcendentals=0,
        ),
        name="stick_tables",
    )(pltpu.with_memory_space_constraint(stick_column.reshape(1, stick_count), pltpu.HBM))
    chunk = min(grid_len, stick_count)
    norm_factor = 1.0 / float(bands * stick_count * grid_len)
    blocks = own_planes * (grid_len // math.gcd(grid_len, P_BLOCK))
    return pl.pallas_call(
        functools.partial(plane_kernel, bands, own_planes, norm_factor),
        out_shape=jax.ShapeDtypeStruct((own_planes, grid_len, grid_len), jnp.float32),
        in_specs=[vmem] * 3,
        out_specs=hbm,
        scratch_shapes=[
            pltpu.VMEM((stick_count // chunk, rows, chunk), jnp.float32),
            pltpu.VMEM((bands, LANES), jnp.float32),
            pltpu.VMEM((own_planes, grid_len, grid_len), jnp.float32),
            pltpu.SemaphoreType.DMA((blocks,)),
        ],
        compiler_params=room(table_bytes, message_bytes),
        name="plane_density",
    )(arrived, left, right)


def solution(mesh):
    return jax.shard_map(
        shards,
        mesh=mesh,
        in_specs=(P(None, None, ("band", "pw"), None), P(), P(), P(), P(), P("band")),
        out_specs=P("pw", None, None),
        check_vma=False,
    )
```

```python
import functools
import math

import jax
import jax.numpy as jnp
from jax import lax
from jax.experimental import pallas as pl
from jax.experimental.pallas import tpu as pltpu
from jax.sharding import PartitionSpec as P

LANES = 128
PACK = 16
P_BLOCK = 64
BAND_GROUP = 8
MIB = 1024 * 1024


def wrap(value, period):
    if period & (period - 1) == 0:
        return value & (period - 1)
    return lax.rem(value, period)


def cut(value, size):
    if size & (size - 1) == 0:
        return value >> (size.bit_length() - 1)
    return lax.div(value, size)


def cosine(index, period):
    fold = jnp.abs(wrap(index, period) - period // 2) - period // 4
    angle = fold.astype(jnp.float32) * (2.0 * math.pi / period)
    square = angle * angle
    series = -2.39e-08
    for factor in (2.7526e-06, -1.984090e-04, 8.3333315e-03, -1.666666664e-01, 1.0):
        series = series * square + factor
    return angle * series


def sine(index, period):
    return cosine(index + (period - period // 4), period)


def iota(shape, dim):
    return lax.broadcasted_iota(jnp.int32, shape, dim)


def dot_last(left, right):
    return lax.dot_general(
        left, right, (((1,), (1,)), ((), ())), preferred_element_type=jnp.float32
    )


def dot(left, right):
    return jnp.dot(left, right, preferred_element_type=jnp.float32)


def loop(count, body, carry):
    if count > 16:
        return lax.fori_loop(0, count, body, carry)
    for index in range(count):
        carry = body(index, carry)
    return carry


def room(*sizes):
    return pltpu.CompilerParams(vmem_limit_bytes=min(56 * MIB, 16 * MIB + 2 * sum(sizes)))


def message_form(sticks, own_planes, bands):
    spots = own_planes * 2 * bands
    lanes = -(-spots // LANES) * LANES
    groups = math.gcd(sticks, lanes // spots)
    value_rows = sticks // groups
    rows = 1
    while rows < value_rows + 1:
        rows *= 2
    return groups, value_rows, rows, lanes


def spread(scalars, index, shape):
    result = jnp.full(shape, scalars[0])
    for place, scalar in enumerate(scalars[1:], 1):
        result = jnp.where(index == place, scalar, result)
    return result


def stick_kernel(
    length_hbm,
    plane_hbm,
    occupation_hbm,
    rotation_hbm,
    coeff_hbm,
    out_ref,
    length_ref,
    plane_ref,
    occupation_ref,
    rotation_ref,
    coeff_ref,
    sems,
):
    copies = [
        pltpu.make_async_copy(source, target, sems.at[index])
        for index, (source, target) in enumerate(
            (
                (rotation_hbm, rotation_ref),
                (coeff_hbm, coeff_ref),
                (plane_hbm, plane_ref),
                (length_hbm, length_ref),
                (occupation_hbm, occupation_ref),
            )
        )
    ]
    for copy in copies:
        copy.start()
    out_count, in_count = rotation_ref.shape[1:]
    grid_len = coeff_ref.shape[1]
    sticks = coeff_ref.shape[0] // (2 * in_count)
    plane_count = plane_ref.shape[1]
    pw_count = lax.axis_size("pw")
    own_planes = plane_count // pw_count
    own_bands = occupation_ref.shape[0]
    row_count = 2 * out_count * sticks
    groups, value_rows, message_rows, lanes = message_form(sticks, own_planes, out_count)
    band_index = lax.axis_index("band")
    first_stick = (band_index * pw_count + lax.axis_index("pw")) * sticks

    pick = (
        wrap(cut(iota((row_count, out_count), 0), sticks), out_count)
        == iota((row_count, out_count), 1)
    ).astype(jnp.bfloat16)
    copies[0].wait()
    from_real = dot(pick, rotation_ref[0])
    from_imag = dot(pick, rotation_ref[1])
    is_real = iota((row_count, in_count), 0) < out_count * sticks
    widen = (
        cut(iota((in_count, in_count * sticks), 1), sticks)
        == iota((in_count, in_count * sticks), 0)
    ).astype(jnp.bfloat16)
    shape = (row_count, in_count * sticks)
    same = wrap(iota(shape, 0), sticks) == wrap(iota(shape, 1), sticks)
    mixed = []
    for block in (
        jnp.where(is_real, from_real, from_imag),
        jnp.where(is_real, -from_imag, from_real),
    ):
        wide = dot(block.astype(jnp.bfloat16), widen)
        mixed.append(jnp.where(same, wide, 0.0).astype(jnp.bfloat16))
    rotation = jnp.concatenate(mixed, 1)

    for copy in copies[2:]:
        copy.wait()
    tall = plane_count * message_rows
    shape = (tall, plane_count)
    kind = cut(iota(shape, 0), message_rows)
    plane_of = lax.rem(kind, pw_count) * own_planes + lax.div(kind, pw_count)
    planes = jnp.broadcast_to(plane_ref[...].astype(jnp.float32), (grid_len, plane_count))
    plane_rows = dot_last(
        (plane_of == iota(shape, 1)).astype(jnp.bfloat16), planes.astype(jnp.bfloat16)
    ).astype(jnp.int32)
    product = iota((tall, grid_len), 1) * plane_rows
    table = jnp.concatenate([cosine(product, grid_len), sine(product, grid_len)], 0).astype(
        jnp.bfloat16
    )

    lengths = [length_ref[first_stick + place] for place in range(sticks)]
    shape = (1, row_count)
    lane_lengths = spread(lengths, wrap(iota(shape, 1), sticks), shape)
    repeats = -(-row_count // grid_len)
    wide_planes = jnp.concatenate([plane_rows] * repeats, 1)[:, :row_count]
    shift = (lane_lengths >> 1) * wide_planes
    phase_cos = cosine(shift, grid_len)
    phase_sin = sine(shift, grid_len)
    shape = (tall, row_count)
    real_lane = iota(shape, 1) < row_count // 2

    row_lengths = spread(lengths, iota((sticks, grid_len), 0), (sticks, grid_len))
    live = iota((sticks, grid_len), 1) < row_lengths

    stick_of = wrap(iota(shape, 1), sticks)
    in_row = lax.rem(stick_of, value_rows) == wrap(iota(shape, 0), message_rows)
    shape = (row_count, lanes)
    spots = 2 * out_count
    to_lane = iota(shape, 1)
    from_stick = wrap(iota(shape, 0), sticks)
    place = (
        (cut(iota(shape, 0), sticks) == lax.rem(to_lane, spots))
        & (lax.div(from_stick, value_rows) == lax.div(to_lane, own_planes * spots))
    ).astype(jnp.bfloat16)
    part_rows = pw_count * message_rows
    shape = (part_rows, lanes)
    plane_lane = lax.div(lax.rem(iota(shape, 1), own_planes * spots), spots)
    message = jnp.zeros(shape, jnp.float32)
    is_occupation = wrap(iota(shape, 0), message_rows) == value_rows
    for own_band in range(own_bands):
        lane = band_index * own_bands + own_band
        message = jnp.where(
            is_occupation & (iota(shape, 1) == lane),
            occupation_ref[own_band].astype(jnp.float32),
            message,
        )

    copies[1].wait()
    rotated = dot(rotation, coeff_ref[...])
    rotated = rotated.reshape(row_count // sticks, sticks, grid_len)
    rotated = jnp.where(live[None], rotated, 0.0).reshape(row_count, grid_len)
    sums = dot_last(table, rotated.astype(jnp.bfloat16))
    with_cos, with_sin = sums[:tall], sums[tall:]
    turned = pltpu.roll(with_sin, row_count // 2, 1)
    amplitude = with_cos + jnp.where(real_lane, -turned, turned)
    turned = pltpu.roll(amplitude, row_count // 2, 1) * phase_sin
    values = amplitude * phase_cos + jnp.where(real_lane, turned, -turned)
    laid = dot(jnp.where(in_row, values, 0.0).astype(jnp.bfloat16), place)
    for own_plane in range(own_planes):
        part = laid[own_plane * part_rows : (own_plane + 1) * part_rows]
        message += jnp.where(plane_lane == own_plane, part, 0.0)
    message = message.astype(out_ref.dtype).reshape(pw_count, message_rows, lanes)
    for band in range(out_ref.shape[0] // pw_count):
        out_ref[band * pw_count : (band + 1) * pw_count] = message


def table_kernel(grid_len, chunk, sticks, value_rows, column_hbm, left_ref, right_ref, column_ref, sem):
    copy = pltpu.make_async_copy(column_hbm, column_ref, sem)
    copy.start()
    copy.wait()
    count = column_ref.shape[1]
    half = grid_len // 2
    shape = (chunk, chunk)
    to, pieces = iota(shape, 1), chunk // sticks
    group, rest = lax.div(to, pieces * value_rows), lax.rem(to, pieces * value_rows)
    source = lax.div(rest, value_rows) * sticks + group * value_rows + lax.rem(rest, value_rows)
    order = (iota(shape, 0) == source).astype(jnp.bfloat16)
    columns = jnp.broadcast_to(column_ref[...], (8, count))
    columns = jnp.where(
        iota((8, count), 0) == 0, cut(columns, grid_len), wrap(columns, grid_len)
    ).astype(jnp.float32)
    ordered = [
        dot(columns[:, first : first + chunk].astype(jnp.bfloat16), order)
        for first in range(0, count, chunk)
    ]
    columns = jnp.concatenate(ordered, 1).astype(jnp.int32)
    turns = iota((grid_len, count), 0) * columns[:1]
    left_ref[0] = cosine(turns, grid_len).astype(jnp.bfloat16)
    left_ref[1] = sine(turns, grid_len).astype(jnp.bfloat16)
    tall = jnp.transpose(jnp.broadcast_to(columns[1:2], (half, count)))
    freq = iota((count, half), 1)
    right_ref[:, :half] = cosine(tall * freq, grid_len).astype(jnp.bfloat16)
    turns = jnp.where(freq == 0, tall * half, tall * freq + (grid_len - grid_len // 4))
    right_ref[:, half:] = cosine(turns, grid_len).astype(jnp.bfloat16)


def plane_kernel(
    bands,
    own_planes,
    norm_factor,
    sticks,
    message_ref,
    left_ref,
    right_ref,
    out_ref,
    value_ref,
    weight_ref,
    held_ref,
    sem,
):
    chunks, rows, chunk = value_ref.shape
    grid_len = out_ref.shape[1]
    half = grid_len // 2
    spots = 2 * bands
    height = math.gcd(grid_len, P_BLOCK)
    blocks = grid_len // height
    group = math.gcd(bands, BAND_GROUP)
    groups, value_rows, message_rows, lanes = message_form(sticks, own_planes, bands)
    source_rows = chunk // sticks * message_rows
    shape = (chunk, source_rows)
    wanted = lax.rem(iota(shape, 0), chunk // groups)
    gather = (
        lax.div(wanted, value_rows) * message_rows + lax.rem(wanted, value_rows) == iota(shape, 1)
    ).astype(jnp.bfloat16)
    shape = (chunk, lanes)
    in_group = lax.div(iota(shape, 0), chunk // groups) == lax.div(iota(shape, 1), rows)
    shape = (rows, lanes)
    select = (lax.rem(iota(shape, 1), rows) == iota(shape, 0)).astype(jnp.bfloat16)
    shape = (bands, lanes)
    select_band = (iota(shape, 1) == iota(shape, 0)).astype(jnp.bfloat16)
    is_occupation = wrap(iota((bands, source_rows), 1), message_rows) == value_rows

    def turn(index, peak):
        pieces = chunk // sticks
        message = message_ref[pl.ds(index * pieces, pieces)].reshape(source_rows, lanes)
        picked = jnp.where(in_group, dot(gather, message), 0.0).astype(jnp.bfloat16)
        value_ref[index] = dot_last(select, picked)
        found = jnp.where(is_occupation, dot_last(select_band, message), 0.0)
        return jnp.maximum(peak, jnp.max(found, 1, keepdims=True))

    peak = loop(chunks, turn, jnp.zeros((bands, 1), jnp.float32))
    weight_ref[...] = jnp.broadcast_to(peak * norm_factor, weight_ref.shape)

    def stick_sums(index, plane, block, first_band):
        lane = pl.ds(index * chunk, chunk)
        row = pl.ds(block * height, height)
        cos_table = left_ref[0, row, lane].reshape(height // PACK, PACK, chunk)
        sin_table = left_ref[1, row, lane].reshape(height // PACK, PACK, chunk)
        parts = []
        for band in range(group):
            at = plane * spots + first_band + band
            real, imag = (
                jnp.broadcast_to(value_ref[index, pl.ds(spot, 1), :], (PACK, chunk)).astype(
                    jnp.bfloat16
                )[None]
                for spot in (at, at + bands)
            )
            parts.append((cos_table * real - sin_table * imag).reshape(height, chunk))
            parts.append((sin_table * real + cos_table * imag).reshape(height, chunk))
        return dot(jnp.concatenate(parts, 0), right_ref[pl.ds(index * chunk, chunk), :])

    def one_block(step, carry):
        plane, block = step // blocks, step % blocks

        def one_group(index, sums):
            first_band = index * group
            if chunks == 1:
                found = stick_sums(0, plane, block, first_band)
            else:
                found = lax.fori_loop(
                    0,
                    chunks,
                    lambda at, so_far: so_far + stick_sums(at, plane, block, first_band),
                    jnp.zeros((2 * group * height, grid_len), jnp.float32),
                )
            with_cos, with_sin, mixed = sums
            for band in range(group):
                top = 2 * band * height
                a, d = found[top : top + height, :half], found[top : top + height, half:]
                top += height
                c, b = found[top : top + height, :half], found[top : top + height, half:]
                weight = weight_ref[pl.ds(first_band + band, 1), :half]
                with_cos += weight * (a * a + c * c)
                with_sin += weight * (b * b + d * d)
                mixed += weight * (c * d - a * b)
            return with_cos, with_sin, mixed

        zero = jnp.zeros((height, half), jnp.float32)
        with_cos, with_sin, mixed = loop(bands // group, one_group, (zero, zero, zero))
        lane = iota((height, half), 1)
        both, mixed = with_cos + with_sin, mixed + mixed
        ahead = jnp.where(lane == 0, with_cos, both + mixed)
        back = jnp.where(lane == 0, with_sin, both - mixed)
        row = pl.ds(block * height, height)
        held_ref[plane, row, :half] = ahead
        held_ref[plane, row, half:] = jnp.take_along_axis(
            back, jnp.where(lane == 0, 0, half - lane), axis=1
        )
        pltpu.make_async_copy(
            held_ref.at[plane, row], out_ref.at[plane, row], sem.at[step]
        ).start()
        return carry

    loop(own_planes * blocks, one_block, 0)
    for step in range(own_planes * blocks):
        where = (step // blocks, pl.ds(step % blocks * height, height))
        pltpu.make_async_copy(held_ref.at[where], out_ref.at[where], sem.at[step]).wait()


def shards(coeffs, rotation_matrix, stick_length, stick_column, plane_index, occupation):
    band_count = lax.axis_size("band")
    pw_count = lax.axis_size("pw")
    devices = band_count * pw_count
    in_count, sticks, grid_len = coeffs.shape[1:]
    bands = rotation_matrix.shape[2]
    stick_count = stick_column.shape[0]
    own_planes = plane_index.shape[0] // pw_count
    spots = 2 * bands
    rows = own_planes * spots
    groups, value_rows, message_rows, lanes = message_form(sticks, own_planes, bands)
    vmem = pl.BlockSpec(memory_space=pltpu.VMEM)
    hbm = pl.BlockSpec(memory_space=pltpu.HBM)
    table_bytes = 6 * grid_len * stick_count
    message_bytes = 2 * devices * message_rows * lanes

    messages = pl.pallas_call(
        stick_kernel,
        out_shape=jax.ShapeDtypeStruct((devices, message_rows, lanes), jnp.bfloat16),
        in_specs=[hbm] * 5,
        out_specs=vmem,
        scratch_shapes=[
            pltpu.SMEM(stick_length.shape, jnp.int32),
            pltpu.VMEM((1, plane_index.shape[0]), jnp.int32),
            pltpu.SMEM(occupation.shape, jnp.int32),
            pltpu.VMEM((2, bands, in_count), jnp.bfloat16),
            pltpu.VMEM((2 * in_count * sticks, grid_len), jnp.bfloat16),
            pltpu.SemaphoreType.DMA((5,)),
        ],
        compiler_params=room(2 * message_bytes),
        name="stick_values",
    )(
        *(
            pltpu.with_memory_space_constraint(array, pltpu.HBM)
            for array in (
                stick_length,
                plane_index.reshape(1, -1),
                occupation,
                jnp.swapaxes(rotation_matrix, 1, 2),
                coeffs.reshape(2 * in_count * sticks, grid_len),
            )
        )
    )
    arrived = lax.all_to_all(messages, ("band", "pw"), split_axis=0, concat_axis=0, tiled=True)
    chunk = min(grid_len, stick_count)
    left, right = pl.pallas_call(
        functools.partial(table_kernel, grid_len, chunk, sticks, value_rows),
        out_shape=(
            jax.ShapeDtypeStruct((2, grid_len, stick_count), jnp.bfloat16),
            jax.ShapeDtypeStruct((stick_count, grid_len), jnp.bfloat16),
        ),
        in_specs=[hbm],
        out_specs=(vmem, vmem),
        scratch_shapes=[pltpu.VMEM((1, stick_count), jnp.int32), pltpu.SemaphoreType.DMA],
        compiler_params=room(table_bytes),
        cost_estimate=pl.CostEstimate(
            flops=80 * grid_len * stick_count,
            bytes_accessed=12 * grid_len * stick_count,
            transcendentals=0,
        ),
        name="stick_tables",
    )(pltpu.with_memory_space_constraint(stick_column.reshape(1, stick_count), pltpu.HBM))
    norm_factor = 1.0 / float(bands * stick_count * grid_len)
    blocks = own_planes * (grid_len // math.gcd(grid_len, P_BLOCK))
    return pl.pallas_call(
        functools.partial(plane_kernel, bands, own_planes, norm_factor, sticks),
        out_shape=jax.ShapeDtypeStruct((own_planes, grid_len, grid_len), jnp.float32),
        in_specs=[vmem] * 3,
        out_specs=hbm,
        scratch_shapes=[
            pltpu.VMEM((stick_count // chunk, rows, chunk), jnp.float32),
            pltpu.VMEM((bands, LANES), jnp.float32),
            pltpu.VMEM((own_planes, grid_len, grid_len), jnp.float32),
            pltpu.SemaphoreType.DMA((blocks,)),
        ],
        compiler_params=room(table_bytes, message_bytes),
        name="plane_density",
    )(arrived, left, right)


def solution(mesh):
    return jax.shard_map(
        shards,
        mesh=mesh,
        in_specs=(P(None, None, ("band", "pw"), None), P(), P(), P(), P(), P("band")),
        out_specs=P("pw", None, None),
        check_vma=False,
    )
```

```python
import functools
import math

import jax
import jax.numpy as jnp
from jax import lax
from jax.experimental import pallas as pl
from jax.experimental.pallas import tpu as pltpu
from jax.sharding import PartitionSpec as P

LANES = 128
PACK = 16
P_BLOCK = 32
BAND_GROUP = 8
MIB = 1024 * 1024


def wrap(value, period):
    if period & (period - 1) == 0:
        return value & (period - 1)
    return lax.rem(value, period)


def cut(value, size):
    if size & (size - 1) == 0:
        return value >> (size.bit_length() - 1)
    return lax.div(value, size)


def cosine(index, period):
    fold = jnp.abs(wrap(index, period) - period // 2) - period // 4
    angle = fold.astype(jnp.float32) * (2.0 * math.pi / period)
    square = angle * angle
    series = -2.39e-08
    for factor in (2.7526e-06, -1.984090e-04, 8.3333315e-03, -1.666666664e-01, 1.0):
        series = series * square + factor
    return angle * series


def sine(index, period):
    return cosine(index + (period - period // 4), period)


def iota(shape, dim):
    return lax.broadcasted_iota(jnp.int32, shape, dim)


def dot_last(left, right):
    return lax.dot_general(
        left, right, (((1,), (1,)), ((), ())), preferred_element_type=jnp.float32
    )


def dot(left, right):
    return jnp.dot(left, right, preferred_element_type=jnp.float32)


def loop(count, body, carry):
    if count > 16:
        return lax.fori_loop(0, count, body, carry)
    for index in range(count):
        carry = body(index, carry)
    return carry


def room(*sizes):
    return pltpu.CompilerParams(vmem_limit_bytes=min(56 * MIB, 16 * MIB + 2 * sum(sizes)))


def spread(scalars, index, shape):
    result = jnp.full(shape, scalars[0])
    for place, scalar in enumerate(scalars[1:], 1):
        result = jnp.where(index == place, scalar, result)
    return result


def stick_kernel(
    length_hbm,
    plane_hbm,
    occupation_hbm,
    rotation_hbm,
    coeff_hbm,
    out_ref,
    length_ref,
    plane_ref,
    occupation_ref,
    rotation_ref,
    coeff_ref,
    sems,
):
    copies = [
        pltpu.make_async_copy(source, target, sems.at[index])
        for index, (source, target) in enumerate(
            (
                (rotation_hbm, rotation_ref),
                (coeff_hbm, coeff_ref),
                (plane_hbm, plane_ref),
                (length_hbm, length_ref),
                (occupation_hbm, occupation_ref),
            )
        )
    ]
    for copy in copies:
        copy.start()
    out_count, in_count = rotation_ref.shape[1:]
    grid_len = coeff_ref.shape[1]
    sticks = coeff_ref.shape[0] // (2 * in_count)
    plane_count = plane_ref.shape[0]
    pw_count = lax.axis_size("pw")
    own_planes = plane_count // pw_count
    own_bands = occupation_ref.shape[0]
    row_count = 2 * out_count * sticks
    band_index = lax.axis_index("band")
    first_stick = (band_index * pw_count + lax.axis_index("pw")) * sticks

    pick = (
        wrap(cut(iota((row_count, out_count), 0), sticks), out_count)
        == iota((row_count, out_count), 1)
    ).astype(jnp.bfloat16)
    copies[0].wait()
    from_real = dot(pick, rotation_ref[0])
    from_imag = dot(pick, rotation_ref[1])
    is_real = iota((row_count, in_count), 0) < out_count * sticks
    widen = (
        cut(iota((in_count, in_count * sticks), 1), sticks)
        == iota((in_count, in_count * sticks), 0)
    ).astype(jnp.bfloat16)
    shape = (row_count, in_count * sticks)
    same = wrap(iota(shape, 0), sticks) == wrap(iota(shape, 1), sticks)
    mixed = []
    for block in (
        jnp.where(is_real, from_real, from_imag),
        jnp.where(is_real, -from_imag, from_real),
    ):
        wide = dot(block.astype(jnp.bfloat16), widen)
        mixed.append(jnp.where(same, wide, 0.0).astype(jnp.bfloat16))
    rotation = jnp.concatenate(mixed, 1)

    for copy in copies[2:]:
        copy.wait()
    lengths = [length_ref[first_stick + place] for place in range(sticks)]
    planes = [plane_ref[place] for place in range(plane_count)]
    plane_rows = spread(planes, iota((plane_count, grid_len), 0), (plane_count, grid_len))
    product = iota((plane_count, grid_len), 1) * plane_rows
    table = jnp.concatenate([cosine(product, grid_len), sine(product, grid_len)], 0).astype(
        jnp.bfloat16
    )

    shape = (plane_count, row_count)
    lane_lengths = spread(lengths, wrap(iota(shape, 1), sticks), shape)
    shift = (lane_lengths >> 1) * spread(planes, iota(shape, 0), shape)
    phase_cos = cosine(shift, grid_len)
    phase_sin = sine(shift, grid_len)
    real_lane = iota(shape, 1) < row_count // 2

    row_lengths = spread(lengths, iota((sticks, grid_len), 0), (sticks, grid_len))
    live = iota((sticks, grid_len), 1) < row_lengths

    copies[1].wait()
    rotated = dot(rotation, coeff_ref[...])
    rotated = rotated.reshape(row_count // sticks, sticks, grid_len)
    rotated = jnp.where(live[None], rotated, 0.0).reshape(row_count, grid_len)
    sums = dot_last(table, rotated.astype(jnp.bfloat16))
    with_cos, with_sin = sums[:plane_count], sums[plane_count:]
    turned = pltpu.roll(with_sin, row_count // 2, 1)
    amplitude = with_cos + jnp.where(real_lane, -turned, turned)
    turned = pltpu.roll(amplitude, row_count // 2, 1) * phase_sin
    values = amplitude * phase_cos + jnp.where(real_lane, turned, -turned)

    lanes = out_ref.shape[2]
    spots = 2 * out_count
    tall = jnp.broadcast_to(values[:, None, :], (plane_count, sticks, row_count))
    own = iota((sticks, row_count), 0) == wrap(iota((sticks, row_count), 1), sticks)
    tall = jnp.where(own[None], tall, 0.0).reshape(plane_count * sticks, row_count)
    shape = (row_count, lanes)
    place = (
        (cut(iota(shape, 0), sticks) == lax.rem(iota(shape, 1), spots))
        & (iota(shape, 1) < own_planes * spots)
    ).astype(jnp.bfloat16)
    laid = dot(tall.astype(jnp.bfloat16), place).reshape(pw_count, own_planes, sticks, lanes)
    mine = cut(iota((own_planes, sticks, lanes), 2), spots) == iota((own_planes, sticks, lanes), 0)
    message = jnp.sum(jnp.where(mine[None], laid, 0.0), 1)
    occupied = jnp.zeros((sticks, lanes), jnp.int32)
    for own_band in range(own_bands):
        lane = own_planes * spots + band_index * own_bands + own_band
        occupied = jnp.where(
            iota((sticks, lanes), 1) == lane, occupation_ref[own_band], occupied
        )
    message = (message + occupied.astype(jnp.float32)[None]).astype(out_ref.dtype)
    for band in range(out_ref.shape[0] // pw_count):
        out_ref[band * pw_count : (band + 1) * pw_count] = message


def table_kernel(grid_len, column_hbm, left_ref, right_ref, column_ref, sem):
    copy = pltpu.make_async_copy(column_hbm, column_ref, sem)
    copy.start()
    copy.wait()
    count = column_ref.shape[1]
    half = grid_len // 2
    columns = column_ref[...]
    turns = iota((grid_len, count), 0) * cut(columns, grid_len)
    left_ref[0] = cosine(turns, grid_len).astype(jnp.bfloat16)
    left_ref[1] = sine(turns, grid_len).astype(jnp.bfloat16)
    tall = jnp.transpose(jnp.broadcast_to(wrap(columns, grid_len), (half, count)))
    freq = iota((count, half), 1)
    right_ref[:, :half] = cosine(tall * freq, grid_len).astype(jnp.bfloat16)
    turns = jnp.where(freq == 0, tall * half, tall * freq + (grid_len - grid_len // 4))
    right_ref[:, half:] = cosine(turns, grid_len).astype(jnp.bfloat16)


def plane_kernel(
    bands,
    own_planes,
    norm_factor,
    message_ref,
    left_ref,
    right_ref,
    out_ref,
    value_ref,
    weight_ref,
    held_ref,
    sem,
):
    chunks, rows, chunk = value_ref.shape
    grid_len = out_ref.shape[1]
    half = grid_len // 2
    sticks, lanes = message_ref.shape[1:]
    spots = 2 * bands
    height = math.gcd(grid_len, P_BLOCK)
    blocks = grid_len // height
    group = math.gcd(bands, BAND_GROUP)
    select = (iota((rows + bands, lanes), 0) == iota((rows + bands, lanes), 1)).astype(
        jnp.bfloat16
    )

    def turn(index, peak):
        pieces = chunk // sticks
        picked = dot_last(
            select, message_ref[pl.ds(index * pieces, pieces)].reshape(chunk, lanes)
        )
        value_ref[index] = picked[:rows]
        return jnp.maximum(peak, jnp.max(picked[rows:], 1, keepdims=True))

    peak = loop(chunks, turn, jnp.zeros((bands, 1), jnp.float32))
    weight_ref[...] = jnp.broadcast_to(peak * norm_factor, weight_ref.shape)

    def stick_sums(index, plane, block, first_band):
        lane = pl.ds(index * chunk, chunk)
        row = pl.ds(block * height, height)
        cos_table = left_ref[0, row, lane].reshape(height // PACK, PACK, chunk)
        sin_table = left_ref[1, row, lane].reshape(height // PACK, PACK, chunk)
        parts = []
        for band in range(group):
            at = plane * spots + first_band + band
            real, imag = (
                jnp.broadcast_to(value_ref[index, pl.ds(spot, 1), :], (PACK, chunk)).astype(
                    jnp.bfloat16
                )[None]
                for spot in (at, at + bands)
            )
            parts.append((cos_table * real - sin_table * imag).reshape(height, chunk))
            parts.append((sin_table * real + cos_table * imag).reshape(height, chunk))
        return dot(jnp.concatenate(parts, 0), right_ref[pl.ds(index * chunk, chunk), :])

    def one_block(step, carry):
        plane, block = step // blocks, step % blocks

        def one_group(index, sums):
            first_band = index * group
            if chunks == 1:
                found = stick_sums(0, plane, block, first_band)
            else:
                found = lax.fori_loop(
                    0,
                    chunks,
                    lambda at, so_far: so_far + stick_sums(at, plane, block, first_band),
                    jnp.zeros((2 * group * height, grid_len), jnp.float32),
                )
            with_cos, with_sin, mixed = sums
            for band in range(group):
                top = 2 * band * height
                a, d = found[top : top + height, :half], found[top : top + height, half:]
                top += height
                c, b = found[top : top + height, :half], found[top : top + height, half:]
                weight = weight_ref[pl.ds(first_band + band, 1), :half]
                with_cos += weight * (a * a + c * c)
                with_sin += weight * (b * b + d * d)
                mixed += weight * (c * d - a * b)
            return with_cos, with_sin, mixed

        zero = jnp.zeros((height, half), jnp.float32)
        with_cos, with_sin, mixed = loop(bands // group, one_group, (zero, zero, zero))
        lane = iota((height, half), 1)
        both, mixed = with_cos + with_sin, mixed + mixed
        ahead = jnp.where(lane == 0, with_cos, both + mixed)
        back = jnp.where(lane == 0, with_sin, both - mixed)
        row = pl.ds(block * height, height)
        held_ref[plane, row, :half] = ahead
        held_ref[plane, row, half:] = jnp.take_along_axis(
            back, jnp.where(lane == 0, 0, half - lane), axis=1
        )
        pltpu.make_async_copy(
            held_ref.at[plane, row], out_ref.at[plane, row], sem.at[step]
        ).start()
        return carry

    loop(own_planes * blocks, one_block, 0)
    for step in range(own_planes * blocks):
        where = (step // blocks, pl.ds(step % blocks * height, height))
        pltpu.make_async_copy(held_ref.at[where], out_ref.at[where], sem.at[step]).wait()


def shards(coeffs, rotation_matrix, stick_length, stick_column, plane_index, occupation):
    band_count = lax.axis_size("band")
    pw_count = lax.axis_size("pw")
    devices = band_count * pw_count
    in_count, sticks, grid_len = coeffs.shape[1:]
    bands = rotation_matrix.shape[2]
    stick_count = stick_column.shape[0]
    own_planes = plane_index.shape[0] // pw_count
    spots = 2 * bands
    rows = own_planes * spots
    lanes = -(-(rows + bands) // LANES) * LANES
    vmem = pl.BlockSpec(memory_space=pltpu.VMEM)
    hbm = pl.BlockSpec(memory_space=pltpu.HBM)
    table_bytes = 6 * grid_len * stick_count
    message_bytes = 2 * stick_count * lanes

    messages = pl.pallas_call(
        stick_kernel,
        out_shape=pltpu.VMEM((devices, sticks, lanes), jnp.bfloat16),
        in_specs=[hbm] * 5,
        out_specs=vmem,
        scratch_shapes=[
            pltpu.SMEM(stick_length.shape, jnp.int32),
            pltpu.SMEM(plane_index.shape, jnp.int32),
            pltpu.SMEM(occupation.shape, jnp.int32),
            pltpu.VMEM((2, bands, in_count), jnp.bfloat16),
            pltpu.VMEM((2 * in_count * sticks, grid_len), jnp.bfloat16),
            pltpu.SemaphoreType.DMA((5,)),
        ],
        compiler_params=room(2 * message_bytes),
        name="stick_values",
    )(
        *(
            pltpu.with_memory_space_constraint(array, pltpu.HBM)
            for array in (
                stick_length,
                plane_index,
                occupation,
                jnp.swapaxes(rotation_matrix, 1, 2),
                coeffs.reshape(2 * in_count * sticks, grid_len),
            )
        )
    )
    arrived = lax.all_to_all(messages, ("band", "pw"), split_axis=0, concat_axis=0, tiled=True)
    left, right = pl.pallas_call(
        functools.partial(table_kernel, grid_len),
        out_shape=(
            jax.ShapeDtypeStruct((2, grid_len, stick_count), jnp.bfloat16),
            jax.ShapeDtypeStruct((stick_count, grid_len), jnp.bfloat16),
        ),
        in_specs=[hbm],
        out_specs=(vmem, vmem),
        scratch_shapes=[pltpu.VMEM((1, stick_count), jnp.int32), pltpu.SemaphoreType.DMA],
        compiler_params=room(table_bytes),
        cost_estimate=pl.CostEstimate(
            flops=80 * grid_len * stick_count,
            bytes_accessed=12 * grid_len * stick_count,
            transcendentals=0,
        ),
        name="stick_tables",
    )(pltpu.with_memory_space_constraint(stick_column.reshape(1, stick_count), pltpu.HBM))
    chunk = min(grid_len, stick_count)
    norm_factor = 1.0 / float(bands * stick_count * grid_len)
    blocks = own_planes * (grid_len // math.gcd(grid_len, P_BLOCK))
    return pl.pallas_call(
        functools.partial(plane_kernel, bands, own_planes, norm_factor),
        out_shape=jax.ShapeDtypeStruct((own_planes, grid_len, grid_len), jnp.float32),
        in_specs=[vmem] * 3,
        out_specs=hbm,
        scratch_shapes=[
            pltpu.VMEM((stick_count // chunk, rows, chunk), jnp.float32),
            pltpu.VMEM((bands, LANES), jnp.float32),
            pltpu.VMEM((own_planes, grid_len, grid_len), jnp.float32),
            pltpu.SemaphoreType.DMA((blocks,)),
        ],
        compiler_params=room(table_bytes, message_bytes),
        name="plane_density",
    )(arrived, left, right)


def solution(mesh):
    return jax.shard_map(
        shards,
        mesh=mesh,
        in_specs=(P(None, None, ("band", "pw"), None), P(), P(), P(), P(), P("band")),
        out_specs=P("pw", None, None),
        check_vma=False,
    )
```

```python
import functools
import math

import jax
import jax.numpy as jnp
from jax import lax
from jax.experimental import pallas as pl
from jax.experimental.pallas import tpu as pltpu
from jax.sharding import PartitionSpec as P

LANES = 128
PACK = 16
P_BLOCK = 32
BAND_GROUP = 8
MIB = 1024 * 1024


def wrap(value, period):
    if period & (period - 1) == 0:
        return value & (period - 1)
    return lax.rem(value, period)


def cut(value, size):
    if size & (size - 1) == 0:
        return value >> (size.bit_length() - 1)
    return lax.div(value, size)


def cosine(index, period):
    fold = jnp.abs(wrap(index, period) - period // 2) - period // 4
    angle = fold.astype(jnp.float32) * (2.0 * math.pi / period)
    square = angle * angle
    series = -2.39e-08
    for factor in (2.7526e-06, -1.984090e-04, 8.3333315e-03, -1.666666664e-01, 1.0):
        series = series * square + factor
    return angle * series


def sine(index, period):
    return cosine(index + (period - period // 4), period)


def iota(shape, dim):
    return lax.broadcasted_iota(jnp.int32, shape, dim)


def dot_last(left, right):
    return lax.dot_general(
        left, right, (((1,), (1,)), ((), ())), preferred_element_type=jnp.float32
    )


def dot(left, right):
    return jnp.dot(left, right, preferred_element_type=jnp.float32)


def loop(count, body, carry):
    if count > 16:
        return lax.fori_loop(0, count, body, carry)
    for index in range(count):
        carry = body(index, carry)
    return carry


def room(*sizes):
    return pltpu.CompilerParams(vmem_limit_bytes=min(56 * MIB, 16 * MIB + 2 * sum(sizes)))


def spread(scalars, index, shape):
    result = jnp.full(shape, scalars[0])
    for place, scalar in enumerate(scalars[1:], 1):
        result = jnp.where(index == place, scalar, result)
    return result


def stick_kernel(
    length_hbm,
    plane_hbm,
    occupation_hbm,
    rotation_hbm,
    coeff_hbm,
    out_ref,
    length_ref,
    plane_ref,
    occupation_ref,
    rotation_ref,
    coeff_ref,
    sems,
):
    copies = [
        pltpu.make_async_copy(source, target, sems.at[index])
        for index, (source, target) in enumerate(
            (
                (rotation_hbm, rotation_ref),
                (coeff_hbm, coeff_ref),
                (plane_hbm, plane_ref),
                (length_hbm, length_ref),
                (occupation_hbm, occupation_ref),
            )
        )
    ]
    for copy in copies:
        copy.start()
    out_count, in_count = rotation_ref.shape[1:]
    grid_len = coeff_ref.shape[1]
    sticks = coeff_ref.shape[0] // (2 * in_count)
    plane_count = plane_ref.shape[0]
    pw_count = lax.axis_size("pw")
    own_planes = plane_count // pw_count
    own_bands = occupation_ref.shape[0]
    row_count = 2 * out_count * sticks
    band_index = lax.axis_index("band")
    first_stick = (band_index * pw_count + lax.axis_index("pw")) * sticks

    pick = (
        wrap(cut(iota((row_count, out_count), 0), sticks), out_count)
        == iota((row_count, out_count), 1)
    ).astype(jnp.bfloat16)
    copies[0].wait()
    from_real = dot(pick, rotation_ref[0])
    from_imag = dot(pick, rotation_ref[1])
    is_real = iota((row_count, in_count), 0) < out_count * sticks
    widen = (
        cut(iota((in_count, in_count * sticks), 1), sticks)
        == iota((in_count, in_count * sticks), 0)
    ).astype(jnp.bfloat16)
    shape = (row_count, in_count * sticks)
    same = wrap(iota(shape, 0), sticks) == wrap(iota(shape, 1), sticks)
    mixed = []
    for block in (
        jnp.where(is_real, from_real, from_imag),
        jnp.where(is_real, -from_imag, from_real),
    ):
        wide = dot(block.astype(jnp.bfloat16), widen)
        mixed.append(jnp.where(same, wide, 0.0).astype(jnp.bfloat16))
    rotation = jnp.concatenate(mixed, 1)

    for copy in copies[2:]:
        copy.wait()
    lengths = [length_ref[first_stick + place] for place in range(sticks)]
    planes = [plane_ref[place] for place in range(plane_count)]
    plane_rows = spread(planes, iota((plane_count, grid_len), 0), (plane_count, grid_len))
    product = iota((plane_count, grid_len), 1) * plane_rows
    table = jnp.concatenate([cosine(product, grid_len), sine(product, grid_len)], 0).astype(
        jnp.bfloat16
    )

    shape = (plane_count, row_count)
    lane_lengths = spread(lengths, wrap(iota(shape, 1), sticks), shape)
    shift = (lane_lengths >> 1) * spread(planes, iota(shape, 0), shape)
    phase_cos = cosine(shift, grid_len)
    phase_sin = sine(shift, grid_len)
    real_lane = iota(shape, 1) < row_count // 2

    row_lengths = spread(lengths, iota((sticks, grid_len), 0), (sticks, grid_len))
    live = iota((sticks, grid_len), 1) < row_lengths

    copies[1].wait()
    rotated = dot(rotation, coeff_ref[...])
    rotated = rotated.reshape(row_count // sticks, sticks, grid_len)
    rotated = jnp.where(live[None], rotated, 0.0).reshape(row_count, grid_len)
    sums = dot_last(table, rotated.astype(jnp.bfloat16))
    with_cos, with_sin = sums[:plane_count], sums[plane_count:]
    turned = pltpu.roll(with_sin, row_count // 2, 1)
    amplitude = with_cos + jnp.where(real_lane, -turned, turned)
    turned = pltpu.roll(amplitude, row_count // 2, 1) * phase_sin
    values = amplitude * phase_cos + jnp.where(real_lane, turned, -turned)

    lanes = out_ref.shape[2]
    spots = 2 * out_count
    tall = jnp.broadcast_to(values[:, None, :], (plane_count, sticks, row_count))
    own = iota((sticks, row_count), 0) == wrap(iota((sticks, row_count), 1), sticks)
    tall = jnp.where(own[None], tall, 0.0).reshape(plane_count * sticks, row_count)
    shape = (row_count, lanes)
    place = (
        (cut(iota(shape, 0), sticks) == lax.rem(iota(shape, 1), spots))
        & (iota(shape, 1) < own_planes * spots)
    ).astype(jnp.bfloat16)
    laid = dot(tall.astype(jnp.bfloat16), place).reshape(pw_count, own_planes, sticks, lanes)
    mine = cut(iota((own_planes, sticks, lanes), 2), spots) == iota((own_planes, sticks, lanes), 0)
    message = jnp.sum(jnp.where(mine[None], laid, 0.0), 1)
    occupied = jnp.zeros((sticks, lanes), jnp.int32)
    for own_band in range(own_bands):
        lane = own_planes * spots + band_index * own_bands + own_band
        occupied = jnp.where(
            iota((sticks, lanes), 1) == lane, occupation_ref[own_band], occupied
        )
    message = (message + occupied.astype(jnp.float32)[None]).astype(out_ref.dtype)
    message = jnp.concatenate([message[pw_count - 1 :], message[: pw_count - 1]], 0)
    for band in range(out_ref.shape[0] // pw_count):
        out_ref[band * pw_count : (band + 1) * pw_count] = message


def table_kernel(grid_len, sticks, column_hbm, left_ref, right_ref, column_ref, sem):
    copy = pltpu.make_async_copy(column_hbm, column_ref, sem)
    copy.start()
    copy.wait()
    count = column_ref.shape[1]
    half = grid_len // 2
    columns = jnp.broadcast_to(column_ref[...], (8, count))
    columns = pltpu.roll(columns, sticks, 1)[:1]
    turns = iota((grid_len, count), 0) * cut(columns, grid_len)
    left_ref[0] = cosine(turns, grid_len).astype(jnp.bfloat16)
    left_ref[1] = sine(turns, grid_len).astype(jnp.bfloat16)
    tall = jnp.transpose(jnp.broadcast_to(wrap(columns, grid_len), (half, count)))
    freq = iota((count, half), 1)
    right_ref[:, :half] = cosine(tall * freq, grid_len).astype(jnp.bfloat16)
    turns = jnp.where(freq == 0, tall * half, tall * freq + (grid_len - grid_len // 4))
    right_ref[:, half:] = cosine(turns, grid_len).astype(jnp.bfloat16)


def plane_kernel(
    bands,
    own_planes,
    norm_factor,
    message_ref,
    left_ref,
    right_ref,
    out_ref,
    value_ref,
    weight_ref,
    held_ref,
    sem,
):
    chunks, rows, chunk = value_ref.shape
    grid_len = out_ref.shape[1]
    half = grid_len // 2
    sticks, lanes = message_ref.shape[1:]
    spots = 2 * bands
    height = math.gcd(grid_len, P_BLOCK)
    blocks = grid_len // height
    group = math.gcd(bands, BAND_GROUP)
    select = (iota((rows + bands, lanes), 0) == iota((rows + bands, lanes), 1)).astype(
        jnp.bfloat16
    )

    def turn(index, peak):
        pieces = chunk // sticks
        picked = dot_last(
            select, message_ref[pl.ds(index * pieces, pieces)].reshape(chunk, lanes)
        )
        value_ref[index] = picked[:rows]
        return jnp.maximum(peak, jnp.max(picked[rows:], 1, keepdims=True))

    peak = loop(chunks, turn, jnp.zeros((bands, 1), jnp.float32))
    weight_ref[...] = jnp.broadcast_to(peak * norm_factor, weight_ref.shape)

    def stick_sums(index, plane, block, first_band):
        lane = pl.ds(index * chunk, chunk)
        row = pl.ds(block * height, height)
        cos_table = left_ref[0, row, lane].reshape(height // PACK, PACK, chunk)
        sin_table = left_ref[1, row, lane].reshape(height // PACK, PACK, chunk)
        parts = []
        for band in range(group):
            at = plane * spots + first_band + band
            real, imag = (
                jnp.broadcast_to(value_ref[index, pl.ds(spot, 1), :], (PACK, chunk)).astype(
                    jnp.bfloat16
                )[None]
                for spot in (at, at + bands)
            )
            parts.append((cos_table * real - sin_table * imag).reshape(height, chunk))
            parts.append((sin_table * real + cos_table * imag).reshape(height, chunk))
        return dot(jnp.concatenate(parts, 0), right_ref[pl.ds(index * chunk, chunk), :])

    def one_block(step, carry):
        plane, block = step // blocks, step % blocks

        def one_group(index, sums):
            first_band = index * group
            if chunks == 1:
                found = stick_sums(0, plane, block, first_band)
            else:
                found = lax.fori_loop(
                    0,
                    chunks,
                    lambda at, so_far: so_far + stick_sums(at, plane, block, first_band),
                    jnp.zeros((2 * group * height, grid_len), jnp.float32),
                )
            with_cos, with_sin, mixed = sums
            for band in range(group):
                top = 2 * band * height
                a, d = found[top : top + height, :half], found[top : top + height, half:]
                top += height
                c, b = found[top : top + height, :half], found[top : top + height, half:]
                weight = weight_ref[pl.ds(first_band + band, 1), :half]
                with_cos += weight * (a * a + c * c)
                with_sin += weight * (b * b + d * d)
                mixed += weight * (c * d - a * b)
            return with_cos, with_sin, mixed

        zero = jnp.zeros((height, half), jnp.float32)
        with_cos, with_sin, mixed = loop(bands // group, one_group, (zero, zero, zero))
        lane = iota((height, half), 1)
        both, mixed = with_cos + with_sin, mixed + mixed
        ahead = jnp.where(lane == 0, with_cos, both + mixed)
        back = jnp.where(lane == 0, with_sin, both - mixed)
        row = pl.ds(block * height, height)
        held_ref[plane, row, :half] = ahead
        held_ref[plane, row, half:] = jnp.take_along_axis(
            back, jnp.where(lane == 0, 0, half - lane), axis=1
        )
        pltpu.make_async_copy(
            held_ref.at[plane, row], out_ref.at[plane, row], sem.at[step]
        ).start()
        return carry

    loop(own_planes * blocks, one_block, 0)
    for step in range(own_planes * blocks):
        where = (step // blocks, pl.ds(step % blocks * height, height))
        pltpu.make_async_copy(held_ref.at[where], out_ref.at[where], sem.at[step]).wait()


def shards(coeffs, rotation_matrix, stick_length, stick_column, plane_index, occupation):
    band_count = lax.axis_size("band")
    pw_count = lax.axis_size("pw")
    devices = band_count * pw_count
    in_count, sticks, grid_len = coeffs.shape[1:]
    bands = rotation_matrix.shape[2]
    stick_count = stick_column.shape[0]
    own_planes = plane_index.shape[0] // pw_count
    spots = 2 * bands
    rows = own_planes * spots
    lanes = -(-(rows + bands) // LANES) * LANES
    vmem = pl.BlockSpec(memory_space=pltpu.VMEM)
    hbm = pl.BlockSpec(memory_space=pltpu.HBM)
    table_bytes = 6 * grid_len * stick_count
    message_bytes = 2 * stick_count * lanes

    messages = pl.pallas_call(
        stick_kernel,
        out_shape=pltpu.VMEM((devices, sticks, lanes), jnp.bfloat16),
        in_specs=[hbm] * 5,
        out_specs=vmem,
        scratch_shapes=[
            pltpu.SMEM(stick_length.shape, jnp.int32),
            pltpu.SMEM(plane_index.shape, jnp.int32),
            pltpu.SMEM(occupation.shape, jnp.int32),
            pltpu.VMEM((2, bands, in_count), jnp.bfloat16),
            pltpu.VMEM((2 * in_count * sticks, grid_len), jnp.bfloat16),
            pltpu.SemaphoreType.DMA((5,)),
        ],
        compiler_params=room(2 * message_bytes),
        name="stick_values",
    )(
        *(
            pltpu.with_memory_space_constraint(array, pltpu.HBM)
            for array in (
                stick_length,
                plane_index,
                occupation,
                jnp.swapaxes(rotation_matrix, 1, 2),
                coeffs.reshape(2 * in_count * sticks, grid_len),
            )
        )
    )
    arrived = lax.all_to_all(
        messages,
        ("band", "pw"),
        split_axis=0,
        concat_axis=0,
        axis_index_groups=[[devices - 1, *range(devices - 1)]],
        tiled=True,
    )
    left, right = pl.pallas_call(
        functools.partial(table_kernel, grid_len, sticks),
        out_shape=(
            jax.ShapeDtypeStruct((2, grid_len, stick_count), jnp.bfloat16),
            jax.ShapeDtypeStruct((stick_count, grid_len), jnp.bfloat16),
        ),
        in_specs=[hbm],
        out_specs=(vmem, vmem),
        scratch_shapes=[pltpu.VMEM((1, stick_count), jnp.int32), pltpu.SemaphoreType.DMA],
        compiler_params=room(table_bytes),
        cost_estimate=pl.CostEstimate(
            flops=80 * grid_len * stick_count,
            bytes_accessed=12 * grid_len * stick_count,
            transcendentals=0,
        ),
        name="stick_tables",
    )(pltpu.with_memory_space_constraint(stick_column.reshape(1, stick_count), pltpu.HBM))
    chunk = min(grid_len, stick_count)
    norm_factor = 1.0 / float(bands * stick_count * grid_len)
    blocks = own_planes * (grid_len // math.gcd(grid_len, P_BLOCK))
    return pl.pallas_call(
        functools.partial(plane_kernel, bands, own_planes, norm_factor),
        out_shape=jax.ShapeDtypeStruct((own_planes, grid_len, grid_len), jnp.float32),
        in_specs=[vmem] * 3,
        out_specs=hbm,
        scratch_shapes=[
            pltpu.VMEM((stick_count // chunk, rows, chunk), jnp.float32),
            pltpu.VMEM((bands, LANES), jnp.float32),
            pltpu.VMEM((own_planes, grid_len, grid_len), jnp.float32),
            pltpu.SemaphoreType.DMA((blocks,)),
        ],
        compiler_params=room(table_bytes, message_bytes),
        name="plane_density",
    )(arrived, left, right)


def solution(mesh):
    return jax.shard_map(
        shards,
        mesh=mesh,
        in_specs=(P(None, None, ("band", "pw"), None), P(), P(), P(), P(), P("band")),
        out_specs=P("pw", None, None),
        check_vma=False,
    )
```

```python
import functools
import math

import jax
import jax.numpy as jnp
from jax import lax
from jax.experimental import pallas as pl
from jax.experimental.pallas import tpu as pltpu
from jax.sharding import PartitionSpec as P

LANES = 128
PACK = 16
P_BLOCK = 32
BAND_GROUP = 8
COEFF_COPIES = 4
MIB = 1024 * 1024


def wrap(value, period):
    if period & (period - 1) == 0:
        return value & (period - 1)
    return lax.rem(value, period)


def cut(value, size):
    if size & (size - 1) == 0:
        return value >> (size.bit_length() - 1)
    return lax.div(value, size)


def cosine(index, period):
    fold = jnp.abs(wrap(index, period) - period // 2) - period // 4
    angle = fold.astype(jnp.float32) * (2.0 * math.pi / period)
    square = angle * angle
    series = -2.39e-08
    for factor in (2.7526e-06, -1.984090e-04, 8.3333315e-03, -1.666666664e-01, 1.0):
        series = series * square + factor
    return angle * series


def sine(index, period):
    return cosine(index + (period - period // 4), period)


def iota(shape, dim):
    return lax.broadcasted_iota(jnp.int32, shape, dim)


def dot_last(left, right):
    return lax.dot_general(
        left, right, (((1,), (1,)), ((), ())), preferred_element_type=jnp.float32
    )


def dot(left, right):
    return jnp.dot(left, right, preferred_element_type=jnp.float32)


def loop(count, body, carry):
    if count > 16:
        return lax.fori_loop(0, count, body, carry)
    for index in range(count):
        carry = body(index, carry)
    return carry


def room(*sizes):
    return pltpu.CompilerParams(vmem_limit_bytes=min(56 * MIB, 16 * MIB + 2 * sum(sizes)))


def spread(scalars, index, shape):
    result = jnp.full(shape, scalars[0])
    for place, scalar in enumerate(scalars[1:], 1):
        result = jnp.where(index == place, scalar, result)
    return result


def stick_kernel(
    length_hbm,
    plane_hbm,
    occupation_hbm,
    rotation_hbm,
    coeff_hbm,
    out_hbm,
    length_ref,
    plane_ref,
    occupation_ref,
    rotation_ref,
    coeff_ref,
    message_ref,
    sems,
):
    piece = coeff_ref.shape[0] // COEFF_COPIES
    pieces = [pl.ds(first * piece, piece) for first in range(COEFF_COPIES)]
    copies = [
        pltpu.make_async_copy(source, target, sems.at[index])
        for index, (source, target) in enumerate(
            (
                (rotation_hbm, rotation_ref),
                *((coeff_hbm.at[rows], coeff_ref.at[rows]) for rows in pieces),
                (plane_hbm, plane_ref),
                (length_hbm, length_ref),
                (occupation_hbm, occupation_ref),
            )
        )
    ]
    for copy in copies:
        copy.start()
    out_count, in_count = rotation_ref.shape[1:]
    grid_len = coeff_ref.shape[1]
    sticks = coeff_ref.shape[0] // (2 * in_count)
    plane_count = plane_ref.shape[0]
    pw_count = lax.axis_size("pw")
    own_planes = plane_count // pw_count
    own_bands = occupation_ref.shape[0]
    row_count = 2 * out_count * sticks
    band_index = lax.axis_index("band")
    first_stick = (band_index * pw_count + lax.axis_index("pw")) * sticks

    pick = (
        wrap(cut(iota((row_count, out_count), 0), sticks), out_count)
        == iota((row_count, out_count), 1)
    ).astype(jnp.bfloat16)
    copies[0].wait()
    from_real = dot(pick, rotation_ref[0])
    from_imag = dot(pick, rotation_ref[1])
    is_real = iota((row_count, in_count), 0) < out_count * sticks
    widen = (
        cut(iota((in_count, in_count * sticks), 1), sticks)
        == iota((in_count, in_count * sticks), 0)
    ).astype(jnp.bfloat16)
    shape = (row_count, in_count * sticks)
    same = wrap(iota(shape, 0), sticks) == wrap(iota(shape, 1), sticks)
    mixed = []
    for block in (
        jnp.where(is_real, from_real, from_imag),
        jnp.where(is_real, -from_imag, from_real),
    ):
        wide = dot(block.astype(jnp.bfloat16), widen)
        mixed.append(jnp.where(same, wide, 0.0).astype(jnp.bfloat16))
    rotation = jnp.concatenate(mixed, 1)

    for copy in copies[1 + COEFF_COPIES :]:
        copy.wait()
    lengths = [length_ref[first_stick + place] for place in range(sticks)]
    planes = [plane_ref[place] for place in range(plane_count)]
    plane_rows = spread(planes, iota((plane_count, grid_len), 0), (plane_count, grid_len))
    product = iota((plane_count, grid_len), 1) * plane_rows
    table = jnp.concatenate([cosine(product, grid_len), sine(product, grid_len)], 0).astype(
        jnp.bfloat16
    )

    shape = (plane_count, row_count)
    lane_lengths = spread(lengths, wrap(iota(shape, 1), sticks), shape)
    shift = (lane_lengths >> 1) * spread(planes, iota(shape, 0), shape)
    phase_cos = cosine(shift, grid_len)
    phase_sin = sine(shift, grid_len)
    real_lane = iota(shape, 1) < row_count // 2

    row_lengths = spread(lengths, iota((sticks, grid_len), 0), (sticks, grid_len))
    live = iota((sticks, grid_len), 1) < row_lengths

    rotated = jnp.zeros((row_count, grid_len), jnp.float32)
    for index, rows in enumerate(pieces):
        copies[1 + index].wait()
        rotated += dot(rotation[:, index * piece : (index + 1) * piece], coeff_ref[rows])
    rotated = rotated.reshape(row_count // sticks, sticks, grid_len)
    rotated = jnp.where(live[None], rotated, 0.0).reshape(row_count, grid_len)
    sums = dot_last(table, rotated.astype(jnp.bfloat16))
    with_cos, with_sin = sums[:plane_count], sums[plane_count:]
    turned = pltpu.roll(with_sin, row_count // 2, 1)
    amplitude = with_cos + jnp.where(real_lane, -turned, turned)
    turned = pltpu.roll(amplitude, row_count // 2, 1) * phase_sin
    values = amplitude * phase_cos + jnp.where(real_lane, turned, -turned)

    lanes = out_hbm.shape[2]
    spots = 2 * out_count
    tall = jnp.broadcast_to(values[:, None, :], (plane_count, sticks, row_count))
    own = iota((sticks, row_count), 0) == wrap(iota((sticks, row_count), 1), sticks)
    tall = jnp.where(own[None], tall, 0.0).reshape(plane_count * sticks, row_count)
    shape = (row_count, lanes)
    place = (
        (cut(iota(shape, 0), sticks) == lax.rem(iota(shape, 1), spots))
        & (iota(shape, 1) < own_planes * spots)
    ).astype(jnp.bfloat16)
    laid = dot(tall.astype(jnp.bfloat16), place).reshape(pw_count, own_planes, sticks, lanes)
    mine = cut(iota((own_planes, sticks, lanes), 2), spots) == iota((own_planes, sticks, lanes), 0)
    message = jnp.sum(jnp.where(mine[None], laid, 0.0), 1)
    occupied = jnp.zeros((sticks, lanes), jnp.int32)
    for own_band in range(own_bands):
        lane = own_planes * spots + band_index * own_bands + own_band
        occupied = jnp.where(
            iota((sticks, lanes), 1) == lane, occupation_ref[own_band], occupied
        )
    message = (message + occupied.astype(jnp.float32)[None]).astype(out_hbm.dtype)
    message_ref[...] = message
    copies = [
        pltpu.make_async_copy(
            message_ref, out_hbm.at[pl.ds(band * pw_count, pw_count)], sems.at[band]
        )
        for band in range(out_hbm.shape[0] // pw_count)
    ]
    for copy in copies:
        copy.start()
    for copy in copies:
        copy.wait()


def table_kernel(grid_len, column_hbm, left_ref, right_ref, column_ref, sem):
    copy = pltpu.make_async_copy(column_hbm, column_ref, sem)
    copy.start()
    copy.wait()
    count = column_ref.shape[1]
    half = grid_len // 2
    columns = column_ref[...]
    turns = iota((grid_len, count), 0) * cut(columns, grid_len)
    left_ref[0] = cosine(turns, grid_len).astype(jnp.bfloat16)
    left_ref[1] = sine(turns, grid_len).astype(jnp.bfloat16)
    tall = jnp.transpose(jnp.broadcast_to(wrap(columns, grid_len), (half, count)))
    freq = iota((count, half), 1)
    right_ref[:, :half] = cosine(tall * freq, grid_len).astype(jnp.bfloat16)
    turns = jnp.where(freq == 0, tall * half, tall * freq + (grid_len - grid_len // 4))
    right_ref[:, half:] = cosine(turns, grid_len).astype(jnp.bfloat16)


def plane_kernel(
    bands,
    own_planes,
    norm_factor,
    message_ref,
    left_ref,
    right_ref,
    out_ref,
    value_ref,
    weight_ref,
    held_ref,
    sem,
):
    chunks, rows, chunk = value_ref.shape
    grid_len = out_ref.shape[1]
    half = grid_len // 2
    sticks, lanes = message_ref.shape[1:]
    spots = 2 * bands
    height = math.gcd(grid_len, P_BLOCK)
    blocks = grid_len // height
    group = math.gcd(bands, BAND_GROUP)
    select = (iota((rows + bands, lanes), 0) == iota((rows + bands, lanes), 1)).astype(
        jnp.bfloat16
    )

    def turn(index, peak):
        pieces = chunk // sticks
        picked = dot_last(
            select, message_ref[pl.ds(index * pieces, pieces)].reshape(chunk, lanes)
        )
        value_ref[index] = picked[:rows]
        return jnp.maximum(peak, jnp.max(picked[rows:], 1, keepdims=True))

    peak = loop(chunks, turn, jnp.zeros((bands, 1), jnp.float32))
    weight_ref[...] = jnp.broadcast_to(peak * norm_factor, weight_ref.shape)

    def stick_sums(index, plane, block, first_band):
        lane = pl.ds(index * chunk, chunk)
        row = pl.ds(block * height, height)
        cos_table = left_ref[0, row, lane].reshape(height // PACK, PACK, chunk)
        sin_table = left_ref[1, row, lane].reshape(height // PACK, PACK, chunk)
        parts = []
        for band in range(group):
            at = plane * spots + first_band + band
            real, imag = (
                jnp.broadcast_to(value_ref[index, pl.ds(spot, 1), :], (PACK, chunk)).astype(
                    jnp.bfloat16
                )[None]
                for spot in (at, at + bands)
            )
            parts.append((cos_table * real - sin_table * imag).reshape(height, chunk))
            parts.append((sin_table * real + cos_table * imag).reshape(height, chunk))
        return dot(jnp.concatenate(parts, 0), right_ref[pl.ds(index * chunk, chunk), :])

    def group_sums(step):
        first_band, block = step % groups * group, step // groups
        found = []
        for plane in range(own_planes):
            if chunks == 1:
                found.append(stick_sums(0, plane, block, first_band))
            else:
                found.append(
                    lax.fori_loop(
                        0,
                        chunks,
                        lambda at, so_far: so_far + stick_sums(at, plane, block, first_band),
                        jnp.zeros((2 * group * height, grid_len), jnp.float32),
                    )
                )
        return found

    def add_squares(step, found, sums):
        first_band = step % groups * group
        result = []
        for plane in range(own_planes):
            with_cos, with_sin, mixed = sums[plane]
            for band in range(group):
                top = 2 * band * height
                a = found[plane][top : top + height, :half]
                d = found[plane][top : top + height, half:]
                top += height
                c = found[plane][top : top + height, :half]
                b = found[plane][top : top + height, half:]
                weight = weight_ref[pl.ds(first_band + band, 1), :half]
                with_cos += weight * (a * a + c * c)
                with_sin += weight * (b * b + d * d)
                mixed += weight * (c * d - a * b)
            result.append((with_cos, with_sin, mixed))
        return result

    def copy_out(plane, block):
        where = (plane, pl.ds(block * height, height))
        return pltpu.make_async_copy(
            held_ref.at[where], out_ref.at[where], sem.at[plane * blocks + block]
        )

    def finish(block, sums):
        lane = iota((height, half), 1)
        row = pl.ds(block * height, height)
        for plane, (with_cos, with_sin, mixed) in enumerate(sums):
            both, mixed = with_cos + with_sin, mixed + mixed
            ahead = jnp.where(lane == 0, with_cos, both + mixed)
            back = jnp.where(lane == 0, with_sin, both - mixed)
            held_ref[plane, row, :half] = ahead
            held_ref[plane, row, half:] = jnp.take_along_axis(
                back, jnp.where(lane == 0, 0, half - lane), axis=1
            )
            copy_out(plane, block).start()

    zero = jnp.zeros((height, half), jnp.float32)
    empty = [(zero, zero, zero)] * own_planes
    groups = bands // group
    if blocks * groups > 32:

        def one_block(block, carry):
            def one_group(index, sums):
                step = block * groups + index
                return add_squares(step, group_sums(step), sums)

            finish(block, lax.fori_loop(0, groups, one_group, empty))
            return carry

        lax.fori_loop(0, blocks, one_block, 0)
    else:
        sums, ahead = empty, group_sums(0)
        for step in range(blocks * groups):
            found = ahead
            if step + 1 < blocks * groups:
                ahead = group_sums(step + 1)
            sums = add_squares(step, found, sums)
            if (step + 1) % groups == 0:
                finish(step // groups, sums)
                sums = empty
    for plane in range(own_planes):
        for block in range(blocks):
            copy_out(plane, block).wait()


def shards(coeffs, rotation_matrix, stick_length, stick_column, plane_index, occupation):
    band_count = lax.axis_size("band")
    pw_count = lax.axis_size("pw")
    devices = band_count * pw_count
    in_count, sticks, grid_len = coeffs.shape[1:]
    bands = rotation_matrix.shape[2]
    stick_count = stick_column.shape[0]
    own_planes = plane_index.shape[0] // pw_count
    spots = 2 * bands
    rows = own_planes * spots
    lanes = -(-(rows + bands) // LANES) * LANES
    vmem = pl.BlockSpec(memory_space=pltpu.VMEM)
    hbm = pl.BlockSpec(memory_space=pltpu.HBM)
    table_bytes = 6 * grid_len * stick_count
    message_bytes = 2 * stick_count * lanes

    messages = pl.pallas_call(
        stick_kernel,
        out_shape=jax.ShapeDtypeStruct((devices, sticks, lanes), jnp.bfloat16),
        in_specs=[hbm] * 5,
        out_specs=hbm,
        scratch_shapes=[
            pltpu.SMEM(stick_length.shape, jnp.int32),
            pltpu.SMEM(plane_index.shape, jnp.int32),
            pltpu.SMEM(occupation.shape, jnp.int32),
            pltpu.VMEM((2, bands, in_count), jnp.bfloat16),
            pltpu.VMEM((2 * in_count * sticks, grid_len), jnp.bfloat16),
            pltpu.VMEM((pw_count, sticks, lanes), jnp.bfloat16),
            pltpu.SemaphoreType.DMA((max(4 + COEFF_COPIES, band_count),)),
        ],
        compiler_params=room(2 * message_bytes),
        name="stick_values",
    )(
        *(
            pltpu.with_memory_space_constraint(array, pltpu.HBM)
            for array in (
                stick_length,
                plane_index,
                occupation,
                jnp.swapaxes(rotation_matrix, 1, 2),
                coeffs.reshape(2 * in_count * sticks, grid_len),
            )
        )
    )
    arrived = lax.all_to_all(messages, ("band", "pw"), split_axis=0, concat_axis=0, tiled=True)
    left, right = pl.pallas_call(
        functools.partial(table_kernel, grid_len),
        out_shape=(
            jax.ShapeDtypeStruct((2, grid_len, stick_count), jnp.bfloat16),
            jax.ShapeDtypeStruct((stick_count, grid_len), jnp.bfloat16),
        ),
        in_specs=[hbm],
        out_specs=(vmem, vmem),
        scratch_shapes=[pltpu.VMEM((1, stick_count), jnp.int32), pltpu.SemaphoreType.DMA],
        compiler_params=room(table_bytes),
        cost_estimate=pl.CostEstimate(
            flops=80 * grid_len * stick_count,
            bytes_accessed=12 * grid_len * stick_count,
            transcendentals=0,
        ),
        name="stick_tables",
    )(pltpu.with_memory_space_constraint(stick_column.reshape(1, stick_count), pltpu.HBM))
    chunk = min(grid_len, stick_count)
    norm_factor = 1.0 / float(bands * stick_count * grid_len)
    blocks = own_planes * (grid_len // math.gcd(grid_len, P_BLOCK))
    return pl.pallas_call(
        functools.partial(plane_kernel, bands, own_planes, norm_factor),
        out_shape=jax.ShapeDtypeStruct((own_planes, grid_len, grid_len), jnp.float32),
        in_specs=[vmem] * 3,
        out_specs=hbm,
        scratch_shapes=[
            pltpu.VMEM((stick_count // chunk, rows, chunk), jnp.float32),
            pltpu.VMEM((bands, LANES), jnp.float32),
            pltpu.VMEM((own_planes, grid_len, grid_len), jnp.float32),
            pltpu.SemaphoreType.DMA((blocks,)),
        ],
        compiler_params=room(table_bytes, message_bytes),
        name="plane_density",
    )(arrived, left, right)


def solution(mesh):
    return jax.shard_map(
        shards,
        mesh=mesh,
        in_specs=(P(None, None, ("band", "pw"), None), P(), P(), P(), P(), P("band")),
        out_specs=P("pw", None, None),
        check_vma=False,
    )
```

```python
import functools
import math

import jax
import jax.numpy as jnp
from jax import lax
from jax.experimental import pallas as pl
from jax.experimental.pallas import tpu as pltpu
from jax.sharding import PartitionSpec as P

LANES = 128
P_BLOCK = 32
BAND_GROUP = 8
GROUP_LANES = 256
COEFF_COPIES = 1
MIB = 1024 * 1024


def wrap(value, period):
    if period & (period - 1) == 0:
        return value & (period - 1)
    return lax.rem(value, period)


def cut(value, size):
    if size & (size - 1) == 0:
        return value >> (size.bit_length() - 1)
    return lax.div(value, size)


def cosine(index, period):
    fold = jnp.abs(wrap(index, period) - period // 2) - period // 4
    angle = fold.astype(jnp.float32) * (2.0 * math.pi / period)
    square = angle * angle
    series = -2.39e-08
    for factor in (2.7526e-06, -1.984090e-04, 8.3333315e-03, -1.666666664e-01, 1.0):
        series = series * square + factor
    return angle * series


def sine(index, period):
    return cosine(index + (period - period // 4), period)


def iota(shape, dim):
    return lax.broadcasted_iota(jnp.int32, shape, dim)


def dot_last(left, right):
    return lax.dot_general(
        left, right, (((1,), (1,)), ((), ())), preferred_element_type=jnp.float32
    )


def dot(left, right):
    return jnp.dot(left, right, preferred_element_type=jnp.float32)


def loop(count, body, carry):
    if count > 16:
        return lax.fori_loop(0, count, body, carry)
    for index in range(count):
        carry = body(index, carry)
    return carry


def room(*sizes):
    return pltpu.CompilerParams(vmem_limit_bytes=min(56 * MIB, 16 * MIB + 2 * sum(sizes)))


def spread(scalars, index, shape):
    result = jnp.full(shape, scalars[0])
    for place, scalar in enumerate(scalars[1:], 1):
        result = jnp.where(index == place, scalar, result)
    return result


def stick_kernel(
    length_hbm,
    plane_hbm,
    occupation_hbm,
    rotation_hbm,
    coeff_hbm,
    out_hbm,
    length_ref,
    plane_ref,
    occupation_ref,
    rotation_ref,
    coeff_ref,
    message_ref,
    sems,
):
    piece = coeff_ref.shape[0] // COEFF_COPIES
    pieces = [pl.ds(first * piece, piece) for first in range(COEFF_COPIES)]
    copies = [
        pltpu.make_async_copy(source, target, sems.at[index])
        for index, (source, target) in enumerate(
            (
                (rotation_hbm, rotation_ref),
                *((coeff_hbm.at[rows], coeff_ref.at[rows]) for rows in pieces),
                (plane_hbm, plane_ref),
                (length_hbm, length_ref),
                (occupation_hbm, occupation_ref),
            )
        )
    ]
    for copy in copies:
        copy.start()
    out_count, in_count = rotation_ref.shape[1:]
    grid_len = coeff_ref.shape[1]
    sticks = coeff_ref.shape[0] // (2 * in_count)
    plane_count = plane_ref.shape[0]
    pw_count = lax.axis_size("pw")
    own_planes = plane_count // pw_count
    own_bands = occupation_ref.shape[0]
    row_count = 2 * out_count * sticks
    lanes = message_ref.shape[2]
    band_index = lax.axis_index("band")
    first_stick = (band_index * pw_count + lax.axis_index("pw")) * sticks

    group_lanes = GROUP_LANES // (own_planes * 2 * out_count) * (own_planes * 2 * out_count)
    spots = own_planes * 2 * out_count
    group_pw = group_lanes // spots

    wide = in_count * sticks
    widen = (cut(iota((in_count, wide), 1), sticks) == iota((in_count, wide), 0)).astype(
        jnp.bfloat16
    )
    same = wrap(iota((sticks, wide), 1), sticks) == iota((sticks, wide), 0)
    copies[0].wait()
    parts = [dot(rotation_ref[part], widen) for part in range(2)]
    rows = {}
    for band in range(out_count):
        real, imag = (
            jnp.where(same, jnp.broadcast_to(part[band : band + 1], (sticks, wide)), 0.0)
            for part in parts
        )
        rows[0, band] = jnp.concatenate([real, -imag], 1)
        rows[1, band] = jnp.concatenate([imag, real], 1)
    rotation = jnp.concatenate([rows[key] for key in sorted(rows)], 0).astype(jnp.bfloat16)

    for copy in copies[1 + COEFF_COPIES :]:
        copy.wait()
    lengths = [length_ref[first_stick + place] for place in range(sticks)]
    row_lengths = spread(lengths, iota((sticks, grid_len), 0), (sticks, grid_len))
    live = iota((sticks, grid_len), 1) < row_lengths
    shape = (sticks, lanes)
    occupied = jnp.zeros(shape, jnp.int32)
    for own_band in range(own_bands):
        lane = spots + band_index * own_bands + own_band
        occupied = jnp.where(iota(shape, 1) == lane, occupation_ref[own_band], occupied)
    occupied = occupied.astype(jnp.float32)

    shape = (sticks, group_lanes)
    lane = iota(shape, 1)
    lane_plane = lax.div(lane, 2 * out_count)
    real_lane = lax.rem(lane, 2 * out_count) < out_count
    lane_band = lax.rem(lane, out_count)
    half_lengths = spread(lengths, iota(shape, 0), shape) >> 1

    def forms(first_pw):
        planes = [
            plane_ref[first_pw * own_planes + place] for place in range(group_pw * own_planes)
        ]
        lane_planes = spread(planes, lane_plane, shape)
        product = iota((grid_len, group_lanes), 0) * lane_planes[:1]
        table = jnp.concatenate([cosine(product, grid_len), sine(product, grid_len)], 1)
        shift = half_lengths * lane_planes
        return table.astype(jnp.bfloat16), cosine(shift, grid_len), sine(shift, grid_len)

    def pick(sums, part):
        chosen = jnp.zeros(shape, jnp.float32)
        for band in range(out_count):
            top = (part * out_count + band) * sticks
            chosen = jnp.where(lane_band == band, sums[top : top + sticks], chosen)
        return chosen

    def send(first_pw, rotated, form):
        table, phase_cos, phase_sin = form
        sums = dot(rotated, table)
        with_cos, with_sin = sums[:, :group_lanes], sums[:, group_lanes:]
        real = pick(with_cos, 0) - pick(with_sin, 1)
        imag = pick(with_sin, 0) + pick(with_cos, 1)
        values = jnp.where(
            real_lane, real * phase_cos + imag * phase_sin, imag * phase_cos - real * phase_sin
        )
        for place in range(group_pw):
            first = place * spots
            tile = first // lanes * lanes
            piece = values[:, tile : tile + lanes]
            if first > tile:
                piece = pltpu.roll(piece, lanes - (first - tile), 1)
            piece = jnp.where(iota((sticks, lanes), 1) < spots, piece, occupied)
            message_ref[first_pw + place] = piece.astype(message_ref.dtype)

    if group_pw == pw_count:
        form = forms(0)
    rotated = jnp.zeros((row_count, grid_len), jnp.float32)
    for index, where in enumerate(pieces):
        copies[1 + index].wait()
        rotated += dot(rotation[:, index * piece : (index + 1) * piece], coeff_ref[where])
    rotated = rotated.reshape(row_count // sticks, sticks, grid_len)
    rotated = jnp.where(live[None], rotated, 0.0).reshape(row_count, grid_len)
    rotated = rotated.astype(jnp.bfloat16)
    if group_pw == pw_count:
        send(0, rotated, form)
    else:

        def one_group(index, carry):
            send(index * group_pw, rotated, forms(index * group_pw))
            return carry

        lax.fori_loop(0, pw_count // group_pw, one_group, 0)
    copies = [
        pltpu.make_async_copy(
            message_ref, out_hbm.at[pl.ds(band * pw_count, pw_count)], sems.at[band]
        )
        for band in range(out_hbm.shape[0] // pw_count)
    ]
    for copy in copies:
        copy.start()
    for copy in copies:
        copy.wait()


def table_kernel(grid_len, column_hbm, left_ref, right_ref, column_ref, sem):
    copy = pltpu.make_async_copy(column_hbm, column_ref, sem)
    copy.start()
    copy.wait()
    count = column_ref.shape[1]
    half = grid_len // 2
    columns = column_ref[...]
    turns = iota((grid_len, count), 0) * cut(columns, grid_len)
    left_ref[0] = cosine(turns, grid_len).astype(jnp.bfloat16).astype(jnp.float32)
    left_ref[1] = sine(turns, grid_len).astype(jnp.bfloat16).astype(jnp.float32)
    tall = jnp.transpose(jnp.broadcast_to(wrap(columns, grid_len), (half, count)))
    freq = iota((count, half), 1)
    right_ref[:, :half] = cosine(tall * freq, grid_len).astype(jnp.bfloat16)
    turns = jnp.where(freq == 0, tall * half, tall * freq + (grid_len - grid_len // 4))
    right_ref[:, half:] = cosine(turns, grid_len).astype(jnp.bfloat16)


def plane_kernel(
    bands,
    own_planes,
    norm_factor,
    message_ref,
    left_ref,
    right_ref,
    out_ref,
    value_ref,
    held_ref,
    sem,
):
    chunks, rows, chunk = value_ref.shape
    grid_len = out_ref.shape[1]
    half = grid_len // 2
    sticks, lanes = message_ref.shape[1:]
    spots = 2 * bands
    height = math.gcd(grid_len, P_BLOCK)
    blocks = grid_len // height
    group = math.gcd(bands, BAND_GROUP)
    select = (iota((rows + bands, lanes), 0) == iota((rows + bands, lanes), 1)).astype(
        jnp.bfloat16
    )

    def turn(index, peak):
        pieces = chunk // sticks
        picked = dot_last(
            select, message_ref[pl.ds(index * pieces, pieces)].reshape(chunk, lanes)
        )
        value_ref[index] = picked[:rows]
        return jnp.maximum(peak, jnp.max(picked[rows:], 1, keepdims=True))

    peak = loop(chunks, turn, jnp.zeros((bands, 1), jnp.float32))
    scale = jnp.sqrt(peak * norm_factor)[None]
    for first in range(0, rows, bands):
        value_ref[:, first : first + bands] = value_ref[:, first : first + bands] * scale

    def stick_sums(index, plane, block, first_band):
        lane = pl.ds(index * chunk, chunk)
        row = pl.ds(block * height, height)
        cos_table, sin_table = left_ref[0, row, lane], left_ref[1, row, lane]
        parts = []
        for band in range(group):
            at = plane * spots + first_band + band
            real = value_ref[index, pl.ds(at, 1), :]
            imag = value_ref[index, pl.ds(at + bands, 1), :]
            parts.append((cos_table * real - sin_table * imag).astype(jnp.bfloat16))
            parts.append((sin_table * real + cos_table * imag).astype(jnp.bfloat16))
        return dot(jnp.concatenate(parts, 0), right_ref[pl.ds(index * chunk, chunk), :])

    def group_sums(step):
        first_band, block = step % groups * group, step // groups
        found = []
        for plane in range(own_planes):
            if chunks == 1:
                found.append(stick_sums(0, plane, block, first_band))
            else:
                found.append(
                    lax.fori_loop(
                        0,
                        chunks,
                        lambda at, so_far: so_far + stick_sums(at, plane, block, first_band),
                        jnp.zeros((2 * group * height, grid_len), jnp.float32),
                    )
                )
        return found

    def add_squares(found, sums):
        result = []
        for plane in range(own_planes):
            with_cos, with_sin, mixed = sums[plane]
            for band in range(group):
                top = 2 * band * height
                a = found[plane][top : top + height, :half]
                d = found[plane][top : top + height, half:]
                top += height
                c = found[plane][top : top + height, :half]
                b = found[plane][top : top + height, half:]
                with_cos += a * a + c * c
                with_sin += b * b + d * d
                mixed += c * d - a * b
            result.append((with_cos, with_sin, mixed))
        return result

    def copy_out(plane, block):
        where = (plane, pl.ds(block * height, height))
        return pltpu.make_async_copy(
            held_ref.at[where], out_ref.at[where], sem.at[plane * blocks + block]
        )

    def finish(block, sums):
        lane = iota((height, half), 1)
        row = pl.ds(block * height, height)
        for plane, (with_cos, with_sin, mixed) in enumerate(sums):
            both, mixed = with_cos + with_sin, mixed + mixed
            ahead = jnp.where(lane == 0, with_cos, both + mixed)
            back = jnp.where(lane == 0, with_sin, both - mixed)
            held_ref[plane, row, :half] = ahead
            held_ref[plane, row, half:] = jnp.take_along_axis(
                back, jnp.where(lane == 0, 0, half - lane), axis=1
            )
            copy_out(plane, block).start()

    zero = jnp.zeros((height, half), jnp.float32)
    empty = [(zero, zero, zero)] * own_planes
    groups = bands // group
    if blocks * groups > 32:

        def one_block(block, carry):
            def one_group(index, sums):
                step = block * groups + index
                return add_squares(group_sums(step), sums)

            finish(block, lax.fori_loop(0, groups, one_group, empty))
            return carry

        lax.fori_loop(0, blocks, one_block, 0)
    else:
        sums, ahead = empty, group_sums(0)
        for step in range(blocks * groups):
            found = ahead
            if step + 1 < blocks * groups:
                ahead = group_sums(step + 1)
            sums = add_squares(found, sums)
            if (step + 1) % groups == 0:
                finish(step // groups, sums)
                sums = empty
    for plane in range(own_planes):
        for block in range(blocks):
            copy_out(plane, block).wait()


def shards(coeffs, rotation_matrix, stick_length, stick_column, plane_index, occupation):
    band_count = lax.axis_size("band")
    pw_count = lax.axis_size("pw")
    devices = band_count * pw_count
    in_count, sticks, grid_len = coeffs.shape[1:]
    bands = rotation_matrix.shape[2]
    stick_count = stick_column.shape[0]
    own_planes = plane_index.shape[0] // pw_count
    spots = 2 * bands
    rows = own_planes * spots
    lanes = -(-(rows + bands) // LANES) * LANES
    vmem = pl.BlockSpec(memory_space=pltpu.VMEM)
    hbm = pl.BlockSpec(memory_space=pltpu.HBM)
    table_bytes = 10 * grid_len * stick_count
    message_bytes = 2 * stick_count * lanes

    messages = pl.pallas_call(
        stick_kernel,
        out_shape=jax.ShapeDtypeStruct((devices, sticks, lanes), jnp.bfloat16),
        in_specs=[hbm] * 5,
        out_specs=hbm,
        scratch_shapes=[
            pltpu.SMEM(stick_length.shape, jnp.int32),
            pltpu.SMEM(plane_index.shape, jnp.int32),
            pltpu.SMEM(occupation.shape, jnp.int32),
            pltpu.VMEM((2, bands, in_count), jnp.bfloat16),
            pltpu.VMEM((2 * in_count * sticks, grid_len), jnp.bfloat16),
            pltpu.VMEM((pw_count, sticks, lanes), jnp.bfloat16),
            pltpu.SemaphoreType.DMA((max(4 + COEFF_COPIES, band_count),)),
        ],
        compiler_params=room(2 * message_bytes),
        name="stick_values",
    )(
        *(
            pltpu.with_memory_space_constraint(array, pltpu.HBM)
            for array in (
                stick_length,
                plane_index,
                occupation,
                jnp.swapaxes(rotation_matrix, 1, 2),
                coeffs.reshape(2 * in_count * sticks, grid_len),
            )
        )
    )
    arrived = lax.all_to_all(messages, ("band", "pw"), split_axis=0, concat_axis=0, tiled=True)
    left, right = pl.pallas_call(
        functools.partial(table_kernel, grid_len),
        out_shape=(
            jax.ShapeDtypeStruct((2, grid_len, stick_count), jnp.float32),
            jax.ShapeDtypeStruct((stick_count, grid_len), jnp.bfloat16),
        ),
        in_specs=[hbm],
        out_specs=(vmem, vmem),
        scratch_shapes=[pltpu.VMEM((1, stick_count), jnp.int32), pltpu.SemaphoreType.DMA],
        compiler_params=room(table_bytes),
        cost_estimate=pl.CostEstimate(
            flops=80 * grid_len * stick_count,
            bytes_accessed=12 * grid_len * stick_count,
            transcendentals=0,
        ),
        name="stick_tables",
    )(pltpu.with_memory_space_constraint(stick_column.reshape(1, stick_count), pltpu.HBM))
    chunk = min(grid_len, stick_count)
    norm_factor = 1.0 / float(bands * stick_count * grid_len)
    blocks = own_planes * (grid_len // math.gcd(grid_len, P_BLOCK))
    return pl.pallas_call(
        functools.partial(plane_kernel, bands, own_planes, norm_factor),
        out_shape=jax.ShapeDtypeStruct((own_planes, grid_len, grid_len), jnp.float32),
        in_specs=[vmem] * 3,
        out_specs=hbm,
        scratch_shapes=[
            pltpu.VMEM((stick_count // chunk, rows, chunk), jnp.float32),
            pltpu.VMEM((own_planes, grid_len, grid_len), jnp.float32),
            pltpu.SemaphoreType.DMA((blocks,)),
        ],
        compiler_params=room(table_bytes, message_bytes),
        name="plane_density",
    )(arrived, left, right)


def solution(mesh):
    return jax.shard_map(
        shards,
        mesh=mesh,
        in_specs=(P(None, None, ("band", "pw"), None), P(), P(), P(), P(), P("band")),
        out_specs=P("pw", None, None),
        check_vma=False,
    )
```

```python
import functools
import math

import jax
import jax.numpy as jnp
from jax import lax
from jax.experimental import pallas as pl
from jax.experimental.pallas import tpu as pltpu
from jax.sharding import PartitionSpec as P

LANES = 128
PACK = 16
P_BLOCK = 64
BAND_GROUP = 8
GROUP_LANES = 256
COEFF_COPIES = 1
MIB = 1024 * 1024


def wrap(value, period):
    if period & (period - 1) == 0:
        return value & (period - 1)
    return lax.rem(value, period)


def cut(value, size):
    if size & (size - 1) == 0:
        return value >> (size.bit_length() - 1)
    return lax.div(value, size)


def cosine(index, period):
    fold = jnp.abs(wrap(index, period) - period // 2) - period // 4
    angle = fold.astype(jnp.float32) * (2.0 * math.pi / period)
    square = angle * angle
    series = -2.39e-08
    for factor in (2.7526e-06, -1.984090e-04, 8.3333315e-03, -1.666666664e-01, 1.0):
        series = series * square + factor
    return angle * series


def sine(index, period):
    return cosine(index + (period - period // 4), period)


def iota(shape, dim):
    return lax.broadcasted_iota(jnp.int32, shape, dim)


def dot_last(left, right):
    return lax.dot_general(
        left, right, (((1,), (1,)), ((), ())), preferred_element_type=jnp.float32
    )


def dot(left, right):
    return jnp.dot(left, right, preferred_element_type=jnp.float32)


def loop(count, body, carry):
    if count > 16:
        return lax.fori_loop(0, count, body, carry)
    for index in range(count):
        carry = body(index, carry)
    return carry


def room(*sizes):
    return pltpu.CompilerParams(vmem_limit_bytes=min(56 * MIB, 16 * MIB + 2 * sum(sizes)))


def spread(scalars, index, shape):
    result = jnp.full(shape, scalars[0])
    for place, scalar in enumerate(scalars[1:], 1):
        result = jnp.where(index == place, scalar, result)
    return result


def stick_kernel(
    length_hbm,
    plane_hbm,
    occupation_hbm,
    rotation_hbm,
    coeff_hbm,
    out_hbm,
    length_ref,
    plane_ref,
    occupation_ref,
    rotation_ref,
    coeff_ref,
    message_ref,
    sems,
):
    piece = coeff_ref.shape[0] // COEFF_COPIES
    pieces = [pl.ds(first * piece, piece) for first in range(COEFF_COPIES)]
    copies = [
        pltpu.make_async_copy(source, target, sems.at[index])
        for index, (source, target) in enumerate(
            (
                (rotation_hbm, rotation_ref),
                *((coeff_hbm.at[rows], coeff_ref.at[rows]) for rows in pieces),
                (plane_hbm, plane_ref),
                (length_hbm, length_ref),
                (occupation_hbm, occupation_ref),
            )
        )
    ]
    for copy in copies:
        copy.start()
    out_count, in_count = rotation_ref.shape[1:]
    grid_len = coeff_ref.shape[1]
    sticks = coeff_ref.shape[0] // (2 * in_count)
    plane_count = plane_ref.shape[0]
    pw_count = lax.axis_size("pw")
    own_planes = plane_count // pw_count
    own_bands = occupation_ref.shape[0]
    row_count = 2 * out_count * sticks
    lanes = message_ref.shape[2]
    band_index = lax.axis_index("band")
    first_stick = (band_index * pw_count + lax.axis_index("pw")) * sticks

    group_lanes = GROUP_LANES // (own_planes * 2 * out_count) * (own_planes * 2 * out_count)
    spots = own_planes * 2 * out_count
    group_pw = group_lanes // spots

    wide = in_count * sticks
    widen = (cut(iota((in_count, wide), 1), sticks) == iota((in_count, wide), 0)).astype(
        jnp.bfloat16
    )
    same = wrap(iota((sticks, wide), 1), sticks) == iota((sticks, wide), 0)
    copies[0].wait()
    parts = [dot(rotation_ref[part], widen) for part in range(2)]
    rows = {}
    for band in range(out_count):
        real, imag = (
            jnp.where(same, jnp.broadcast_to(part[band : band + 1], (sticks, wide)), 0.0)
            for part in parts
        )
        rows[0, band] = jnp.concatenate([real, -imag], 1)
        rows[1, band] = jnp.concatenate([imag, real], 1)
    rotation = jnp.concatenate([rows[key] for key in sorted(rows)], 0).astype(jnp.bfloat16)

    for copy in copies[1 + COEFF_COPIES :]:
        copy.wait()
    lengths = [length_ref[first_stick + place] for place in range(sticks)]
    row_lengths = spread(lengths, iota((sticks, grid_len), 0), (sticks, grid_len))
    live = iota((sticks, grid_len), 1) < row_lengths
    shape = (sticks, lanes)
    occupied = jnp.zeros(shape, jnp.int32)
    for own_band in range(own_bands):
        lane = spots + band_index * own_bands + own_band
        occupied = jnp.where(iota(shape, 1) == lane, occupation_ref[own_band], occupied)
    occupied = occupied.astype(jnp.float32)

    shape = (sticks, group_lanes)
    lane = iota(shape, 1)
    lane_plane = lax.div(lane, 2 * out_count)
    real_lane = lax.rem(lane, 2 * out_count) < out_count
    lane_band = lax.rem(lane, out_count)
    half_lengths = spread(lengths, iota(shape, 0), shape) >> 1

    def forms(first_pw):
        kinds = group_pw * own_planes
        planes = [plane_ref[first_pw * own_planes + place] for place in range(kinds)]
        kind = iota((2 * kinds, grid_len), 0)
        planes_down = spread(planes, lax.rem(kind, kinds), kind.shape)
        quarter = jnp.where(kind < kinds, 0, grid_len - grid_len // 4)
        waves = cosine(iota(kind.shape, 1) * planes_down + quarter, grid_len)
        place = iota((2 * kinds, 2 * group_lanes), 1)
        wanted = lax.div(lax.rem(place, group_lanes), 2 * out_count)
        wanted = jnp.where(place < group_lanes, wanted, wanted + kinds)
        widen = (iota(place.shape, 0) == wanted).astype(jnp.bfloat16)
        table = lax.dot_general(
            waves.astype(jnp.bfloat16),
            widen,
            (((0,), (0,)), ((), ())),
            preferred_element_type=jnp.float32,
        )
        lane_planes = spread(planes, lane_plane, shape)
        shift = half_lengths * lane_planes
        return table.astype(jnp.bfloat16), cosine(shift, grid_len), sine(shift, grid_len)

    def pick(sums, part):
        chosen = jnp.zeros(shape, jnp.float32)
        for band in range(out_count):
            top = (part * out_count + band) * sticks
            chosen = jnp.where(lane_band == band, sums[top : top + sticks], chosen)
        return chosen

    def send(first_pw, rotated, form):
        table, phase_cos, phase_sin = form
        sums = dot(rotated, table)
        with_cos, with_sin = sums[:, :group_lanes], sums[:, group_lanes:]
        real = pick(with_cos, 0) - pick(with_sin, 1)
        imag = pick(with_sin, 0) + pick(with_cos, 1)
        values = jnp.where(
            real_lane, real * phase_cos + imag * phase_sin, imag * phase_cos - real * phase_sin
        )
        for place in range(group_pw):
            first = place * spots
            tile = first // lanes * lanes
            piece = values[:, tile : tile + lanes]
            if first > tile:
                piece = pltpu.roll(piece, lanes - (first - tile), 1)
            piece = jnp.where(iota((sticks, lanes), 1) < spots, piece, occupied)
            message_ref[first_pw + place] = piece.astype(message_ref.dtype)

    if group_pw == pw_count:
        form = forms(0)
    rotated = jnp.zeros((row_count, grid_len), jnp.float32)
    for index, where in enumerate(pieces):
        copies[1 + index].wait()
        rotated += dot(rotation[:, index * piece : (index + 1) * piece], coeff_ref[where])
    rotated = rotated.reshape(row_count // sticks, sticks, grid_len)
    rotated = jnp.where(live[None], rotated, 0.0).reshape(row_count, grid_len)
    rotated = rotated.astype(jnp.bfloat16)
    if group_pw == pw_count:
        send(0, rotated, form)
    else:

        def one_group(index, carry):
            send(index * group_pw, rotated, forms(index * group_pw))
            return carry

        lax.fori_loop(0, pw_count // group_pw, one_group, 0)
    copies = [
        pltpu.make_async_copy(
            message_ref, out_hbm.at[pl.ds(band * pw_count, pw_count)], sems.at[band]
        )
        for band in range(out_hbm.shape[0] // pw_count)
    ]
    for copy in copies:
        copy.start()
    for copy in copies:
        copy.wait()


def table_kernel(grid_len, column_hbm, left_ref, right_ref, column_ref, sem):
    copy = pltpu.make_async_copy(column_hbm, column_ref, sem)
    copy.start()
    copy.wait()
    count = column_ref.shape[1]
    half = grid_len // 2
    columns = column_ref[...]
    turns = iota((grid_len, count), 0) * cut(columns, grid_len)
    left_ref[0] = cosine(turns, grid_len).astype(jnp.bfloat16)
    left_ref[1] = sine(turns, grid_len).astype(jnp.bfloat16)
    tall = jnp.transpose(jnp.broadcast_to(wrap(columns, grid_len), (half, count)))
    freq = iota((count, half), 1)
    right_ref[:, :half] = cosine(tall * freq, grid_len).astype(jnp.bfloat16)
    turns = jnp.where(freq == 0, tall * half, tall * freq + (grid_len - grid_len // 4))
    right_ref[:, half:] = cosine(turns, grid_len).astype(jnp.bfloat16)


def plane_kernel(
    bands,
    own_planes,
    norm_factor,
    message_ref,
    left_ref,
    right_ref,
    out_ref,
    value_ref,
    weight_ref,
    held_ref,
    sem,
):
    chunks, rows, chunk = value_ref.shape
    grid_len = out_ref.shape[1]
    half = grid_len // 2
    sticks, lanes = message_ref.shape[1:]
    spots = 2 * bands
    height = math.gcd(grid_len, P_BLOCK)
    blocks = grid_len // height
    group = math.gcd(bands, BAND_GROUP)
    select = (iota((rows + bands, lanes), 0) == iota((rows + bands, lanes), 1)).astype(
        jnp.bfloat16
    )

    def turn(index, peak):
        pieces = chunk // sticks
        picked = dot_last(
            select, message_ref[pl.ds(index * pieces, pieces)].reshape(chunk, lanes)
        )
        value_ref[index] = picked[:rows]
        return jnp.maximum(peak, jnp.max(picked[rows:], 1, keepdims=True))

    peak = loop(chunks, turn, jnp.zeros((bands, 1), jnp.float32))
    weight_ref[...] = jnp.broadcast_to(peak * norm_factor, weight_ref.shape)

    def stick_sums(index, plane, block, first_band):
        lane = pl.ds(index * chunk, chunk)
        row = pl.ds(block * height, height)
        cos_table = left_ref[0, row, lane].reshape(height // PACK, PACK, chunk)
        sin_table = left_ref[1, row, lane].reshape(height // PACK, PACK, chunk)
        parts = []
        for band in range(group):
            at = plane * spots + first_band + band
            real, imag = (
                jnp.broadcast_to(value_ref[index, pl.ds(spot, 1), :], (PACK, chunk)).astype(
                    jnp.bfloat16
                )[None]
                for spot in (at, at + bands)
            )
            parts.append((cos_table * real - sin_table * imag).reshape(height, chunk))
            parts.append((sin_table * real + cos_table * imag).reshape(height, chunk))
        return dot(jnp.concatenate(parts, 0), right_ref[pl.ds(index * chunk, chunk), :])

    def group_sums(step):
        first_band, block = step % groups * group, step // groups
        found = []
        for plane in range(own_planes):
            if chunks == 1:
                found.append(stick_sums(0, plane, block, first_band))
            else:
                found.append(
                    lax.fori_loop(
                        0,
                        chunks,
                        lambda at, so_far: so_far + stick_sums(at, plane, block, first_band),
                        jnp.zeros((2 * group * height, grid_len), jnp.float32),
                    )
                )
        return found

    def add_squares(step, found, sums):
        first_band = step % groups * group
        result = []
        for plane in range(own_planes):
            with_cos, with_sin, mixed = sums[plane]
            for band in range(group):
                top = 2 * band * height
                a = found[plane][top : top + height, :half]
                d = found[plane][top : top + height, half:]
                top += height
                c = found[plane][top : top + height, :half]
                b = found[plane][top : top + height, half:]
                weight = weight_ref[pl.ds(first_band + band, 1), :half]
                with_cos += weight * (a * a + c * c)
                with_sin += weight * (b * b + d * d)
                mixed += weight * (c * d - a * b)
            result.append((with_cos, with_sin, mixed))
        return result

    def copy_out(plane, block):
        where = (plane, pl.ds(block * height, height))
        return pltpu.make_async_copy(
            held_ref.at[where], out_ref.at[where], sem.at[plane * blocks + block]
        )

    def finish(block, sums):
        lane = iota((height, half), 1)
        row = pl.ds(block * height, height)
        for plane, (with_cos, with_sin, mixed) in enumerate(sums):
            both, mixed = with_cos + with_sin, mixed + mixed
            ahead = jnp.where(lane == 0, with_cos, both + mixed)
            back = jnp.where(lane == 0, with_sin, both - mixed)
            held_ref[plane, row, :half] = ahead
            held_ref[plane, row, half:] = jnp.take_along_axis(
                back, jnp.where(lane == 0, 0, half - lane), axis=1
            )
            copy_out(plane, block).start()

    zero = jnp.zeros((height, half), jnp.float32)
    empty = [(zero, zero, zero)] * own_planes
    groups = bands // group

    def one_block(block, carry):
        def one_group(index, sums):
            step = block * groups + index
            return add_squares(step, group_sums(step), sums)

        finish(block, loop(groups, one_group, empty))
        return carry

    lax.fori_loop(0, blocks, one_block, 0)
    for plane in range(own_planes):
        for block in range(blocks):
            copy_out(plane, block).wait()


def shards(coeffs, rotation_matrix, stick_length, stick_column, plane_index, occupation):
    band_count = lax.axis_size("band")
    pw_count = lax.axis_size("pw")
    devices = band_count * pw_count
    in_count, sticks, grid_len = coeffs.shape[1:]
    bands = rotation_matrix.shape[2]
    stick_count = stick_column.shape[0]
    own_planes = plane_index.shape[0] // pw_count
    spots = 2 * bands
    rows = own_planes * spots
    lanes = -(-(rows + bands) // LANES) * LANES
    vmem = pl.BlockSpec(memory_space=pltpu.VMEM)
    hbm = pl.BlockSpec(memory_space=pltpu.HBM)
    table_bytes = 6 * grid_len * stick_count
    message_bytes = 2 * stick_count * lanes

    messages = pl.pallas_call(
        stick_kernel,
        out_shape=jax.ShapeDtypeStruct((devices, sticks, lanes), jnp.bfloat16),
        in_specs=[hbm] * 5,
        out_specs=hbm,
        scratch_shapes=[
            pltpu.SMEM(stick_length.shape, jnp.int32),
            pltpu.SMEM(plane_index.shape, jnp.int32),
            pltpu.SMEM(occupation.shape, jnp.int32),
            pltpu.VMEM((2, bands, in_count), jnp.bfloat16),
            pltpu.VMEM((2 * in_count * sticks, grid_len), jnp.bfloat16),
            pltpu.VMEM((pw_count, sticks, lanes), jnp.bfloat16),
            pltpu.SemaphoreType.DMA((max(4 + COEFF_COPIES, band_count),)),
        ],
        compiler_params=room(2 * message_bytes),
        name="stick_values",
    )(
        *(
            pltpu.with_memory_space_constraint(array, pltpu.HBM)
            for array in (
                stick_length,
                plane_index,
                occupation,
                jnp.swapaxes(rotation_matrix, 1, 2),
                coeffs.reshape(2 * in_count * sticks, grid_len),
            )
        )
    )
    arrived = lax.all_to_all(messages, ("band", "pw"), split_axis=0, concat_axis=0, tiled=True)
    left, right = pl.pallas_call(
        functools.partial(table_kernel, grid_len),
        out_shape=(
            jax.ShapeDtypeStruct((2, grid_len, stick_count), jnp.bfloat16),
            jax.ShapeDtypeStruct((stick_count, grid_len), jnp.bfloat16),
        ),
        in_specs=[hbm],
        out_specs=(vmem, vmem),
        scratch_shapes=[pltpu.VMEM((1, stick_count), jnp.int32), pltpu.SemaphoreType.DMA],
        compiler_params=room(table_bytes),
        cost_estimate=pl.CostEstimate(
            flops=80 * grid_len * stick_count,
            bytes_accessed=12 * grid_len * stick_count,
            transcendentals=0,
        ),
        name="stick_tables",
    )(pltpu.with_memory_space_constraint(stick_column.reshape(1, stick_count), pltpu.HBM))
    chunk = min(grid_len, stick_count)
    norm_factor = 1.0 / float(bands * stick_count * grid_len)
    blocks = own_planes * (grid_len // math.gcd(grid_len, P_BLOCK))
    return pl.pallas_call(
        functools.partial(plane_kernel, bands, own_planes, norm_factor),
        out_shape=jax.ShapeDtypeStruct((own_planes, grid_len, grid_len), jnp.float32),
        in_specs=[vmem] * 3,
        out_specs=hbm,
        scratch_shapes=[
            pltpu.VMEM((stick_count // chunk, rows, chunk), jnp.float32),
            pltpu.VMEM((bands, LANES), jnp.float32),
            pltpu.VMEM((own_planes, grid_len, grid_len), jnp.float32),
            pltpu.SemaphoreType.DMA((blocks,)),
        ],
        compiler_params=room(table_bytes, message_bytes),
        name="plane_density",
    )(arrived, left, right)


def solution(mesh):
    return jax.shard_map(
        shards,
        mesh=mesh,
        in_specs=(P(None, None, ("band", "pw"), None), P(), P(), P(), P(), P("band")),
        out_specs=P("pw", None, None),
        check_vma=False,
    )
```

```python
import functools
import math

import jax
import jax.numpy as jnp
from jax import lax
from jax.experimental import pallas as pl
from jax.experimental.pallas import tpu as pltpu
from jax.sharding import PartitionSpec as P

LANES = 128
PACK = 16
P_BLOCK = 32
BAND_GROUP = 8
GROUP_LANES = 256
COEFF_COPIES = 1
MIB = 1024 * 1024


def wrap(value, period):
    if period & (period - 1) == 0:
        return value & (period - 1)
    return lax.rem(value, period)


def cut(value, size):
    if size & (size - 1) == 0:
        return value >> (size.bit_length() - 1)
    return lax.div(value, size)


def cosine(index, period):
    fold = jnp.abs(wrap(index, period) - period // 2) - period // 4
    angle = fold.astype(jnp.float32) * (2.0 * math.pi / period)
    square = angle * angle
    series = -2.39e-08
    for factor in (2.7526e-06, -1.984090e-04, 8.3333315e-03, -1.666666664e-01, 1.0):
        series = series * square + factor
    return angle * series


def sine(index, period):
    return cosine(index + (period - period // 4), period)


def iota(shape, dim):
    return lax.broadcasted_iota(jnp.int32, shape, dim)


def dot_last(left, right):
    return lax.dot_general(
        left, right, (((1,), (1,)), ((), ())), preferred_element_type=jnp.float32
    )


def dot(left, right):
    return jnp.dot(left, right, preferred_element_type=jnp.float32)


def loop(count, body, carry):
    if count > 16:
        return lax.fori_loop(0, count, body, carry)
    for index in range(count):
        carry = body(index, carry)
    return carry


def room(*sizes):
    return pltpu.CompilerParams(vmem_limit_bytes=min(56 * MIB, 16 * MIB + 2 * sum(sizes)))


def spread(scalars, index, shape):
    result = jnp.full(shape, scalars[0])
    for place, scalar in enumerate(scalars[1:], 1):
        result = jnp.where(index == place, scalar, result)
    return result


def stick_kernel(
    length_hbm,
    plane_hbm,
    occupation_hbm,
    rotation_hbm,
    coeff_hbm,
    out_hbm,
    length_ref,
    plane_ref,
    occupation_ref,
    rotation_ref,
    coeff_ref,
    message_ref,
    sems,
):
    piece = coeff_ref.shape[0] // COEFF_COPIES
    pieces = [pl.ds(first * piece, piece) for first in range(COEFF_COPIES)]
    copies = [
        pltpu.make_async_copy(source, target, sems.at[index])
        for index, (source, target) in enumerate(
            (
                (rotation_hbm, rotation_ref),
                *((coeff_hbm.at[rows], coeff_ref.at[rows]) for rows in pieces),
                (plane_hbm, plane_ref),
                (length_hbm, length_ref),
                (occupation_hbm, occupation_ref),
            )
        )
    ]
    for copy in copies:
        copy.start()
    out_count, in_count = rotation_ref.shape[1:]
    grid_len = coeff_ref.shape[1]
    sticks = coeff_ref.shape[0] // (2 * in_count)
    plane_count = plane_ref.shape[0]
    pw_count = lax.axis_size("pw")
    own_planes = plane_count // pw_count
    own_bands = occupation_ref.shape[0]
    row_count = 2 * out_count * sticks
    lanes = message_ref.shape[2]
    band_index = lax.axis_index("band")
    first_stick = (band_index * pw_count + lax.axis_index("pw")) * sticks

    group_lanes = GROUP_LANES // (own_planes * 2 * out_count) * (own_planes * 2 * out_count)
    spots = own_planes * 2 * out_count
    group_pw = group_lanes // spots

    wide = in_count * sticks
    widen = (cut(iota((in_count, wide), 1), sticks) == iota((in_count, wide), 0)).astype(
        jnp.bfloat16
    )
    same = wrap(iota((sticks, wide), 1), sticks) == iota((sticks, wide), 0)
    copies[0].wait()
    parts = [dot(rotation_ref[part], widen) for part in range(2)]
    rows = {}
    for band in range(out_count):
        real, imag = (
            jnp.where(same, jnp.broadcast_to(part[band : band + 1], (sticks, wide)), 0.0)
            for part in parts
        )
        rows[0, band] = jnp.concatenate([real, -imag], 1)
        rows[1, band] = jnp.concatenate([imag, real], 1)
    rotation = jnp.concatenate([rows[key] for key in sorted(rows)], 0).astype(jnp.bfloat16)

    for copy in copies[1 + COEFF_COPIES :]:
        copy.wait()
    lengths = [length_ref[first_stick + place] for place in range(sticks)]
    row_lengths = spread(lengths, iota((sticks, grid_len), 0), (sticks, grid_len))
    live = iota((sticks, grid_len), 1) < row_lengths
    shape = (sticks, lanes)
    occupied = jnp.zeros(shape, jnp.int32)
    for own_band in range(own_bands):
        lane = spots + band_index * own_bands + own_band
        occupied = jnp.where(iota(shape, 1) == lane, occupation_ref[own_band], occupied)
    occupied = occupied.astype(jnp.float32)

    shape = (sticks, group_lanes)
    lane = iota(shape, 1)
    lane_plane = lax.div(lane, 2 * out_count)
    real_lane = lax.rem(lane, 2 * out_count) < out_count
    lane_band = lax.rem(lane, out_count)
    half_lengths = spread(lengths, iota(shape, 0), shape) >> 1

    def forms(first_pw):
        kinds = group_pw * own_planes
        planes = [plane_ref[first_pw * own_planes + place] for place in range(kinds)]
        kind = iota((2 * kinds, grid_len), 0)
        planes_down = spread(planes, lax.rem(kind, kinds), kind.shape)
        quarter = jnp.where(kind < kinds, 0, grid_len - grid_len // 4)
        waves = cosine(iota(kind.shape, 1) * planes_down + quarter, grid_len)
        place = iota((2 * kinds, 2 * group_lanes), 1)
        wanted = lax.div(lax.rem(place, group_lanes), 2 * out_count)
        wanted = jnp.where(place < group_lanes, wanted, wanted + kinds)
        widen = (iota(place.shape, 0) == wanted).astype(jnp.bfloat16)
        table = lax.dot_general(
            waves.astype(jnp.bfloat16),
            widen,
            (((0,), (0,)), ((), ())),
            preferred_element_type=jnp.float32,
        )
        lane_planes = spread(planes, lane_plane, shape)
        shift = half_lengths * lane_planes
        return table.astype(jnp.bfloat16), cosine(shift, grid_len), sine(shift, grid_len)

    def pick(sums, part):
        chosen = jnp.zeros(shape, jnp.float32)
        for band in range(out_count):
            top = (part * out_count + band) * sticks
            chosen = jnp.where(lane_band == band, sums[top : top + sticks], chosen)
        return chosen

    def send(first_pw, rotated, form):
        table, phase_cos, phase_sin = form
        sums = dot(rotated, table)
        with_cos, with_sin = sums[:, :group_lanes], sums[:, group_lanes:]
        real = pick(with_cos, 0) - pick(with_sin, 1)
        imag = pick(with_sin, 0) + pick(with_cos, 1)
        values = jnp.where(
            real_lane, real * phase_cos + imag * phase_sin, imag * phase_cos - real * phase_sin
        )
        for place in range(group_pw):
            first = place * spots
            tile = first // lanes * lanes
            piece = values[:, tile : tile + lanes]
            if first > tile:
                piece = pltpu.roll(piece, lanes - (first - tile), 1)
            piece = jnp.where(iota((sticks, lanes), 1) < spots, piece, occupied)
            message_ref[first_pw + place] = piece.astype(message_ref.dtype)

    if group_pw == pw_count:
        form = forms(0)
    rotated = jnp.zeros((row_count, grid_len), jnp.float32)
    for index, where in enumerate(pieces):
        copies[1 + index].wait()
        rotated += dot(rotation[:, index * piece : (index + 1) * piece], coeff_ref[where])
    rotated = rotated.reshape(row_count // sticks, sticks, grid_len)
    rotated = jnp.where(live[None], rotated, 0.0).reshape(row_count, grid_len)
    rotated = rotated.astype(jnp.bfloat16)
    if group_pw == pw_count:
        send(0, rotated, form)
    else:

        def one_group(index, carry):
            send(index * group_pw, rotated, forms(index * group_pw))
            return carry

        lax.fori_loop(0, pw_count // group_pw, one_group, 0)
    copies = [
        pltpu.make_async_copy(
            message_ref, out_hbm.at[pl.ds(band * pw_count, pw_count)], sems.at[band]
        )
        for band in range(out_hbm.shape[0] // pw_count)
    ]
    for copy in copies:
        copy.start()
    for copy in copies:
        copy.wait()


def table_kernel(grid_len, column_hbm, left_ref, right_ref, column_ref, sem):
    copy = pltpu.make_async_copy(column_hbm, column_ref, sem)
    copy.start()
    copy.wait()
    count = column_ref.shape[1]
    half = grid_len // 2
    columns = column_ref[...]
    turns = iota((half, count), 0) * cut(columns, grid_len)
    left_ref[0] = cosine(turns, grid_len).astype(jnp.bfloat16)
    left_ref[1] = sine(turns, grid_len).astype(jnp.bfloat16)
    tall = jnp.transpose(jnp.broadcast_to(columns, (half, count)))
    sign = (1 - 2 * (cut(tall, grid_len) & 1)).astype(jnp.float32)
    tall = wrap(tall, grid_len)
    freq = iota((count, half), 1)
    values = cosine(tall * freq, grid_len)
    right_ref[:, :half] = values.astype(jnp.bfloat16)
    right_ref[:, grid_len : grid_len + half] = (sign * values).astype(jnp.bfloat16)
    turns = jnp.where(freq == 0, tall * half, tall * freq + (grid_len - grid_len // 4))
    values = cosine(turns, grid_len)
    right_ref[:, half:grid_len] = values.astype(jnp.bfloat16)
    right_ref[:, grid_len + half :] = (sign * values).astype(jnp.bfloat16)


def plane_kernel(
    bands,
    own_planes,
    norm_factor,
    message_ref,
    left_ref,
    right_ref,
    out_ref,
    value_ref,
    weight_ref,
    held_ref,
    sem,
):
    rows, _, count = value_ref.shape
    chunk = min(out_ref.shape[1], count)
    chunks = count // chunk
    grid_len = out_ref.shape[1]
    half = grid_len // 2
    sticks, lanes = message_ref.shape[1:]
    spots = 2 * bands
    height = math.gcd(half, P_BLOCK)
    blocks = half // height
    group = math.gcd(bands, BAND_GROUP)
    select = (iota((rows + bands, lanes), 0) == iota((rows + bands, lanes), 1)).astype(
        jnp.bfloat16
    )

    def turn(index, peak):
        pieces = chunk // sticks
        picked = dot_last(
            select, message_ref[pl.ds(index * pieces, pieces)].reshape(chunk, lanes)
        )
        for row in range(rows):
            value_ref[row, :, pl.ds(index * chunk, chunk)] = jnp.broadcast_to(
                picked[row : row + 1], (PACK, chunk)
            ).astype(jnp.bfloat16)
        return jnp.maximum(peak, jnp.max(picked[rows:], 1, keepdims=True))

    peak = loop(chunks, turn, jnp.zeros((bands, 1), jnp.float32))
    weight_ref[...] = jnp.broadcast_to(peak * norm_factor, weight_ref.shape)

    def stick_sums(index, plane, block, first_band):
        lane = pl.ds(index * chunk, chunk)
        row = pl.ds(block * height, height)
        cos_table = left_ref[0, row, lane].reshape(height // PACK, PACK, chunk)
        sin_table = left_ref[1, row, lane].reshape(height // PACK, PACK, chunk)
        parts = []
        for band in range(group):
            at = plane * spots + first_band + band
            real, imag = value_ref[at, :, lane][None], value_ref[at + bands, :, lane][None]
            parts.append((cos_table * real - sin_table * imag).reshape(height, chunk))
            parts.append((sin_table * real + cos_table * imag).reshape(height, chunk))
        return dot(jnp.concatenate(parts, 0), right_ref[pl.ds(index * chunk, chunk), :])

    def group_sums(step):
        first_band, block = step % groups * group, step // groups
        found = []
        for plane in range(own_planes):
            if chunks == 1:
                found.append(stick_sums(0, plane, block, first_band))
            else:
                found.append(
                    lax.fori_loop(
                        0,
                        chunks,
                        lambda at, so_far: so_far + stick_sums(at, plane, block, first_band),
                        jnp.zeros((2 * group * height, 2 * grid_len), jnp.float32),
                    )
                )
        return found

    def add_squares(step, found, sums):
        first_band = step % groups * group
        result = []
        for place, (with_cos, with_sin, mixed) in enumerate(sums):
            plane, left = place // 2, place % 2 * grid_len
            for band in range(group):
                top = 2 * band * height
                a = found[plane][top : top + height, left : left + half]
                d = found[plane][top : top + height, left + half : left + grid_len]
                top += height
                c = found[plane][top : top + height, left : left + half]
                b = found[plane][top : top + height, left + half : left + grid_len]
                weight = weight_ref[pl.ds(first_band + band, 1), :half]
                with_cos += weight * (a * a + c * c)
                with_sin += weight * (b * b + d * d)
                mixed += weight * (c * d - a * b)
            result.append((with_cos, with_sin, mixed))
        return result

    def copy_out(place, block):
        where = (place // 2, pl.ds(place % 2 * half + block * height, height))
        return pltpu.make_async_copy(
            held_ref.at[where], out_ref.at[where], sem.at[place * blocks + block]
        )

    def finish(block, sums):
        lane = iota((height, half), 1)
        for place, (with_cos, with_sin, mixed) in enumerate(sums):
            both, mixed = with_cos + with_sin, mixed + mixed
            ahead = jnp.where(lane == 0, with_cos, both + mixed)
            back = jnp.where(lane == 0, with_sin, both - mixed)
            row = pl.ds(place % 2 * half + block * height, height)
            held_ref[place // 2, row, :half] = ahead
            held_ref[place // 2, row, half:] = jnp.take_along_axis(
                back, jnp.where(lane == 0, 0, half - lane), axis=1
            )
            copy_out(place, block).start()

    zero = jnp.zeros((height, half), jnp.float32)
    empty = [(zero, zero, zero)] * (2 * own_planes)
    groups = bands // group
    if blocks * groups > 32:

        def one_block(block, carry):
            def one_group(index, sums):
                step = block * groups + index
                return add_squares(step, group_sums(step), sums)

            finish(block, lax.fori_loop(0, groups, one_group, empty))
            return carry

        lax.fori_loop(0, blocks, one_block, 0)
    else:
        sums, ahead = empty, group_sums(0)
        for step in range(blocks * groups):
            found = ahead
            if step + 1 < blocks * groups:
                ahead = group_sums(step + 1)
            sums = add_squares(step, found, sums)
            if (step + 1) % groups == 0:
                finish(step // groups, sums)
                sums = empty
    for place in range(2 * own_planes):
        for block in range(blocks):
            copy_out(place, block).wait()


def shards(coeffs, rotation_matrix, stick_length, stick_column, plane_index, occupation):
    band_count = lax.axis_size("band")
    pw_count = lax.axis_size("pw")
    devices = band_count * pw_count
    in_count, sticks, grid_len = coeffs.shape[1:]
    bands = rotation_matrix.shape[2]
    stick_count = stick_column.shape[0]
    own_planes = plane_index.shape[0] // pw_count
    spots = 2 * bands
    rows = own_planes * spots
    lanes = -(-(rows + bands) // LANES) * LANES
    vmem = pl.BlockSpec(memory_space=pltpu.VMEM)
    hbm = pl.BlockSpec(memory_space=pltpu.HBM)
    table_bytes = 8 * grid_len * stick_count
    message_bytes = 2 * stick_count * lanes

    messages = pl.pallas_call(
        stick_kernel,
        out_shape=jax.ShapeDtypeStruct((devices, sticks, lanes), jnp.bfloat16),
        in_specs=[hbm] * 5,
        out_specs=hbm,
        scratch_shapes=[
            pltpu.SMEM(stick_length.shape, jnp.int32),
            pltpu.SMEM(plane_index.shape, jnp.int32),
            pltpu.SMEM(occupation.shape, jnp.int32),
            pltpu.VMEM((2, bands, in_count), jnp.bfloat16),
            pltpu.VMEM((2 * in_count * sticks, grid_len), jnp.bfloat16),
            pltpu.VMEM((pw_count, sticks, lanes), jnp.bfloat16),
            pltpu.SemaphoreType.DMA((max(4 + COEFF_COPIES, band_count),)),
        ],
        compiler_params=room(2 * message_bytes),
        name="stick_values",
    )(
        *(
            pltpu.with_memory_space_constraint(array, pltpu.HBM)
            for array in (
                stick_length,
                plane_index,
                occupation,
                jnp.swapaxes(rotation_matrix, 1, 2),
                coeffs.reshape(2 * in_count * sticks, grid_len),
            )
        )
    )
    arrived = lax.all_to_all(messages, ("band", "pw"), split_axis=0, concat_axis=0, tiled=True)
    left, right = pl.pallas_call(
        functools.partial(table_kernel, grid_len),
        out_shape=(
            jax.ShapeDtypeStruct((2, grid_len // 2, stick_count), jnp.bfloat16),
            jax.ShapeDtypeStruct((stick_count, 2 * grid_len), jnp.bfloat16),
        ),
        in_specs=[hbm],
        out_specs=(vmem, vmem),
        scratch_shapes=[pltpu.VMEM((1, stick_count), jnp.int32), pltpu.SemaphoreType.DMA],
        compiler_params=room(table_bytes),
        cost_estimate=pl.CostEstimate(
            flops=80 * grid_len * stick_count,
            bytes_accessed=12 * grid_len * stick_count,
            transcendentals=0,
        ),
        name="stick_tables",
    )(pltpu.with_memory_space_constraint(stick_column.reshape(1, stick_count), pltpu.HBM))
    norm_factor = 1.0 / float(bands * stick_count * grid_len)
    blocks = 2 * own_planes * (grid_len // 2 // math.gcd(grid_len // 2, P_BLOCK))
    return pl.pallas_call(
        functools.partial(plane_kernel, bands, own_planes, norm_factor),
        out_shape=jax.ShapeDtypeStruct((own_planes, grid_len, grid_len), jnp.float32),
        in_specs=[vmem] * 3,
        out_specs=hbm,
        scratch_shapes=[
            pltpu.VMEM((rows, PACK, stick_count), jnp.bfloat16),
            pltpu.VMEM((bands, LANES), jnp.float32),
            pltpu.VMEM((own_planes, grid_len, grid_len), jnp.float32),
            pltpu.SemaphoreType.DMA((blocks,)),
        ],
        compiler_params=room(table_bytes, message_bytes),
        name="plane_density",
    )(arrived, left, right)


def solution(mesh):
    return jax.shard_map(
        shards,
        mesh=mesh,
        in_specs=(P(None, None, ("band", "pw"), None), P(), P(), P(), P(), P("band")),
        out_specs=P("pw", None, None),
        check_vma=False,
    )
```

```python
import functools
import math

import jax
import jax.numpy as jnp
from jax import lax
from jax.experimental import pallas as pl
from jax.experimental.pallas import tpu as pltpu
from jax.sharding import PartitionSpec as P

LANES = 128
PACK = 16
P_BLOCK = 32
BAND_GROUP = 8
GROUP_LANES = 256
GATHER_LIMIT = 1 << 22
COEFF_COPIES = 1
MIB = 1024 * 1024


def wrap(value, period):
    if period & (period - 1) == 0:
        return value & (period - 1)
    return lax.rem(value, period)


def cut(value, size):
    if size & (size - 1) == 0:
        return value >> (size.bit_length() - 1)
    return lax.div(value, size)


def cosine(index, period):
    fold = jnp.abs(wrap(index, period) - period // 2) - period // 4
    angle = fold.astype(jnp.float32) * (2.0 * math.pi / period)
    square = angle * angle
    series = -2.39e-08
    for factor in (2.7526e-06, -1.984090e-04, 8.3333315e-03, -1.666666664e-01, 1.0):
        series = series * square + factor
    return angle * series


def sine(index, period):
    return cosine(index + (period - period // 4), period)


def iota(shape, dim):
    return lax.broadcasted_iota(jnp.int32, shape, dim)


def dot_last(left, right):
    return lax.dot_general(
        left, right, (((1,), (1,)), ((), ())), preferred_element_type=jnp.float32
    )


def dot(left, right):
    return jnp.dot(left, right, preferred_element_type=jnp.float32)


def loop(count, body, carry):
    if count > 16:
        return lax.fori_loop(0, count, body, carry)
    for index in range(count):
        carry = body(index, carry)
    return carry


def room(*sizes):
    return pltpu.CompilerParams(vmem_limit_bytes=min(56 * MIB, 16 * MIB + 2 * sum(sizes)))


def spread(scalars, index, shape):
    result = jnp.full(shape, scalars[0])
    for place, scalar in enumerate(scalars[1:], 1):
        result = jnp.where(index == place, scalar, result)
    return result


def stick_kernel(
    length_hbm,
    plane_hbm,
    occupation_hbm,
    rotation_hbm,
    coeff_hbm,
    out_hbm,
    length_ref,
    plane_ref,
    occupation_ref,
    rotation_ref,
    coeff_ref,
    message_ref,
    sems,
):
    piece = coeff_ref.shape[0] // COEFF_COPIES
    pieces = [pl.ds(first * piece, piece) for first in range(COEFF_COPIES)]
    copies = [
        pltpu.make_async_copy(source, target, sems.at[index])
        for index, (source, target) in enumerate(
            (
                (rotation_hbm, rotation_ref),
                *((coeff_hbm.at[rows], coeff_ref.at[rows]) for rows in pieces),
                (plane_hbm, plane_ref),
                (length_hbm, length_ref),
                (occupation_hbm, occupation_ref),
            )
        )
    ]
    for copy in copies:
        copy.start()
    out_count, in_count = rotation_ref.shape[1:]
    grid_len = coeff_ref.shape[1]
    sticks = coeff_ref.shape[0] // (2 * in_count)
    plane_count = plane_ref.shape[0]
    pw_count = lax.axis_size("pw")
    own_planes = plane_count // pw_count
    own_bands = occupation_ref.shape[0]
    row_count = 2 * out_count * sticks
    lanes = message_ref.shape[2]
    band_index = lax.axis_index("band")
    first_stick = (band_index * pw_count + lax.axis_index("pw")) * sticks

    group_lanes = GROUP_LANES // (own_planes * 2 * out_count) * (own_planes * 2 * out_count)
    spots = own_planes * 2 * out_count
    group_pw = group_lanes // spots

    wide = in_count * sticks
    widen = (cut(iota((in_count, wide), 1), sticks) == iota((in_count, wide), 0)).astype(
        jnp.bfloat16
    )
    same = wrap(iota((sticks, wide), 1), sticks) == iota((sticks, wide), 0)
    copies[0].wait()
    parts = [dot(rotation_ref[part], widen) for part in range(2)]
    rows = {}
    for band in range(out_count):
        real, imag = (
            jnp.where(same, jnp.broadcast_to(part[band : band + 1], (sticks, wide)), 0.0)
            for part in parts
        )
        rows[0, band] = jnp.concatenate([real, -imag], 1)
        rows[1, band] = jnp.concatenate([imag, real], 1)
    rotation = jnp.concatenate([rows[key] for key in sorted(rows)], 0).astype(jnp.bfloat16)

    for copy in copies[1 + COEFF_COPIES :]:
        copy.wait()
    lengths = [length_ref[first_stick + place] for place in range(sticks)]
    row_lengths = spread(lengths, iota((sticks, grid_len), 0), (sticks, grid_len))
    live = iota((sticks, grid_len), 1) < row_lengths
    shape = (sticks, lanes)
    occupied = jnp.zeros(shape, jnp.int32)
    for own_band in range(own_bands):
        lane = spots + band_index * own_bands + own_band
        occupied = jnp.where(iota(shape, 1) == lane, occupation_ref[own_band], occupied)
    occupied = occupied.astype(jnp.float32)

    shape = (sticks, group_lanes)
    lane = iota(shape, 1)
    lane_plane = lax.div(lane, 2 * out_count)
    real_lane = lax.rem(lane, 2 * out_count) < out_count
    lane_band = lax.rem(lane, out_count)
    half_lengths = spread(lengths, iota(shape, 0), shape) >> 1

    def forms(first_pw):
        kinds = group_pw * own_planes
        planes = [plane_ref[first_pw * own_planes + place] for place in range(kinds)]
        kind = iota((2 * kinds, grid_len), 0)
        planes_down = spread(planes, lax.rem(kind, kinds), kind.shape)
        quarter = jnp.where(kind < kinds, 0, grid_len - grid_len // 4)
        waves = cosine(iota(kind.shape, 1) * planes_down + quarter, grid_len)
        place = iota((2 * kinds, 2 * group_lanes), 1)
        wanted = lax.div(lax.rem(place, group_lanes), 2 * out_count)
        wanted = jnp.where(place < group_lanes, wanted, wanted + kinds)
        widen = (iota(place.shape, 0) == wanted).astype(jnp.bfloat16)
        table = lax.dot_general(
            waves.astype(jnp.bfloat16),
            widen,
            (((0,), (0,)), ((), ())),
            preferred_element_type=jnp.float32,
        )
        lane_planes = spread(planes, lane_plane, shape)
        shift = half_lengths * lane_planes
        return table.astype(jnp.bfloat16), cosine(shift, grid_len), sine(shift, grid_len)

    def pick(sums, part):
        chosen = jnp.zeros(shape, jnp.float32)
        for band in range(out_count):
            top = (part * out_count + band) * sticks
            chosen = jnp.where(lane_band == band, sums[top : top + sticks], chosen)
        return chosen

    def send(first_pw, rotated, form):
        table, phase_cos, phase_sin = form
        sums = dot(rotated, table)
        with_cos, with_sin = sums[:, :group_lanes], sums[:, group_lanes:]
        real = pick(with_cos, 0) - pick(with_sin, 1)
        imag = pick(with_sin, 0) + pick(with_cos, 1)
        values = jnp.where(
            real_lane, real * phase_cos + imag * phase_sin, imag * phase_cos - real * phase_sin
        )
        for place in range(group_pw):
            first = place * spots
            tile = first // lanes * lanes
            piece = values[:, tile : tile + lanes]
            if first > tile:
                piece = pltpu.roll(piece, lanes - (first - tile), 1)
            piece = jnp.where(iota((sticks, lanes), 1) < spots, piece, occupied)
            message_ref[first_pw + place] = piece.astype(message_ref.dtype)

    if group_pw == pw_count:
        form = forms(0)
    rotated = jnp.zeros((row_count, grid_len), jnp.float32)
    for index, where in enumerate(pieces):
        copies[1 + index].wait()
        rotated += dot(rotation[:, index * piece : (index + 1) * piece], coeff_ref[where])
    rotated = rotated.reshape(row_count // sticks, sticks, grid_len)
    rotated = jnp.where(live[None], rotated, 0.0).reshape(row_count, grid_len)
    rotated = rotated.astype(jnp.bfloat16)
    if group_pw == pw_count:
        send(0, rotated, form)
    else:

        def one_group(index, carry):
            send(index * group_pw, rotated, forms(index * group_pw))
            return carry

        lax.fori_loop(0, pw_count // group_pw, one_group, 0)
    copy = pltpu.make_async_copy(message_ref, out_hbm, sems.at[0])
    copy.start()
    copy.wait()


def table_kernel(grid_len, column_hbm, left_ref, right_ref, column_ref, sem):
    copy = pltpu.make_async_copy(column_hbm, column_ref, sem)
    copy.start()
    copy.wait()
    count = column_ref.shape[1]
    half = grid_len // 2
    columns = column_ref[...]
    turns = iota((half, count), 0) * cut(columns, grid_len)
    left_ref[0] = cosine(turns, grid_len).astype(jnp.bfloat16)
    left_ref[1] = sine(turns, grid_len).astype(jnp.bfloat16)
    tall = jnp.transpose(jnp.broadcast_to(columns, (half, count)))
    sign = (1 - 2 * (cut(tall, grid_len) & 1)).astype(jnp.float32)
    tall = wrap(tall, grid_len)
    freq = iota((count, half), 1)
    values = cosine(tall * freq, grid_len)
    right_ref[:, :half] = values.astype(jnp.bfloat16)
    right_ref[:, grid_len : grid_len + half] = (sign * values).astype(jnp.bfloat16)
    turns = jnp.where(freq == 0, tall * half, tall * freq + (grid_len - grid_len // 4))
    values = cosine(turns, grid_len)
    right_ref[:, half:grid_len] = values.astype(jnp.bfloat16)
    right_ref[:, grid_len + half :] = (sign * values).astype(jnp.bfloat16)


def plane_kernel(
    bands,
    own_planes,
    norm_factor,
    gathered_ref,
    left_ref,
    right_ref,
    out_ref,
    message_ref,
    message_sem,
    value_ref,
    weight_ref,
    held_ref,
    sem,
):
    place = lax.axis_index("pw") if gathered_ref.shape[1] > 1 else 0
    copy = pltpu.make_async_copy(
        gathered_ref.at[:, place], message_ref, message_sem
    )
    copy.start()
    rows, _, count = value_ref.shape
    chunk = min(out_ref.shape[1], count)
    chunks = count // chunk
    grid_len = out_ref.shape[1]
    half = grid_len // 2
    sticks, lanes = message_ref.shape[1:]
    spots = 2 * bands
    height = math.gcd(half, P_BLOCK)
    blocks = half // height
    group = math.gcd(bands, BAND_GROUP)
    select = (iota((rows + bands, lanes), 0) == iota((rows + bands, lanes), 1)).astype(
        jnp.bfloat16
    )

    def turn(index, peak):
        pieces = chunk // sticks
        picked = dot_last(
            select, message_ref[pl.ds(index * pieces, pieces)].reshape(chunk, lanes)
        )
        for row in range(rows):
            value_ref[row, :, pl.ds(index * chunk, chunk)] = jnp.broadcast_to(
                picked[row : row + 1], (PACK, chunk)
            ).astype(jnp.bfloat16)
        return jnp.maximum(peak, jnp.max(picked[rows:], 1, keepdims=True))

    copy.wait()
    peak = loop(chunks, turn, jnp.zeros((bands, 1), jnp.float32))
    weight_ref[...] = jnp.broadcast_to(peak * norm_factor, weight_ref.shape)

    def stick_sums(index, plane, block, first_band):
        lane = pl.ds(index * chunk, chunk)
        row = pl.ds(block * height, height)
        cos_table = left_ref[0, row, lane].reshape(height // PACK, PACK, chunk)
        sin_table = left_ref[1, row, lane].reshape(height // PACK, PACK, chunk)
        parts = []
        for band in range(group):
            at = plane * spots + first_band + band
            real, imag = value_ref[at, :, lane][None], value_ref[at + bands, :, lane][None]
            parts.append((cos_table * real - sin_table * imag).reshape(height, chunk))
            parts.append((sin_table * real + cos_table * imag).reshape(height, chunk))
        return dot(jnp.concatenate(parts, 0), right_ref[pl.ds(index * chunk, chunk), :])

    def group_sums(step):
        first_band, block = step % groups * group, step // groups
        found = []
        for plane in range(own_planes):
            if chunks == 1:
                found.append(stick_sums(0, plane, block, first_band))
            else:
                found.append(
                    lax.fori_loop(
                        0,
                        chunks,
                        lambda at, so_far: so_far + stick_sums(at, plane, block, first_band),
                        jnp.zeros((2 * group * height, 2 * grid_len), jnp.float32),
                    )
                )
        return found

    def add_squares(step, found, sums):
        first_band = step % groups * group
        result = []
        for place, (with_cos, with_sin, mixed) in enumerate(sums):
            plane, left = place // 2, place % 2 * grid_len
            for band in range(group):
                top = 2 * band * height
                a = found[plane][top : top + height, left : left + half]
                d = found[plane][top : top + height, left + half : left + grid_len]
                top += height
                c = found[plane][top : top + height, left : left + half]
                b = found[plane][top : top + height, left + half : left + grid_len]
                weight = weight_ref[pl.ds(first_band + band, 1), :half]
                with_cos += weight * (a * a + c * c)
                with_sin += weight * (b * b + d * d)
                mixed += weight * (c * d - a * b)
            result.append((with_cos, with_sin, mixed))
        return result

    def copy_out(place, block):
        where = (place // 2, pl.ds(place % 2 * half + block * height, height))
        return pltpu.make_async_copy(
            held_ref.at[where], out_ref.at[where], sem.at[place * blocks + block]
        )

    def finish(block, sums):
        lane = iota((height, half), 1)
        for place, (with_cos, with_sin, mixed) in enumerate(sums):
            both, mixed = with_cos + with_sin, mixed + mixed
            ahead = jnp.where(lane == 0, with_cos, both + mixed)
            back = jnp.where(lane == 0, with_sin, both - mixed)
            row = pl.ds(place % 2 * half + block * height, height)
            held_ref[place // 2, row, :half] = ahead
            held_ref[place // 2, row, half:] = jnp.take_along_axis(
                back, jnp.where(lane == 0, 0, half - lane), axis=1
            )
            copy_out(place, block).start()

    zero = jnp.zeros((height, half), jnp.float32)
    empty = [(zero, zero, zero)] * (2 * own_planes)
    groups = bands // group
    if blocks * groups > 32:

        def one_block(block, carry):
            def one_group(index, sums):
                step = block * groups + index
                return add_squares(step, group_sums(step), sums)

            finish(block, lax.fori_loop(0, groups, one_group, empty))
            return carry

        lax.fori_loop(0, blocks, one_block, 0)
    else:
        sums, ahead = empty, group_sums(0)
        for step in range(blocks * groups):
            found = ahead
            if step + 1 < blocks * groups:
                ahead = group_sums(step + 1)
            sums = add_squares(step, found, sums)
            if (step + 1) % groups == 0:
                finish(step // groups, sums)
                sums = empty
    for place in range(2 * own_planes):
        for block in range(blocks):
            copy_out(place, block).wait()


def shards(coeffs, rotation_matrix, stick_length, stick_column, plane_index, occupation):
    band_count = lax.axis_size("band")
    pw_count = lax.axis_size("pw")
    devices = band_count * pw_count
    in_count, sticks, grid_len = coeffs.shape[1:]
    bands = rotation_matrix.shape[2]
    stick_count = stick_column.shape[0]
    own_planes = plane_index.shape[0] // pw_count
    spots = 2 * bands
    rows = own_planes * spots
    lanes = -(-(rows + bands) // LANES) * LANES
    vmem = pl.BlockSpec(memory_space=pltpu.VMEM)
    hbm = pl.BlockSpec(memory_space=pltpu.HBM)
    table_bytes = 8 * grid_len * stick_count
    message_bytes = 2 * stick_count * lanes

    messages = pl.pallas_call(
        stick_kernel,
        out_shape=jax.ShapeDtypeStruct((pw_count, sticks, lanes), jnp.bfloat16),
        in_specs=[hbm] * 5,
        out_specs=hbm,
        scratch_shapes=[
            pltpu.SMEM(stick_length.shape, jnp.int32),
            pltpu.SMEM(plane_index.shape, jnp.int32),
            pltpu.SMEM(occupation.shape, jnp.int32),
            pltpu.VMEM((2, bands, in_count), jnp.bfloat16),
            pltpu.VMEM((2 * in_count * sticks, grid_len), jnp.bfloat16),
            pltpu.VMEM((pw_count, sticks, lanes), jnp.bfloat16),
            pltpu.SemaphoreType.DMA((max(4 + COEFF_COPIES, band_count),)),
        ],
        compiler_params=room(2 * message_bytes),
        name="stick_values",
    )(
        *(
            pltpu.with_memory_space_constraint(array, pltpu.HBM)
            for array in (
                stick_length,
                plane_index,
                occupation,
                jnp.swapaxes(rotation_matrix, 1, 2),
                coeffs.reshape(2 * in_count * sticks, grid_len),
            )
        )
    )
    if devices * pw_count * sticks * lanes <= GATHER_LIMIT:
        arrived = lax.all_gather(messages, ("band", "pw"), axis=0)
    else:
        arrived = lax.all_to_all(
            jnp.concatenate([messages] * band_count, 0),
            ("band", "pw"),
            split_axis=0,
            concat_axis=0,
            tiled=True,
        )[:, None]
    left, right = pl.pallas_call(
        functools.partial(table_kernel, grid_len),
        out_shape=(
            jax.ShapeDtypeStruct((2, grid_len // 2, stick_count), jnp.bfloat16),
            jax.ShapeDtypeStruct((stick_count, 2 * grid_len), jnp.bfloat16),
        ),
        in_specs=[hbm],
        out_specs=(vmem, vmem),
        scratch_shapes=[pltpu.VMEM((1, stick_count), jnp.int32), pltpu.SemaphoreType.DMA],
        compiler_params=room(table_bytes),
        cost_estimate=pl.CostEstimate(
            flops=80 * grid_len * stick_count,
            bytes_accessed=12 * grid_len * stick_count,
            transcendentals=0,
        ),
        name="stick_tables",
    )(pltpu.with_memory_space_constraint(stick_column.reshape(1, stick_count), pltpu.HBM))
    norm_factor = 1.0 / float(bands * stick_count * grid_len)
    blocks = 2 * own_planes * (grid_len // 2 // math.gcd(grid_len // 2, P_BLOCK))
    return pl.pallas_call(
        functools.partial(plane_kernel, bands, own_planes, norm_factor),
        out_shape=jax.ShapeDtypeStruct((own_planes, grid_len, grid_len), jnp.float32),
        in_specs=[hbm, vmem, vmem],
        out_specs=hbm,
        scratch_shapes=[
            pltpu.VMEM((devices, sticks, lanes), jnp.bfloat16),
            pltpu.SemaphoreType.DMA,
            pltpu.VMEM((rows, PACK, stick_count), jnp.bfloat16),
            pltpu.VMEM((bands, LANES), jnp.float32),
            pltpu.VMEM((own_planes, grid_len, grid_len), jnp.float32),
            pltpu.SemaphoreType.DMA((blocks,)),
        ],
        compiler_params=room(table_bytes, message_bytes),
        name="plane_density",
    )(pltpu.with_memory_space_constraint(arrived, pltpu.HBM), left, right)


def solution(mesh):
    return jax.shard_map(
        shards,
        mesh=mesh,
        in_specs=(P(None, None, ("band", "pw"), None), P(), P(), P(), P(), P("band")),
        out_specs=P("pw", None, None),
        check_vma=False,
    )
```

```python
import functools
import math

import jax
import jax.numpy as jnp
from jax import lax
from jax.experimental import pallas as pl
from jax.experimental.pallas import tpu as pltpu
from jax.sharding import PartitionSpec as P

LANES = 128
PACK = 16
P_BLOCK = 32
BAND_GROUP = 8
GROUP_LANES = 256
COEFF_COPIES = 1
MIB = 1024 * 1024


def wrap(value, period):
    if period & (period - 1) == 0:
        return value & (period - 1)
    return lax.rem(value, period)


def cut(value, size):
    if size & (size - 1) == 0:
        return value >> (size.bit_length() - 1)
    return lax.div(value, size)


def cosine(index, period):
    fold = jnp.abs(wrap(index, period) - period // 2) - period // 4
    angle = fold.astype(jnp.float32) * (2.0 * math.pi / period)
    square = angle * angle
    series = -2.39e-08
    for factor in (2.7526e-06, -1.984090e-04, 8.3333315e-03, -1.666666664e-01, 1.0):
        series = series * square + factor
    return angle * series


def sine(index, period):
    return cosine(index + (period - period // 4), period)


def iota(shape, dim):
    return lax.broadcasted_iota(jnp.int32, shape, dim)


def dot_last(left, right):
    return lax.dot_general(
        left, right, (((1,), (1,)), ((), ())), preferred_element_type=jnp.float32
    )


def dot(left, right):
    return jnp.dot(left, right, preferred_element_type=jnp.float32)


def loop(count, body, carry):
    if count > 16:
        return lax.fori_loop(0, count, body, carry)
    for index in range(count):
        carry = body(index, carry)
    return carry


def room(*sizes):
    return pltpu.CompilerParams(vmem_limit_bytes=min(56 * MIB, 16 * MIB + 2 * sum(sizes)))


def lane_groups(sticks, spots, bands, lanes):
    groups = 1
    while 2 * groups * spots + bands <= lanes and sticks % (2 * groups) == 0 and sticks > 4 * groups:
        groups *= 2
    return groups


def spread(scalars, index, shape):
    result = jnp.full(shape, scalars[0])
    for place, scalar in enumerate(scalars[1:], 1):
        result = jnp.where(index == place, scalar, result)
    return result


def stick_kernel(
    length_hbm,
    plane_hbm,
    occupation_hbm,
    rotation_hbm,
    coeff_hbm,
    out_hbm,
    length_ref,
    plane_ref,
    occupation_ref,
    rotation_ref,
    coeff_ref,
    message_ref,
    sems,
):
    piece = coeff_ref.shape[0] // COEFF_COPIES
    pieces = [pl.ds(first * piece, piece) for first in range(COEFF_COPIES)]
    copies = [
        pltpu.make_async_copy(source, target, sems.at[index])
        for index, (source, target) in enumerate(
            (
                (rotation_hbm, rotation_ref),
                *((coeff_hbm.at[rows], coeff_ref.at[rows]) for rows in pieces),
                (plane_hbm, plane_ref),
                (length_hbm, length_ref),
                (occupation_hbm, occupation_ref),
            )
        )
    ]
    for copy in copies:
        copy.start()
    out_count, in_count = rotation_ref.shape[1:]
    grid_len = coeff_ref.shape[1]
    sticks = coeff_ref.shape[0] // (2 * in_count)
    plane_count = plane_ref.shape[0]
    pw_count = lax.axis_size("pw")
    own_planes = plane_count // pw_count
    own_bands = occupation_ref.shape[0]
    row_count = 2 * out_count * sticks
    lanes = message_ref.shape[2]
    band_index = lax.axis_index("band")
    first_stick = (band_index * pw_count + lax.axis_index("pw")) * sticks

    group_lanes = GROUP_LANES // (own_planes * 2 * out_count) * (own_planes * 2 * out_count)
    spots = own_planes * 2 * out_count
    side = lane_groups(sticks, spots, out_count, lanes)
    group_pw = group_lanes // spots

    wide = in_count * sticks
    widen = (cut(iota((in_count, wide), 1), sticks) == iota((in_count, wide), 0)).astype(
        jnp.bfloat16
    )
    same = wrap(iota((sticks, wide), 1), sticks) == iota((sticks, wide), 0)
    copies[0].wait()
    parts = [dot(rotation_ref[part], widen) for part in range(2)]
    rows = {}
    for band in range(out_count):
        real, imag = (
            jnp.where(same, jnp.broadcast_to(part[band : band + 1], (sticks, wide)), 0.0)
            for part in parts
        )
        rows[0, band] = jnp.concatenate([real, -imag], 1)
        rows[1, band] = jnp.concatenate([imag, real], 1)
    rotation = jnp.concatenate([rows[key] for key in sorted(rows)], 0).astype(jnp.bfloat16)

    for copy in copies[1 + COEFF_COPIES :]:
        copy.wait()
    lengths = [length_ref[first_stick + place] for place in range(sticks)]
    row_lengths = spread(lengths, iota((sticks, grid_len), 0), (sticks, grid_len))
    live = iota((sticks, grid_len), 1) < row_lengths
    shape = (sticks, lanes)
    occupied = jnp.zeros(shape, jnp.int32)
    for own_band in range(own_bands):
        lane = side * spots + band_index * own_bands + own_band
        occupied = jnp.where(iota(shape, 1) == lane, occupation_ref[own_band], occupied)
    occupied = occupied.astype(jnp.float32)

    shape = (sticks, group_lanes)
    lane = iota(shape, 1)
    lane_plane = lax.div(lane, 2 * out_count)
    real_lane = lax.rem(lane, 2 * out_count) < out_count
    lane_band = lax.rem(lane, out_count)
    half_lengths = spread(lengths, iota(shape, 0), shape) >> 1

    def forms(first_pw):
        kinds = group_pw * own_planes
        planes = [plane_ref[first_pw * own_planes + place] for place in range(kinds)]
        kind = iota((2 * kinds, grid_len), 0)
        planes_down = spread(planes, lax.rem(kind, kinds), kind.shape)
        quarter = jnp.where(kind < kinds, 0, grid_len - grid_len // 4)
        waves = cosine(iota(kind.shape, 1) * planes_down + quarter, grid_len)
        place = iota((2 * kinds, 2 * group_lanes), 1)
        wanted = lax.div(lax.rem(place, group_lanes), 2 * out_count)
        wanted = jnp.where(place < group_lanes, wanted, wanted + kinds)
        widen = (iota(place.shape, 0) == wanted).astype(jnp.bfloat16)
        table = lax.dot_general(
            waves.astype(jnp.bfloat16),
            widen,
            (((0,), (0,)), ((), ())),
            preferred_element_type=jnp.float32,
        )
        lane_planes = spread(planes, lane_plane, shape)
        shift = half_lengths * lane_planes
        return table.astype(jnp.bfloat16), cosine(shift, grid_len), sine(shift, grid_len)

    def pick(sums, part):
        chosen = jnp.zeros(shape, jnp.float32)
        for band in range(out_count):
            top = (part * out_count + band) * sticks
            chosen = jnp.where(lane_band == band, sums[top : top + sticks], chosen)
        return chosen

    def send(first_pw, rotated, form):
        table, phase_cos, phase_sin = form
        sums = dot(rotated, table)
        with_cos, with_sin = sums[:, :group_lanes], sums[:, group_lanes:]
        real = pick(with_cos, 0) - pick(with_sin, 1)
        imag = pick(with_sin, 0) + pick(with_cos, 1)
        values = jnp.where(
            real_lane, real * phase_cos + imag * phase_sin, imag * phase_cos - real * phase_sin
        )
        for place in range(group_pw):
            first = place * spots
            tile = first // lanes * lanes
            part = values[:, tile : tile + lanes]
            message = occupied
            for index in reversed(range(side)):
                shift = (index * spots - (first - tile)) % lanes
                piece = pltpu.roll(part, shift, 1) if shift else part
                if index:
                    piece = pltpu.roll(piece, sticks - index * (sticks // side), 0)
                message = jnp.where(
                    iota((sticks, lanes), 1) < (index + 1) * spots, piece, message
                )
            message_ref[first_pw + place] = message[: sticks // side].astype(message_ref.dtype)

    if group_pw == pw_count:
        form = forms(0)
    rotated = jnp.zeros((row_count, grid_len), jnp.float32)
    for index, where in enumerate(pieces):
        copies[1 + index].wait()
        rotated += dot(rotation[:, index * piece : (index + 1) * piece], coeff_ref[where])
    rotated = rotated.reshape(row_count // sticks, sticks, grid_len)
    rotated = jnp.where(live[None], rotated, 0.0).reshape(row_count, grid_len)
    rotated = rotated.astype(jnp.bfloat16)
    if group_pw == pw_count:
        send(0, rotated, form)
    else:

        def one_group(index, carry):
            send(index * group_pw, rotated, forms(index * group_pw))
            return carry

        lax.fori_loop(0, pw_count // group_pw, one_group, 0)
    copies = [
        pltpu.make_async_copy(
            message_ref, out_hbm.at[pl.ds(band * pw_count, pw_count)], sems.at[band]
        )
        for band in range(out_hbm.shape[0] // pw_count)
    ]
    for copy in copies:
        copy.start()
    for copy in copies:
        copy.wait()


def reorder(columns, grid_len, chunk, sticks, side):
    count = columns.shape[1]
    shape = (chunk, chunk)
    to, rows = iota(shape, 1), sticks // side
    index, rest = lax.div(to, chunk // side), lax.rem(to, chunk // side)
    source = lax.div(rest, rows) * sticks + index * rows + lax.rem(rest, rows)
    order = (iota(shape, 0) == source).astype(jnp.bfloat16)
    shape = (8, count)
    columns = jnp.broadcast_to(columns, shape)
    halves = jnp.where(iota(shape, 0) == 0, cut(columns, grid_len), wrap(columns, grid_len))
    halves = halves.astype(jnp.float32).astype(jnp.bfloat16)
    ordered = [
        dot(halves[:, first : first + chunk], order) for first in range(0, count, chunk)
    ]
    ordered = jnp.concatenate(ordered, 1).astype(jnp.int32)
    return ordered[:1] * grid_len + ordered[1:2]


def table_kernel(grid_len, chunk, sticks, side, column_hbm, left_ref, right_ref, column_ref, sem):
    copy = pltpu.make_async_copy(column_hbm, column_ref, sem)
    copy.start()
    copy.wait()
    count = column_ref.shape[1]
    half = grid_len // 2
    columns = column_ref[...]
    if side > 1:
        columns = reorder(columns, grid_len, chunk, sticks, side)
    turns = iota((half, count), 0) * cut(columns, grid_len)
    left_ref[0] = cosine(turns, grid_len).astype(jnp.bfloat16)
    left_ref[1] = sine(turns, grid_len).astype(jnp.bfloat16)
    tall = jnp.transpose(jnp.broadcast_to(columns, (half, count)))
    sign = (1 - 2 * (cut(tall, grid_len) & 1)).astype(jnp.float32)
    tall = wrap(tall, grid_len)
    freq = iota((count, half), 1)
    values = cosine(tall * freq, grid_len)
    right_ref[:, :half] = values.astype(jnp.bfloat16)
    right_ref[:, grid_len : grid_len + half] = (sign * values).astype(jnp.bfloat16)
    turns = jnp.where(freq == 0, tall * half, tall * freq + (grid_len - grid_len // 4))
    values = cosine(turns, grid_len)
    right_ref[:, half:grid_len] = values.astype(jnp.bfloat16)
    right_ref[:, grid_len + half :] = (sign * values).astype(jnp.bfloat16)


def plane_kernel(
    bands,
    own_planes,
    norm_factor,
    sticks,
    message_ref,
    left_ref,
    right_ref,
    out_ref,
    value_ref,
    held_ref,
    sem,
):
    rows, _, count = value_ref.shape
    chunk = min(out_ref.shape[1], count)
    chunks = count // chunk
    grid_len = out_ref.shape[1]
    half = grid_len // 2
    message_rows, lanes = message_ref.shape[1:]
    side = sticks // message_rows
    spots = 2 * bands
    height = math.gcd(half, P_BLOCK)
    blocks = half // height
    group = math.gcd(bands, BAND_GROUP)
    shape = (side * rows + bands, lanes)
    select = (iota(shape, 0) == iota(shape, 1)).astype(jnp.bfloat16)

    def turn(index):
        pieces = chunk // sticks
        message = message_ref[pl.ds(index * pieces, pieces)]
        return dot_last(select, message.reshape(pieces * message_rows, lanes))

    def occupations(picked):
        return jnp.max(picked[side * rows :], 1, keepdims=True)

    def keep(index, picked, scale):
        width = chunk // side
        for row in range(rows):
            for place in range(side):
                piece = picked[place * rows + row : place * rows + row + 1]
                piece = piece * scale[row % bands : row % bands + 1]
                value_ref[row, :, pl.ds(index * chunk + place * width, width)] = (
                    jnp.broadcast_to(piece, (PACK, width)).astype(jnp.bfloat16)
                )

    picked = turn(0)
    found = occupations(picked)
    for index in range(1, chunks):
        found = jnp.maximum(found, occupations(turn(index)))
    peak = jnp.max(found, 0, keepdims=True)
    scale = jnp.where(found == peak, 1.0, jnp.sqrt(found / jnp.maximum(peak, 1.0)))
    keep(0, picked, scale)
    for index in range(1, chunks):
        keep(index, turn(index), scale)
    factor = peak * norm_factor

    def stick_sums(index, plane, block, first_band):
        lane = pl.ds(index * chunk, chunk)
        row = pl.ds(block * height, height)
        cos_table = left_ref[0, row, lane].reshape(height // PACK, PACK, chunk)
        sin_table = left_ref[1, row, lane].reshape(height // PACK, PACK, chunk)
        parts = []
        for band in range(group):
            at = plane * spots + first_band + band
            real, imag = value_ref[at, :, lane][None], value_ref[at + bands, :, lane][None]
            parts.append((cos_table * real - sin_table * imag).reshape(height, chunk))
            parts.append((sin_table * real + cos_table * imag).reshape(height, chunk))
        return dot(jnp.concatenate(parts, 0), right_ref[pl.ds(index * chunk, chunk), :])

    def group_sums(step):
        first_band, block = step % groups * group, step // groups
        found = []
        for plane in range(own_planes):
            if chunks == 1:
                found.append(stick_sums(0, plane, block, first_band))
            else:
                found.append(
                    lax.fori_loop(
                        0,
                        chunks,
                        lambda at, so_far: so_far + stick_sums(at, plane, block, first_band),
                        jnp.zeros((2 * group * height, 2 * grid_len), jnp.float32),
                    )
                )
        return found

    def add_squares(found, sums):
        result = []
        for place, (with_cos, with_sin, mixed) in enumerate(sums):
            plane, left = place // 2, place % 2 * grid_len
            for band in range(group):
                top = 2 * band * height
                a = found[plane][top : top + height, left : left + half]
                d = found[plane][top : top + height, left + half : left + grid_len]
                top += height
                c = found[plane][top : top + height, left : left + half]
                b = found[plane][top : top + height, left + half : left + grid_len]
                with_cos += a * a + c * c
                with_sin += b * b + d * d
                mixed += c * d - a * b
            result.append((with_cos, with_sin, mixed))
        return result

    def copy_out(place, block):
        where = (place // 2, pl.ds(place % 2 * half + block * height, height))
        return pltpu.make_async_copy(
            held_ref.at[where], out_ref.at[where], sem.at[place * blocks + block]
        )

    def finish(block, sums):
        lane = iota((height, half), 1)
        for place, (with_cos, with_sin, mixed) in enumerate(sums):
            both, mixed = with_cos + with_sin, mixed + mixed
            ahead = jnp.where(lane == 0, with_cos, both + mixed)
            back = jnp.where(lane == 0, with_sin, both - mixed)
            row = pl.ds(place % 2 * half + block * height, height)
            held_ref[place // 2, row, :half] = ahead * factor
            held_ref[place // 2, row, half:] = jnp.take_along_axis(
                back * factor, jnp.where(lane == 0, 0, half - lane), axis=1
            )
            copy_out(place, block).start()

    zero = jnp.zeros((height, half), jnp.float32)
    empty = [(zero, zero, zero)] * (2 * own_planes)
    groups = bands // group
    if blocks * groups > 32:

        def one_block(block, carry):
            def one_group(index, sums):
                step = block * groups + index
                return add_squares(group_sums(step), sums)

            finish(block, lax.fori_loop(0, groups, one_group, empty))
            return carry

        lax.fori_loop(0, blocks, one_block, 0)
    else:
        sums, ahead = empty, group_sums(0)
        for step in range(blocks * groups):
            found = ahead
            if step + 1 < blocks * groups:
                ahead = group_sums(step + 1)
            sums = add_squares(found, sums)
            if (step + 1) % groups == 0:
                finish(step // groups, sums)
                sums = empty
    for place in range(2 * own_planes):
        for block in range(blocks):
            copy_out(place, block).wait()


def shards(coeffs, rotation_matrix, stick_length, stick_column, plane_index, occupation):
    band_count = lax.axis_size("band")
    pw_count = lax.axis_size("pw")
    devices = band_count * pw_count
    in_count, sticks, grid_len = coeffs.shape[1:]
    bands = rotation_matrix.shape[2]
    stick_count = stick_column.shape[0]
    own_planes = plane_index.shape[0] // pw_count
    spots = 2 * bands
    rows = own_planes * spots
    lanes = -(-(rows + bands) // LANES) * LANES
    side = lane_groups(sticks, rows, bands, lanes)
    message_rows = sticks // side
    vmem = pl.BlockSpec(memory_space=pltpu.VMEM)
    hbm = pl.BlockSpec(memory_space=pltpu.HBM)
    table_bytes = 8 * grid_len * stick_count
    message_bytes = 2 * stick_count * lanes

    messages = pl.pallas_call(
        stick_kernel,
        out_shape=jax.ShapeDtypeStruct((devices, message_rows, lanes), jnp.bfloat16),
        in_specs=[hbm] * 5,
        out_specs=hbm,
        scratch_shapes=[
            pltpu.SMEM(stick_length.shape, jnp.int32),
            pltpu.SMEM(plane_index.shape, jnp.int32),
            pltpu.SMEM(occupation.shape, jnp.int32),
            pltpu.VMEM((2, bands, in_count), jnp.bfloat16),
            pltpu.VMEM((2 * in_count * sticks, grid_len), jnp.bfloat16),
            pltpu.VMEM((pw_count, message_rows, lanes), jnp.bfloat16),
            pltpu.SemaphoreType.DMA((max(4 + COEFF_COPIES, band_count),)),
        ],
        compiler_params=room(2 * message_bytes),
        name="stick_values",
    )(
        *(
            pltpu.with_memory_space_constraint(array, pltpu.HBM)
            for array in (
                stick_length,
                plane_index,
                occupation,
                jnp.swapaxes(rotation_matrix, 1, 2),
                coeffs.reshape(2 * in_count * sticks, grid_len),
            )
        )
    )
    arrived = lax.all_to_all(messages, ("band", "pw"), split_axis=0, concat_axis=0, tiled=True)
    left, right = pl.pallas_call(
        functools.partial(table_kernel, grid_len, min(grid_len, stick_count), sticks, side),
        out_shape=(
            jax.ShapeDtypeStruct((2, grid_len // 2, stick_count), jnp.bfloat16),
            jax.ShapeDtypeStruct((stick_count, 2 * grid_len), jnp.bfloat16),
        ),
        in_specs=[hbm],
        out_specs=(vmem, vmem),
        scratch_shapes=[pltpu.VMEM((1, stick_count), jnp.int32), pltpu.SemaphoreType.DMA],
        compiler_params=room(table_bytes),
        cost_estimate=pl.CostEstimate(
            flops=80 * grid_len * stick_count,
            bytes_accessed=12 * grid_len * stick_count,
            transcendentals=0,
        ),
        name="stick_tables",
    )(pltpu.with_memory_space_constraint(stick_column.reshape(1, stick_count), pltpu.HBM))
    norm_factor = 1.0 / float(bands * stick_count * grid_len)
    blocks = 2 * own_planes * (grid_len // 2 // math.gcd(grid_len // 2, P_BLOCK))
    return pl.pallas_call(
        functools.partial(plane_kernel, bands, own_planes, norm_factor, sticks),
        out_shape=jax.ShapeDtypeStruct((own_planes, grid_len, grid_len), jnp.float32),
        in_specs=[vmem] * 3,
        out_specs=hbm,
        scratch_shapes=[
            pltpu.VMEM((rows, PACK, stick_count), jnp.bfloat16),
            pltpu.VMEM((own_planes, grid_len, grid_len), jnp.float32),
            pltpu.SemaphoreType.DMA((blocks,)),
        ],
        compiler_params=room(table_bytes, message_bytes),
        name="plane_density",
    )(arrived, left, right)


def solution(mesh):
    return jax.shard_map(
        shards,
        mesh=mesh,
        in_specs=(P(None, None, ("band", "pw"), None), P(), P(), P(), P(), P("band")),
        out_specs=P("pw", None, None),
        check_vma=False,
    )
```

```python
import functools
import math

import jax
import jax.numpy as jnp
from jax import lax
from jax.experimental import pallas as pl
from jax.experimental.pallas import tpu as pltpu
from jax.sharding import PartitionSpec as P

LANES = 128
PACK = 16
P_BLOCK = 32
BAND_GROUP = 8
GROUP_LANES = 256
COEFF_COPIES = 4
MIB = 1024 * 1024


def wrap(value, period):
    if period & (period - 1) == 0:
        return value & (period - 1)
    return lax.rem(value, period)


def cut(value, size):
    if size & (size - 1) == 0:
        return value >> (size.bit_length() - 1)
    return lax.div(value, size)


def cosine(index, period):
    fold = jnp.abs(wrap(index, period) - period // 2) - period // 4
    angle = fold.astype(jnp.float32) * (2.0 * math.pi / period)
    square = angle * angle
    series = -2.39e-08
    for factor in (2.7526e-06, -1.984090e-04, 8.3333315e-03, -1.666666664e-01, 1.0):
        series = series * square + factor
    return angle * series


def sine(index, period):
    return cosine(index + (period - period // 4), period)


def iota(shape, dim):
    return lax.broadcasted_iota(jnp.int32, shape, dim)


def dot_last(left, right):
    return lax.dot_general(
        left, right, (((1,), (1,)), ((), ())), preferred_element_type=jnp.float32
    )


def dot(left, right):
    return jnp.dot(left, right, preferred_element_type=jnp.float32)


def loop(count, body, carry):
    if count > 16:
        return lax.fori_loop(0, count, body, carry)
    for index in range(count):
        carry = body(index, carry)
    return carry


def room(*sizes):
    return pltpu.CompilerParams(vmem_limit_bytes=min(56 * MIB, 16 * MIB + 2 * sum(sizes)))


def lane_groups(sticks, spots, bands, lanes):
    groups = 1
    while 2 * groups * spots + bands <= lanes and sticks % (2 * groups) == 0 and sticks > 4 * groups:
        groups *= 2
    return groups


def spread(scalars, index, shape):
    result = jnp.full(shape, scalars[0])
    for place, scalar in enumerate(scalars[1:], 1):
        result = jnp.where(index == place, scalar, result)
    return result


def stick_kernel(
    length_hbm,
    plane_hbm,
    occupation_hbm,
    rotation_hbm,
    coeff_hbm,
    out_hbm,
    length_ref,
    plane_ref,
    occupation_ref,
    rotation_ref,
    coeff_ref,
    message_ref,
    sems,
):
    piece = coeff_ref.shape[0] // COEFF_COPIES
    pieces = [pl.ds(first * piece, piece) for first in range(COEFF_COPIES)]
    copies = [
        pltpu.make_async_copy(source, target, sems.at[index])
        for index, (source, target) in enumerate(
            (
                (rotation_hbm, rotation_ref),
                (plane_hbm, plane_ref),
                (length_hbm, length_ref),
                (occupation_hbm, occupation_ref),
                *((coeff_hbm.at[rows], coeff_ref.at[rows]) for rows in pieces),
            )
        )
    ]
    for copy in copies:
        copy.start()
    out_count, in_count = rotation_ref.shape[1:]
    grid_len = coeff_ref.shape[1]
    sticks = coeff_ref.shape[0] // (2 * in_count)
    plane_count = plane_ref.shape[0]
    pw_count = lax.axis_size("pw")
    own_planes = plane_count // pw_count
    own_bands = occupation_ref.shape[0]
    row_count = 2 * out_count * sticks
    lanes = message_ref.shape[2]
    band_index = lax.axis_index("band")
    first_stick = (band_index * pw_count + lax.axis_index("pw")) * sticks

    group_lanes = GROUP_LANES // (own_planes * 2 * out_count) * (own_planes * 2 * out_count)
    spots = own_planes * 2 * out_count
    side = lane_groups(sticks, spots, out_count, lanes)
    group_pw = group_lanes // spots

    wide = in_count * sticks
    widen = (cut(iota((in_count, wide), 1), sticks) == iota((in_count, wide), 0)).astype(
        jnp.bfloat16
    )
    same = wrap(iota((sticks, wide), 1), sticks) == iota((sticks, wide), 0)
    copies[0].wait()
    parts = [dot(rotation_ref[part], widen) for part in range(2)]
    rows = {}
    for band in range(out_count):
        real, imag = (
            jnp.where(same, jnp.broadcast_to(part[band : band + 1], (sticks, wide)), 0.0)
            for part in parts
        )
        rows[0, band] = jnp.concatenate([real, -imag], 1)
        rows[1, band] = jnp.concatenate([imag, real], 1)
    rotation = jnp.concatenate([rows[key] for key in sorted(rows)], 0).astype(jnp.bfloat16)

    for copy in copies[1:4]:
        copy.wait()
    lengths = [length_ref[first_stick + place] for place in range(sticks)]
    row_lengths = spread(lengths, iota((sticks, grid_len), 0), (sticks, grid_len))
    live = iota((sticks, grid_len), 1) < row_lengths
    shape = (sticks, lanes)
    occupied = jnp.zeros(shape, jnp.int32)
    for own_band in range(own_bands):
        lane = side * spots + band_index * own_bands + own_band
        occupied = jnp.where(iota(shape, 1) == lane, occupation_ref[own_band], occupied)
    occupied = occupied.astype(jnp.float32)

    shape = (sticks, group_lanes)
    lane = iota(shape, 1)
    lane_plane = lax.div(lane, 2 * out_count)
    real_lane = lax.rem(lane, 2 * out_count) < out_count
    lane_band = lax.rem(lane, out_count)
    half_lengths = spread(lengths, iota(shape, 0), shape) >> 1

    def forms(first_pw):
        kinds = group_pw * own_planes
        planes = [plane_ref[first_pw * own_planes + place] for place in range(kinds)]
        kind = iota((2 * kinds, grid_len), 0)
        planes_down = spread(planes, lax.rem(kind, kinds), kind.shape)
        quarter = jnp.where(kind < kinds, 0, grid_len - grid_len // 4)
        waves = cosine(iota(kind.shape, 1) * planes_down + quarter, grid_len)
        place = iota((2 * kinds, 2 * group_lanes), 1)
        wanted = lax.div(lax.rem(place, group_lanes), 2 * out_count)
        wanted = jnp.where(place < group_lanes, wanted, wanted + kinds)
        widen = (iota(place.shape, 0) == wanted).astype(jnp.bfloat16)
        table = lax.dot_general(
            waves.astype(jnp.bfloat16),
            widen,
            (((0,), (0,)), ((), ())),
            preferred_element_type=jnp.float32,
        )
        lane_planes = spread(planes, lane_plane, shape)
        shift = half_lengths * lane_planes
        return table.astype(jnp.bfloat16), cosine(shift, grid_len), sine(shift, grid_len)

    def pick(sums, part):
        chosen = jnp.zeros(shape, jnp.float32)
        for band in range(out_count):
            top = (part * out_count + band) * sticks
            chosen = jnp.where(lane_band == band, sums[top : top + sticks], chosen)
        return chosen

    def send(first_pw, rotated, form):
        table, phase_cos, phase_sin = form
        sums = dot(rotated, table)
        with_cos, with_sin = sums[:, :group_lanes], sums[:, group_lanes:]
        real = pick(with_cos, 0) - pick(with_sin, 1)
        imag = pick(with_sin, 0) + pick(with_cos, 1)
        values = jnp.where(
            real_lane, real * phase_cos + imag * phase_sin, imag * phase_cos - real * phase_sin
        )
        for place in range(group_pw):
            first = place * spots
            tile = first // lanes * lanes
            part = values[:, tile : tile + lanes]
            message = occupied
            for index in reversed(range(side)):
                shift = (index * spots - (first - tile)) % lanes
                piece = pltpu.roll(part, shift, 1) if shift else part
                if index:
                    piece = pltpu.roll(piece, sticks - index * (sticks // side), 0)
                message = jnp.where(
                    iota((sticks, lanes), 1) < (index + 1) * spots, piece, message
                )
            message_ref[first_pw + place] = message[: sticks // side].astype(message_ref.dtype)

    if group_pw == pw_count:
        form = forms(0)
    for copy in copies[4:]:
        copy.wait()
    rotated = dot(rotation, coeff_ref[...])
    rotated = rotated.reshape(row_count // sticks, sticks, grid_len)
    rotated = jnp.where(live[None], rotated, 0.0).reshape(row_count, grid_len)
    rotated = rotated.astype(jnp.bfloat16)
    if group_pw == pw_count:
        send(0, rotated, form)
    else:

        def one_group(index, carry):
            send(index * group_pw, rotated, forms(index * group_pw))
            return carry

        lax.fori_loop(0, pw_count // group_pw, one_group, 0)
    copies = [
        pltpu.make_async_copy(
            message_ref, out_hbm.at[pl.ds(band * pw_count, pw_count)], sems.at[band]
        )
        for band in range(out_hbm.shape[0] // pw_count)
    ]
    for copy in copies:
        copy.start()
    for copy in copies:
        copy.wait()


def reorder(columns, grid_len, chunk, sticks, side):
    count = columns.shape[1]
    shape = (chunk, chunk)
    to, rows = iota(shape, 1), sticks // side
    index, rest = lax.div(to, chunk // side), lax.rem(to, chunk // side)
    source = lax.div(rest, rows) * sticks + index * rows + lax.rem(rest, rows)
    order = (iota(shape, 0) == source).astype(jnp.bfloat16)
    shape = (8, count)
    columns = jnp.broadcast_to(columns, shape)
    halves = jnp.where(iota(shape, 0) == 0, cut(columns, grid_len), wrap(columns, grid_len))
    halves = halves.astype(jnp.float32).astype(jnp.bfloat16)
    ordered = [
        dot(halves[:, first : first + chunk], order) for first in range(0, count, chunk)
    ]
    ordered = jnp.concatenate(ordered, 1).astype(jnp.int32)
    return ordered[:1] * grid_len + ordered[1:2]


def table_kernel(grid_len, chunk, sticks, side, column_hbm, left_ref, right_ref, column_ref, sem):
    copy = pltpu.make_async_copy(column_hbm, column_ref, sem)
    copy.start()
    copy.wait()
    count = column_ref.shape[1]
    half = grid_len // 2
    columns = column_ref[...]
    if side > 1:
        columns = reorder(columns, grid_len, chunk, sticks, side)
    turns = iota((half, count), 0) * cut(columns, grid_len)
    left_ref[0] = cosine(turns, grid_len).astype(jnp.bfloat16)
    left_ref[1] = sine(turns, grid_len).astype(jnp.bfloat16)
    tall = jnp.transpose(jnp.broadcast_to(columns, (half, count)))
    sign = (1 - 2 * (cut(tall, grid_len) & 1)).astype(jnp.float32)
    tall = wrap(tall, grid_len)
    freq = iota((count, half), 1)
    values = cosine(tall * freq, grid_len)
    right_ref[:, :half] = values.astype(jnp.bfloat16)
    right_ref[:, grid_len : grid_len + half] = (sign * values).astype(jnp.bfloat16)
    turns = jnp.where(freq == 0, tall * half, tall * freq + (grid_len - grid_len // 4))
    values = cosine(turns, grid_len)
    right_ref[:, half:grid_len] = values.astype(jnp.bfloat16)
    right_ref[:, grid_len + half :] = (sign * values).astype(jnp.bfloat16)


def plane_kernel(
    bands,
    own_planes,
    norm_factor,
    sticks,
    message_ref,
    left_ref,
    right_ref,
    out_ref,
    value_ref,
    held_ref,
    sem,
):
    rows, _, count = value_ref.shape
    chunk = min(out_ref.shape[1], count)
    chunks = count // chunk
    grid_len = out_ref.shape[1]
    half = grid_len // 2
    message_rows, lanes = message_ref.shape[1:]
    side = sticks // message_rows
    spots = 2 * bands
    height = math.gcd(half, P_BLOCK)
    blocks = half // height
    group = math.gcd(bands, BAND_GROUP)
    shape = (side * rows + bands, lanes)
    select = (iota(shape, 0) == iota(shape, 1)).astype(jnp.bfloat16)

    def turn(index):
        pieces = chunk // sticks
        message = message_ref[pl.ds(index * pieces, pieces)]
        return dot_last(select, message.reshape(pieces * message_rows, lanes))

    def occupations(picked):
        return jnp.max(picked[side * rows :], 1, keepdims=True)

    def keep(index, picked, scale):
        width = chunk // side
        for row in range(rows):
            for place in range(side):
                piece = picked[place * rows + row : place * rows + row + 1]
                piece = piece * scale[row % bands : row % bands + 1]
                value_ref[row, :, pl.ds(index * chunk + place * width, width)] = (
                    jnp.broadcast_to(piece, (PACK, width)).astype(jnp.bfloat16)
                )

    picked = turn(0)
    found = occupations(picked)
    for index in range(1, chunks):
        found = jnp.maximum(found, occupations(turn(index)))
    peak = jnp.max(found, 0, keepdims=True)
    scale = jnp.where(found == peak, 1.0, jnp.sqrt(found / jnp.maximum(peak, 1.0)))
    keep(0, picked, scale)
    for index in range(1, chunks):
        keep(index, turn(index), scale)
    factor = peak * norm_factor

    def stick_sums(index, plane, block, first_band):
        lane = pl.ds(index * chunk, chunk)
        row = pl.ds(block * height, height)
        cos_table = left_ref[0, row, lane].reshape(height // PACK, PACK, chunk)
        sin_table = left_ref[1, row, lane].reshape(height // PACK, PACK, chunk)
        parts = []
        for band in range(group):
            at = plane * spots + first_band + band
            real, imag = value_ref[at, :, lane][None], value_ref[at + bands, :, lane][None]
            parts.append((cos_table * real - sin_table * imag).reshape(height, chunk))
            parts.append((sin_table * real + cos_table * imag).reshape(height, chunk))
        return dot(jnp.concatenate(parts, 0), right_ref[pl.ds(index * chunk, chunk), :])

    def group_sums(step):
        first_band, block = step % groups * group, step // groups
        found = []
        for plane in range(own_planes):
            if chunks == 1:
                found.append(stick_sums(0, plane, block, first_band))
            else:
                found.append(
                    lax.fori_loop(
                        0,
                        chunks,
                        lambda at, so_far: so_far + stick_sums(at, plane, block, first_band),
                        jnp.zeros((2 * group * height, 2 * grid_len), jnp.float32),
                    )
                )
        return found

    def add_squares(found, sums):
        result = []
        for place, (with_cos, with_sin, mixed) in enumerate(sums):
            plane, left = place // 2, place % 2 * grid_len
            for band in range(group):
                top = 2 * band * height
                a = found[plane][top : top + height, left : left + half]
                d = found[plane][top : top + height, left + half : left + grid_len]
                top += height
                c = found[plane][top : top + height, left : left + half]
                b = found[plane][top : top + height, left + half : left + grid_len]
                with_cos += a * a + c * c
                with_sin += b * b + d * d
                mixed += c * d - a * b
            result.append((with_cos, with_sin, mixed))
        return result

    def copy_out(place, block):
        where = (place // 2, pl.ds(place % 2 * half + block * height, height))
        return pltpu.make_async_copy(
            held_ref.at[where], out_ref.at[where], sem.at[place * blocks + block]
        )

    def finish(block, sums):
        lane = iota((height, half), 1)
        for place, (with_cos, with_sin, mixed) in enumerate(sums):
            both, mixed = with_cos + with_sin, mixed + mixed
            ahead = jnp.where(lane == 0, with_cos, both + mixed)
            back = jnp.where(lane == 0, with_sin, both - mixed)
            row = pl.ds(place % 2 * half + block * height, height)
            held_ref[place // 2, row, :half] = ahead * factor
            held_ref[place // 2, row, half:] = jnp.take_along_axis(
                back * factor, jnp.where(lane == 0, 0, half - lane), axis=1
            )
            copy_out(place, block).start()

    zero = jnp.zeros((height, half), jnp.float32)
    empty = [(zero, zero, zero)] * (2 * own_planes)
    groups = bands // group
    if blocks * groups > 32:

        def one_block(block, carry):
            def one_group(index, sums):
                step = block * groups + index
                return add_squares(group_sums(step), sums)

            finish(block, lax.fori_loop(0, groups, one_group, empty))
            return carry

        lax.fori_loop(0, blocks, one_block, 0)
    else:
        sums, ahead = empty, group_sums(0)
        for step in range(blocks * groups):
            found = ahead
            if step + 1 < blocks * groups:
                ahead = group_sums(step + 1)
            sums = add_squares(found, sums)
            if (step + 1) % groups == 0:
                finish(step // groups, sums)
                sums = empty
    for place in range(2 * own_planes):
        for block in range(blocks):
            copy_out(place, block).wait()


def shards(coeffs, rotation_matrix, stick_length, stick_column, plane_index, occupation):
    band_count = lax.axis_size("band")
    pw_count = lax.axis_size("pw")
    devices = band_count * pw_count
    in_count, sticks, grid_len = coeffs.shape[1:]
    bands = rotation_matrix.shape[2]
    stick_count = stick_column.shape[0]
    own_planes = plane_index.shape[0] // pw_count
    spots = 2 * bands
    rows = own_planes * spots
    lanes = -(-(rows + bands) // LANES) * LANES
    side = lane_groups(sticks, rows, bands, lanes)
    message_rows = sticks // side
    vmem = pl.BlockSpec(memory_space=pltpu.VMEM)
    hbm = pl.BlockSpec(memory_space=pltpu.HBM)
    table_bytes = 8 * grid_len * stick_count
    message_bytes = 2 * stick_count * lanes

    messages = pl.pallas_call(
        stick_kernel,
        out_shape=jax.ShapeDtypeStruct((devices, message_rows, lanes), jnp.bfloat16),
        in_specs=[hbm] * 5,
        out_specs=hbm,
        scratch_shapes=[
            pltpu.SMEM(stick_length.shape, jnp.int32),
            pltpu.SMEM(plane_index.shape, jnp.int32),
            pltpu.SMEM(occupation.shape, jnp.int32),
            pltpu.VMEM((2, bands, in_count), jnp.bfloat16),
            pltpu.VMEM((2 * in_count * sticks, grid_len), jnp.bfloat16),
            pltpu.VMEM((pw_count, message_rows, lanes), jnp.bfloat16),
            pltpu.SemaphoreType.DMA((max(4 + COEFF_COPIES, band_count),)),
        ],
        compiler_params=room(2 * message_bytes),
        name="stick_values",
    )(
        *(
            pltpu.with_memory_space_constraint(array, pltpu.HBM)
            for array in (
                stick_length,
                plane_index,
                occupation,
                jnp.swapaxes(rotation_matrix, 1, 2),
                coeffs.reshape(2 * in_count * sticks, grid_len),
            )
        )
    )
    arrived = lax.all_to_all(messages, ("band", "pw"), split_axis=0, concat_axis=0, tiled=True)
    left, right = pl.pallas_call(
        functools.partial(table_kernel, grid_len, min(grid_len, stick_count), sticks, side),
        out_shape=(
            jax.ShapeDtypeStruct((2, grid_len // 2, stick_count), jnp.bfloat16),
            jax.ShapeDtypeStruct((stick_count, 2 * grid_len), jnp.bfloat16),
        ),
        in_specs=[hbm],
        out_specs=(vmem, vmem),
        scratch_shapes=[pltpu.VMEM((1, stick_count), jnp.int32), pltpu.SemaphoreType.DMA],
        compiler_params=room(table_bytes),
        cost_estimate=pl.CostEstimate(
            flops=80 * grid_len * stick_count,
            bytes_accessed=12 * grid_len * stick_count,
            transcendentals=0,
        ),
        name="stick_tables",
    )(pltpu.with_memory_space_constraint(stick_column.reshape(1, stick_count), pltpu.HBM))
    norm_factor = 1.0 / float(bands * stick_count * grid_len)
    blocks = 2 * own_planes * (grid_len // 2 // math.gcd(grid_len // 2, P_BLOCK))
    return pl.pallas_call(
        functools.partial(plane_kernel, bands, own_planes, norm_factor, sticks),
        out_shape=jax.ShapeDtypeStruct((own_planes, grid_len, grid_len), jnp.float32),
        in_specs=[vmem] * 3,
        out_specs=hbm,
        scratch_shapes=[
            pltpu.VMEM((rows, PACK, stick_count), jnp.bfloat16),
            pltpu.VMEM((own_planes, grid_len, grid_len), jnp.float32),
            pltpu.SemaphoreType.DMA((blocks,)),
        ],
        compiler_params=room(table_bytes, message_bytes),
        name="plane_density",
    )(arrived, left, right)


def solution(mesh):
    return jax.shard_map(
        shards,
        mesh=mesh,
        in_specs=(P(None, None, ("band", "pw"), None), P(), P(), P(), P(), P("band")),
        out_specs=P("pw", None, None),
        check_vma=False,
    )
```

```python
import functools
import math

import jax
import jax.numpy as jnp
from jax import lax
from jax.experimental import pallas as pl
from jax.experimental.pallas import tpu as pltpu
from jax.sharding import PartitionSpec as P

LANES = 128
PACK = 16
P_BLOCK = 64
BAND_GROUP = 8
GROUP_LANES = 256
COEFF_COPIES = 4
MIB = 1024 * 1024


def wrap(value, period):
    if period & (period - 1) == 0:
        return value & (period - 1)
    return lax.rem(value, period)


def cut(value, size):
    if size & (size - 1) == 0:
        return value >> (size.bit_length() - 1)
    return lax.div(value, size)


def cosine(index, period):
    fold = jnp.abs(wrap(index, period) - period // 2) - period // 4
    angle = fold.astype(jnp.float32) * (2.0 * math.pi / period)
    square = angle * angle
    series = -2.39e-08
    for factor in (2.7526e-06, -1.984090e-04, 8.3333315e-03, -1.666666664e-01, 1.0):
        series = series * square + factor
    return angle * series


def sine(index, period):
    return cosine(index + (period - period // 4), period)


def iota(shape, dim):
    return lax.broadcasted_iota(jnp.int32, shape, dim)


def dot_last(left, right):
    return lax.dot_general(
        left, right, (((1,), (1,)), ((), ())), preferred_element_type=jnp.float32
    )


def dot(left, right):
    return jnp.dot(left, right, preferred_element_type=jnp.float32)


def loop(count, body, carry):
    if count > 16:
        return lax.fori_loop(0, count, body, carry)
    for index in range(count):
        carry = body(index, carry)
    return carry


def room(*sizes):
    return pltpu.CompilerParams(vmem_limit_bytes=min(56 * MIB, 16 * MIB + 2 * sum(sizes)))


def row_block(grid_len, stick_count):
    return math.gcd(grid_len // 2, P_BLOCK if stick_count <= grid_len else P_BLOCK // 2)


def lane_groups(sticks, spots, bands, lanes):
    groups = 1
    while 2 * groups * spots + bands <= lanes and sticks % (2 * groups) == 0 and sticks > 4 * groups:
        groups *= 2
    return groups


def spread(scalars, index, shape):
    result = jnp.full(shape, scalars[0])
    for place, scalar in enumerate(scalars[1:], 1):
        result = jnp.where(index == place, scalar, result)
    return result


def stick_kernel(
    length_hbm,
    plane_hbm,
    occupation_hbm,
    rotation_hbm,
    coeff_hbm,
    out_hbm,
    length_ref,
    plane_ref,
    occupation_ref,
    rotation_ref,
    coeff_ref,
    message_ref,
    sems,
):
    piece = coeff_ref.shape[0] // COEFF_COPIES
    pieces = [pl.ds(first * piece, piece) for first in range(COEFF_COPIES)]
    copies = [
        pltpu.make_async_copy(source, target, sems.at[index])
        for index, (source, target) in enumerate(
            (
                (rotation_hbm, rotation_ref),
                (plane_hbm, plane_ref),
                (length_hbm, length_ref),
                (occupation_hbm, occupation_ref),
                *((coeff_hbm.at[rows], coeff_ref.at[rows]) for rows in pieces),
            )
        )
    ]
    for copy in copies:
        copy.start()
    out_count, in_count = rotation_ref.shape[1:]
    grid_len = coeff_ref.shape[1]
    sticks = coeff_ref.shape[0] // (2 * in_count)
    plane_count = plane_ref.shape[0]
    pw_count = lax.axis_size("pw")
    own_planes = plane_count // pw_count
    own_bands = occupation_ref.shape[0]
    row_count = 2 * out_count * sticks
    lanes = message_ref.shape[2]
    band_index = lax.axis_index("band")
    first_stick = (band_index * pw_count + lax.axis_index("pw")) * sticks

    group_lanes = GROUP_LANES // (own_planes * 2 * out_count) * (own_planes * 2 * out_count)
    spots = own_planes * 2 * out_count
    side = lane_groups(sticks, spots, out_count, lanes)
    group_pw = group_lanes // spots

    wide = in_count * sticks
    widen = (cut(iota((in_count, wide), 1), sticks) == iota((in_count, wide), 0)).astype(
        jnp.bfloat16
    )
    same = wrap(iota((sticks, wide), 1), sticks) == iota((sticks, wide), 0)
    copies[0].wait()
    parts = [dot(rotation_ref[part], widen) for part in range(2)]
    rows = {}
    for band in range(out_count):
        real, imag = (
            jnp.where(same, jnp.broadcast_to(part[band : band + 1], (sticks, wide)), 0.0)
            for part in parts
        )
        rows[0, band] = jnp.concatenate([real, -imag], 1)
        rows[1, band] = jnp.concatenate([imag, real], 1)
    rotation = jnp.concatenate([rows[key] for key in sorted(rows)], 0).astype(jnp.bfloat16)

    for copy in copies[1:]:
        copy.wait()
    rotated = dot(rotation, coeff_ref[...])
    lengths = [length_ref[first_stick + place] for place in range(sticks)]
    row_lengths = spread(lengths, iota((sticks, grid_len), 0), (sticks, grid_len))
    live = iota((sticks, grid_len), 1) < row_lengths
    shape = (sticks, lanes)
    occupied = jnp.zeros(shape, jnp.int32)
    for own_band in range(own_bands):
        lane = side * spots + band_index * own_bands + own_band
        occupied = jnp.where(iota(shape, 1) == lane, occupation_ref[own_band], occupied)
    occupied = occupied.astype(jnp.float32)

    shape = (sticks, group_lanes)
    lane = iota(shape, 1)
    lane_plane = lax.div(lane, 2 * out_count)
    real_lane = lax.rem(lane, 2 * out_count) < out_count
    lane_band = lax.rem(lane, out_count)
    half_lengths = spread(lengths, iota(shape, 0), shape) >> 1

    def forms(first_pw):
        kinds = group_pw * own_planes
        planes = [plane_ref[first_pw * own_planes + place] for place in range(kinds)]
        kind = iota((2 * kinds, grid_len), 0)
        planes_down = spread(planes, lax.rem(kind, kinds), kind.shape)
        quarter = jnp.where(kind < kinds, 0, grid_len - grid_len // 4)
        waves = cosine(iota(kind.shape, 1) * planes_down + quarter, grid_len)
        place = iota((2 * kinds, 2 * group_lanes), 1)
        wanted = lax.div(lax.rem(place, group_lanes), 2 * out_count)
        wanted = jnp.where(place < group_lanes, wanted, wanted + kinds)
        widen = (iota(place.shape, 0) == wanted).astype(jnp.bfloat16)
        table = lax.dot_general(
            waves.astype(jnp.bfloat16),
            widen,
            (((0,), (0,)), ((), ())),
            preferred_element_type=jnp.float32,
        )
        lane_planes = spread(planes, lane_plane, shape)
        shift = half_lengths * lane_planes
        return table.astype(jnp.bfloat16), cosine(shift, grid_len), sine(shift, grid_len)

    def pick(sums, part):
        chosen = jnp.zeros(shape, jnp.float32)
        for band in range(out_count):
            top = (part * out_count + band) * sticks
            chosen = jnp.where(lane_band == band, sums[top : top + sticks], chosen)
        return chosen

    def send(first_pw, rotated, form):
        table, phase_cos, phase_sin = form
        sums = dot(rotated, table)
        with_cos, with_sin = sums[:, :group_lanes], sums[:, group_lanes:]
        real = pick(with_cos, 0) - pick(with_sin, 1)
        imag = pick(with_sin, 0) + pick(with_cos, 1)
        values = jnp.where(
            real_lane, real * phase_cos + imag * phase_sin, imag * phase_cos - real * phase_sin
        )
        for place in range(group_pw):
            first = place * spots
            tile = first // lanes * lanes
            part = values[:, tile : tile + lanes]
            message = occupied
            for index in reversed(range(side)):
                shift = (index * spots - (first - tile)) % lanes
                piece = pltpu.roll(part, shift, 1) if shift else part
                if index:
                    piece = pltpu.roll(piece, sticks - index * (sticks // side), 0)
                message = jnp.where(
                    iota((sticks, lanes), 1) < (index + 1) * spots, piece, message
                )
            message_ref[first_pw + place] = message[: sticks // side].astype(message_ref.dtype)

    if group_pw == pw_count:
        form = forms(0)
    rotated = rotated.reshape(row_count // sticks, sticks, grid_len)
    rotated = jnp.where(live[None], rotated, 0.0).reshape(row_count, grid_len)
    rotated = rotated.astype(jnp.bfloat16)
    if group_pw == pw_count:
        send(0, rotated, form)
    else:

        def one_group(index, carry):
            send(index * group_pw, rotated, forms(index * group_pw))
            return carry

        lax.fori_loop(0, pw_count // group_pw, one_group, 0)
    copies = [
        pltpu.make_async_copy(
            message_ref, out_hbm.at[pl.ds(band * pw_count, pw_count)], sems.at[band]
        )
        for band in range(out_hbm.shape[0] // pw_count)
    ]
    for copy in copies:
        copy.start()
    for copy in copies:
        copy.wait()


def reorder(columns, grid_len, chunk, sticks, side):
    count = columns.shape[1]
    shape = (chunk, chunk)
    to, rows = iota(shape, 1), sticks // side
    index, rest = lax.div(to, chunk // side), lax.rem(to, chunk // side)
    source = lax.div(rest, rows) * sticks + index * rows + lax.rem(rest, rows)
    order = (iota(shape, 0) == source).astype(jnp.bfloat16)
    shape = (8, count)
    columns = jnp.broadcast_to(columns, shape)
    halves = jnp.where(iota(shape, 0) == 0, cut(columns, grid_len), wrap(columns, grid_len))
    halves = halves.astype(jnp.float32).astype(jnp.bfloat16)
    ordered = [
        dot(halves[:, first : first + chunk], order) for first in range(0, count, chunk)
    ]
    ordered = jnp.concatenate(ordered, 1).astype(jnp.int32)
    return ordered[:1] * grid_len + ordered[1:2]


def table_kernel(grid_len, chunk, sticks, side, column_hbm, left_ref, right_ref, column_ref, sem):
    copy = pltpu.make_async_copy(column_hbm, column_ref, sem)
    copy.start()
    copy.wait()
    count = column_ref.shape[1]
    half = grid_len // 2
    columns = column_ref[...]
    if side > 1:
        columns = reorder(columns, grid_len, chunk, sticks, side)
    turns = iota((half, count), 0) * cut(columns, grid_len)
    left_ref[0] = cosine(turns, grid_len).astype(jnp.bfloat16)
    left_ref[1] = sine(turns, grid_len).astype(jnp.bfloat16)
    tall = jnp.transpose(jnp.broadcast_to(columns, (half, count)))
    sign = (1 - 2 * (cut(tall, grid_len) & 1)).astype(jnp.float32)
    tall = wrap(tall, grid_len)
    freq = iota((count, half), 1)
    values = cosine(tall * freq, grid_len)
    right_ref[:, :half] = values.astype(jnp.bfloat16)
    right_ref[:, grid_len : grid_len + half] = (sign * values).astype(jnp.bfloat16)
    turns = jnp.where(freq == 0, tall * half, tall * freq + (grid_len - grid_len // 4))
    values = cosine(turns, grid_len)
    right_ref[:, half:grid_len] = values.astype(jnp.bfloat16)
    right_ref[:, grid_len + half :] = (sign * values).astype(jnp.bfloat16)


def plane_kernel(
    bands,
    own_planes,
    norm_factor,
    sticks,
    message_ref,
    left_ref,
    right_ref,
    out_ref,
    value_ref,
    held_ref,
    sem,
):
    rows, _, count = value_ref.shape
    chunk = min(out_ref.shape[1], count)
    chunks = count // chunk
    grid_len = out_ref.shape[1]
    half = grid_len // 2
    message_rows, lanes = message_ref.shape[1:]
    side = sticks // message_rows
    spots = 2 * bands
    height = row_block(grid_len, count)
    blocks = half // height
    group = math.gcd(bands, BAND_GROUP)
    shape = (side * rows + bands, lanes)
    select = (iota(shape, 0) == iota(shape, 1)).astype(jnp.bfloat16)

    def turn(index):
        pieces = chunk // sticks
        message = message_ref[pl.ds(index * pieces, pieces)]
        return dot_last(select, message.reshape(pieces * message_rows, lanes))

    def occupations(picked):
        return jnp.max(picked[side * rows :], 1, keepdims=True)

    def keep(index, picked, scale):
        width = chunk // side
        for row in range(rows):
            for place in range(side):
                piece = picked[place * rows + row : place * rows + row + 1]
                piece = piece * scale[row % bands : row % bands + 1]
                value_ref[row, :, pl.ds(index * chunk + place * width, width)] = (
                    jnp.broadcast_to(piece, (PACK, width)).astype(jnp.bfloat16)
                )

    picked = turn(0)
    found = occupations(picked)
    for index in range(1, chunks):
        found = jnp.maximum(found, occupations(turn(index)))
    peak = jnp.max(found, 0, keepdims=True)
    scale = jnp.where(found == peak, 1.0, jnp.sqrt(found / jnp.maximum(peak, 1.0)))
    keep(0, picked, scale)
    for index in range(1, chunks):
        keep(index, turn(index), scale)
    factor = peak * norm_factor

    def stick_sums(index, plane, block, first_band):
        lane = pl.ds(index * chunk, chunk)
        row = pl.ds(block * height, height)
        cos_table = left_ref[0, row, lane].reshape(height // PACK, PACK, chunk)
        sin_table = left_ref[1, row, lane].reshape(height // PACK, PACK, chunk)
        parts = []
        for band in range(group):
            at = plane * spots + first_band + band
            real, imag = value_ref[at, :, lane][None], value_ref[at + bands, :, lane][None]
            parts.append((cos_table * real - sin_table * imag).reshape(height, chunk))
            parts.append((sin_table * real + cos_table * imag).reshape(height, chunk))
        return dot(jnp.concatenate(parts, 0), right_ref[pl.ds(index * chunk, chunk), :])

    def group_sums(step):
        first_band, block = step % groups * group, step // groups
        found = []
        for plane in range(own_planes):
            if chunks == 1:
                found.append(stick_sums(0, plane, block, first_band))
            else:
                found.append(
                    lax.fori_loop(
                        0,
                        chunks,
                        lambda at, so_far: so_far + stick_sums(at, plane, block, first_band),
                        jnp.zeros((2 * group * height, 2 * grid_len), jnp.float32),
                    )
                )
        return found

    def add_squares(found, sums):
        result = []
        for place, (with_cos, with_sin, mixed) in enumerate(sums):
            plane, left = place // 2, place % 2 * grid_len
            for band in range(group):
                top = 2 * band * height
                a = found[plane][top : top + height, left : left + half]
                d = found[plane][top : top + height, left + half : left + grid_len]
                top += height
                c = found[plane][top : top + height, left : left + half]
                b = found[plane][top : top + height, left + half : left + grid_len]
                with_cos += a * a + c * c
                with_sin += b * b + d * d
                mixed += c * d - a * b
            result.append((with_cos, with_sin, mixed))
        return result

    def copy_out(place, block):
        where = (place // 2, pl.ds(place % 2 * half + block * height, height))
        return pltpu.make_async_copy(
            held_ref.at[where], out_ref.at[where], sem.at[place * blocks + block]
        )

    def finish(block, sums):
        lane = iota((height, half), 1)
        for place, (with_cos, with_sin, mixed) in enumerate(sums):
            both, mixed = with_cos + with_sin, mixed + mixed
            ahead = jnp.where(lane == 0, with_cos, both + mixed)
            back = jnp.where(lane == 0, with_sin, both - mixed)
            row = pl.ds(place % 2 * half + block * height, height)
            held_ref[place // 2, row, :half] = ahead * factor
            held_ref[place // 2, row, half:] = jnp.take_along_axis(
                back * factor, jnp.where(lane == 0, 0, half - lane), axis=1
            )
            copy_out(place, block).start()

    zero = jnp.zeros((height, half), jnp.float32)
    empty = [(zero, zero, zero)] * (2 * own_planes)
    groups = bands // group
    if blocks * groups > 32:

        def one_block(block, carry):
            def one_group(index, sums):
                step = block * groups + index
                return add_squares(group_sums(step), sums)

            finish(block, lax.fori_loop(0, groups, one_group, empty))
            return carry

        lax.fori_loop(0, blocks, one_block, 0)
    else:
        sums, ahead = empty, group_sums(0)
        for step in range(blocks * groups):
            found = ahead
            if step + 1 < blocks * groups:
                ahead = group_sums(step + 1)
            sums = add_squares(found, sums)
            if (step + 1) % groups == 0:
                finish(step // groups, sums)
                sums = empty
    for place in range(2 * own_planes):
        for block in range(blocks):
            copy_out(place, block).wait()


def shards(coeffs, rotation_matrix, stick_length, stick_column, plane_index, occupation):
    band_count = lax.axis_size("band")
    pw_count = lax.axis_size("pw")
    devices = band_count * pw_count
    in_count, sticks, grid_len = coeffs.shape[1:]
    bands = rotation_matrix.shape[2]
    stick_count = stick_column.shape[0]
    own_planes = plane_index.shape[0] // pw_count
    spots = 2 * bands
    rows = own_planes * spots
    lanes = -(-(rows + bands) // LANES) * LANES
    side = lane_groups(sticks, rows, bands, lanes)
    message_rows = sticks // side
    vmem = pl.BlockSpec(memory_space=pltpu.VMEM)
    hbm = pl.BlockSpec(memory_space=pltpu.HBM)
    table_bytes = 8 * grid_len * stick_count
    message_bytes = 2 * stick_count * lanes

    messages = pl.pallas_call(
        stick_kernel,
        out_shape=jax.ShapeDtypeStruct((devices, message_rows, lanes), jnp.bfloat16),
        in_specs=[hbm] * 5,
        out_specs=hbm,
        scratch_shapes=[
            pltpu.SMEM(stick_length.shape, jnp.int32),
            pltpu.SMEM(plane_index.shape, jnp.int32),
            pltpu.SMEM(occupation.shape, jnp.int32),
            pltpu.VMEM((2, bands, in_count), jnp.bfloat16),
            pltpu.VMEM((2 * in_count * sticks, grid_len), jnp.bfloat16),
            pltpu.VMEM((pw_count, message_rows, lanes), jnp.bfloat16),
            pltpu.SemaphoreType.DMA((max(4 + COEFF_COPIES, band_count),)),
        ],
        compiler_params=room(2 * message_bytes),
        name="stick_values",
    )(
        *(
            pltpu.with_memory_space_constraint(array, pltpu.HBM)
            for array in (
                stick_length,
                plane_index,
                occupation,
                jnp.swapaxes(rotation_matrix, 1, 2),
                coeffs.reshape(2 * in_count * sticks, grid_len),
            )
        )
    )
    arrived = lax.all_to_all(messages, ("band", "pw"), split_axis=0, concat_axis=0, tiled=True)
    left, right = pl.pallas_call(
        functools.partial(table_kernel, grid_len, min(grid_len, stick_count), sticks, side),
        out_shape=(
            jax.ShapeDtypeStruct((2, grid_len // 2, stick_count), jnp.bfloat16),
            jax.ShapeDtypeStruct((stick_count, 2 * grid_len), jnp.bfloat16),
        ),
        in_specs=[hbm],
        out_specs=(vmem, vmem),
        scratch_shapes=[pltpu.VMEM((1, stick_count), jnp.int32), pltpu.SemaphoreType.DMA],
        compiler_params=room(table_bytes),
        cost_estimate=pl.CostEstimate(
            flops=80 * grid_len * stick_count,
            bytes_accessed=12 * grid_len * stick_count,
            transcendentals=0,
        ),
        name="stick_tables",
    )(pltpu.with_memory_space_constraint(stick_column.reshape(1, stick_count), pltpu.HBM))
    norm_factor = 1.0 / float(bands * stick_count * grid_len)
    blocks = 2 * own_planes * (grid_len // 2 // row_block(grid_len, stick_count))
    return pl.pallas_call(
        functools.partial(plane_kernel, bands, own_planes, norm_factor, sticks),
        out_shape=jax.ShapeDtypeStruct((own_planes, grid_len, grid_len), jnp.float32),
        in_specs=[vmem] * 3,
        out_specs=hbm,
        scratch_shapes=[
            pltpu.VMEM((rows, PACK, stick_count), jnp.bfloat16),
            pltpu.VMEM((own_planes, grid_len, grid_len), jnp.float32),
            pltpu.SemaphoreType.DMA((blocks,)),
        ],
        compiler_params=room(table_bytes, message_bytes),
        name="plane_density",
    )(arrived, left, right)


def solution(mesh):
    return jax.shard_map(
        shards,
        mesh=mesh,
        in_specs=(P(None, None, ("band", "pw"), None), P(), P(), P(), P(), P("band")),
        out_specs=P("pw", None, None),
        check_vma=False,
    )
```

```python
import functools
import math

import jax
import jax.numpy as jnp
from jax import lax
from jax.experimental import pallas as pl
from jax.experimental.pallas import tpu as pltpu
from jax.sharding import PartitionSpec as P

LANES = 128
PACK = 16
P_BLOCK = 32
BAND_GROUP = 8
GROUP_LANES = 256
COEFF_COPIES = 4
MIB = 1024 * 1024


def wrap(value, period):
    if period & (period - 1) == 0:
        return value & (period - 1)
    return lax.rem(value, period)


def cut(value, size):
    if size & (size - 1) == 0:
        return value >> (size.bit_length() - 1)
    return lax.div(value, size)


def cosine(index, period):
    fold = jnp.abs(wrap(index, period) - period // 2) - period // 4
    angle = fold.astype(jnp.float32) * (2.0 * math.pi / period)
    square = angle * angle
    series = -2.39e-08
    for factor in (2.7526e-06, -1.984090e-04, 8.3333315e-03, -1.666666664e-01, 1.0):
        series = series * square + factor
    return angle * series


def sine(index, period):
    return cosine(index + (period - period // 4), period)


def iota(shape, dim):
    return lax.broadcasted_iota(jnp.int32, shape, dim)


def dot_last(left, right):
    return lax.dot_general(
        left, right, (((1,), (1,)), ((), ())), preferred_element_type=jnp.float32
    )


def dot(left, right):
    return jnp.dot(left, right, preferred_element_type=jnp.float32)


def loop(count, body, carry):
    if count > 16:
        return lax.fori_loop(0, count, body, carry)
    for index in range(count):
        carry = body(index, carry)
    return carry


def room(*sizes):
    return pltpu.CompilerParams(vmem_limit_bytes=min(56 * MIB, 16 * MIB + 2 * sum(sizes)))


def row_block(grid_len, stick_count):
    return math.gcd(grid_len // 2, P_BLOCK if stick_count <= grid_len else P_BLOCK // 2)


def lane_groups(sticks, spots, bands, lanes):
    groups = 1
    while 2 * groups * spots + bands <= lanes and sticks % (2 * groups) == 0 and sticks > 4 * groups:
        groups *= 2
    return groups


def spread(scalars, index, shape):
    result = jnp.full(shape, scalars[0])
    for place, scalar in enumerate(scalars[1:], 1):
        result = jnp.where(index == place, scalar, result)
    return result


def stick_kernel(
    length_hbm,
    plane_hbm,
    occupation_hbm,
    rotation_hbm,
    coeff_hbm,
    out_hbm,
    length_ref,
    plane_ref,
    occupation_ref,
    rotation_ref,
    coeff_ref,
    message_ref,
    sems,
):
    piece = coeff_ref.shape[0] // COEFF_COPIES
    pieces = [pl.ds(first * piece, piece) for first in range(COEFF_COPIES)]
    copies = [
        pltpu.make_async_copy(source, target, sems.at[index])
        for index, (source, target) in enumerate(
            (
                (rotation_hbm, rotation_ref),
                (plane_hbm, plane_ref),
                (length_hbm, length_ref),
                (occupation_hbm, occupation_ref),
                *((coeff_hbm.at[rows], coeff_ref.at[rows]) for rows in pieces),
            )
        )
    ]
    for copy in copies:
        copy.start()
    out_count, in_count = rotation_ref.shape[1:]
    grid_len = coeff_ref.shape[1]
    sticks = coeff_ref.shape[0] // (2 * in_count)
    plane_count = plane_ref.shape[0]
    pw_count = lax.axis_size("pw")
    own_planes = plane_count // pw_count
    own_bands = occupation_ref.shape[0]
    row_count = 2 * out_count * sticks
    lanes = message_ref.shape[2]
    band_index = lax.axis_index("band")
    first_stick = (band_index * pw_count + lax.axis_index("pw")) * sticks

    group_lanes = GROUP_LANES // (own_planes * 2 * out_count) * (own_planes * 2 * out_count)
    spots = own_planes * 2 * out_count
    side = lane_groups(sticks, spots, out_count, lanes)
    group_pw = group_lanes // spots

    wide = in_count * sticks
    widen = (cut(iota((in_count, wide), 1), sticks) == iota((in_count, wide), 0)).astype(
        jnp.bfloat16
    )
    same = wrap(iota((sticks, wide), 1), sticks) == iota((sticks, wide), 0)
    copies[0].wait()
    parts = [dot(rotation_ref[part], widen) for part in range(2)]
    rows = {}
    for band in range(out_count):
        real, imag = (
            jnp.where(same, jnp.broadcast_to(part[band : band + 1], (sticks, wide)), 0.0)
            for part in parts
        )
        rows[0, band] = jnp.concatenate([real, -imag], 1)
        rows[1, band] = jnp.concatenate([imag, real], 1)
    rotation = jnp.concatenate([rows[key] for key in sorted(rows)], 0).astype(jnp.bfloat16)

    for copy in copies[1:]:
        copy.wait()
    rotated = dot(rotation, coeff_ref[...])
    lengths = [length_ref[first_stick + place] for place in range(sticks)]
    row_lengths = spread(lengths, iota((sticks, grid_len), 0), (sticks, grid_len))
    live = iota((sticks, grid_len), 1) < row_lengths
    shape = (sticks, lanes)
    occupied = jnp.zeros(shape, jnp.int32)
    for own_band in range(own_bands):
        lane = side * spots + band_index * own_bands + own_band
        occupied = jnp.where(iota(shape, 1) == lane, occupation_ref[own_band], occupied)
    occupied = occupied.astype(jnp.float32)

    shape = (sticks, group_lanes)
    lane = iota(shape, 1)
    lane_plane = lax.div(lane, 2 * out_count)
    real_lane = lax.rem(lane, 2 * out_count) < out_count
    lane_band = lax.rem(lane, out_count)
    half_lengths = spread(lengths, iota(shape, 0), shape) >> 1

    def forms(first_pw):
        kinds = group_pw * own_planes
        planes = [plane_ref[first_pw * own_planes + place] for place in range(kinds)]
        kind = iota((2 * kinds, grid_len), 0)
        planes_down = spread(planes, lax.rem(kind, kinds), kind.shape)
        quarter = jnp.where(kind < kinds, 0, grid_len - grid_len // 4)
        waves = cosine(iota(kind.shape, 1) * planes_down + quarter, grid_len)
        place = iota((2 * kinds, 2 * group_lanes), 1)
        wanted = lax.div(lax.rem(place, group_lanes), 2 * out_count)
        wanted = jnp.where(place < group_lanes, wanted, wanted + kinds)
        widen = (iota(place.shape, 0) == wanted).astype(jnp.bfloat16)
        table = lax.dot_general(
            waves.astype(jnp.bfloat16),
            widen,
            (((0,), (0,)), ((), ())),
            preferred_element_type=jnp.float32,
        )
        lane_planes = spread(planes, lane_plane, shape)
        shift = half_lengths * lane_planes
        return table.astype(jnp.bfloat16), cosine(shift, grid_len), sine(shift, grid_len)

    def pick(sums, part):
        chosen = jnp.zeros(shape, jnp.float32)
        for band in range(out_count):
            top = (part * out_count + band) * sticks
            chosen = jnp.where(lane_band == band, sums[top : top + sticks], chosen)
        return chosen

    def send(first_pw, rotated, form):
        table, phase_cos, phase_sin = form
        sums = dot(rotated, table)
        with_cos, with_sin = sums[:, :group_lanes], sums[:, group_lanes:]
        real = pick(with_cos, 0) - pick(with_sin, 1)
        imag = pick(with_sin, 0) + pick(with_cos, 1)
        values = jnp.where(
            real_lane, real * phase_cos + imag * phase_sin, imag * phase_cos - real * phase_sin
        )
        for place in range(group_pw):
            first = place * spots
            tile = first // lanes * lanes
            part = values[:, tile : tile + lanes]
            message = occupied
            for index in reversed(range(side)):
                shift = (index * spots - (first - tile)) % lanes
                piece = pltpu.roll(part, shift, 1) if shift else part
                if index:
                    piece = pltpu.roll(piece, sticks - index * (sticks // side), 0)
                message = jnp.where(
                    iota((sticks, lanes), 1) < (index + 1) * spots, piece, message
                )
            message_ref[pw_count - 1 - first_pw - place] = message[: sticks // side].astype(message_ref.dtype)

    if group_pw == pw_count:
        form = forms(0)
    rotated = rotated.reshape(row_count // sticks, sticks, grid_len)
    rotated = jnp.where(live[None], rotated, 0.0).reshape(row_count, grid_len)
    rotated = rotated.astype(jnp.bfloat16)
    if group_pw == pw_count:
        send(0, rotated, form)
    else:

        def one_group(index, carry):
            send(index * group_pw, rotated, forms(index * group_pw))
            return carry

        lax.fori_loop(0, pw_count // group_pw, one_group, 0)
    copies = [
        pltpu.make_async_copy(
            message_ref, out_hbm.at[pl.ds(band * pw_count, pw_count)], sems.at[band]
        )
        for band in range(out_hbm.shape[0] // pw_count)
    ]
    for copy in copies:
        copy.start()
    for copy in copies:
        copy.wait()


def reorder(columns, grid_len, chunk, sticks, side):
    count = columns.shape[1]
    shape = (chunk, chunk)
    to, rows = iota(shape, 1), sticks // side
    index, rest = lax.div(to, chunk // side), lax.rem(to, chunk // side)
    device = chunk // sticks - 1 - lax.div(rest, rows)
    source = device * sticks + index * rows + lax.rem(rest, rows)
    order = (iota(shape, 0) == source).astype(jnp.bfloat16)
    shape = (8, count)
    columns = jnp.broadcast_to(columns, shape)
    halves = jnp.where(iota(shape, 0) == 0, cut(columns, grid_len), wrap(columns, grid_len))
    halves = halves.astype(jnp.float32).astype(jnp.bfloat16)
    ordered = [
        dot(halves[:, first : first + chunk], order) for first in range(0, count, chunk)[::-1]
    ]
    ordered = jnp.concatenate(ordered, 1).astype(jnp.int32)
    return ordered[:1] * grid_len + ordered[1:2]


def table_kernel(grid_len, chunk, sticks, side, column_hbm, left_ref, right_ref, column_ref, sem):
    copy = pltpu.make_async_copy(column_hbm, column_ref, sem)
    copy.start()
    copy.wait()
    count = column_ref.shape[1]
    half = grid_len // 2
    columns = column_ref[...]
    columns = reorder(columns, grid_len, chunk, sticks, side)
    turns = iota((half, count), 0) * cut(columns, grid_len)
    left_ref[0] = cosine(turns, grid_len).astype(jnp.bfloat16)
    left_ref[1] = sine(turns, grid_len).astype(jnp.bfloat16)
    tall = jnp.transpose(jnp.broadcast_to(columns, (half, count)))
    sign = (1 - 2 * (cut(tall, grid_len) & 1)).astype(jnp.float32)
    tall = wrap(tall, grid_len)
    freq = iota((count, half), 1)
    values = cosine(tall * freq, grid_len)
    right_ref[:, :half] = values.astype(jnp.bfloat16)
    right_ref[:, grid_len : grid_len + half] = (sign * values).astype(jnp.bfloat16)
    turns = jnp.where(freq == 0, tall * half, tall * freq + (grid_len - grid_len // 4))
    values = cosine(turns, grid_len)
    right_ref[:, half:grid_len] = values.astype(jnp.bfloat16)
    right_ref[:, grid_len + half :] = (sign * values).astype(jnp.bfloat16)


def plane_kernel(
    bands,
    own_planes,
    norm_factor,
    sticks,
    message_ref,
    left_ref,
    right_ref,
    out_ref,
    value_ref,
    held_ref,
    sem,
):
    rows, _, count = value_ref.shape
    chunk = min(out_ref.shape[1], count)
    chunks = count // chunk
    grid_len = out_ref.shape[1]
    half = grid_len // 2
    message_rows, lanes = message_ref.shape[1:]
    side = sticks // message_rows
    spots = 2 * bands
    height = row_block(grid_len, count)
    blocks = half // height
    group = math.gcd(bands, BAND_GROUP)
    shape = (side * rows + bands, lanes)
    select = (iota(shape, 0) == iota(shape, 1)).astype(jnp.bfloat16)

    def turn(index):
        pieces = chunk // sticks
        message = message_ref[pl.ds(index * pieces, pieces)]
        return dot_last(select, message.reshape(pieces * message_rows, lanes))

    def occupations(picked):
        return jnp.max(picked[side * rows :], 1, keepdims=True)

    def keep(index, picked, scale):
        width = chunk // side
        for row in range(rows):
            for place in range(side):
                piece = picked[place * rows + row : place * rows + row + 1]
                piece = piece * scale[row % bands : row % bands + 1]
                value_ref[row, :, pl.ds(index * chunk + place * width, width)] = (
                    jnp.broadcast_to(piece, (PACK, width)).astype(jnp.bfloat16)
                )

    picked = turn(0)
    found = occupations(picked)
    for index in range(1, chunks):
        found = jnp.maximum(found, occupations(turn(index)))
    peak = jnp.max(found, 0, keepdims=True)
    scale = jnp.where(found == peak, 1.0, jnp.sqrt(found / jnp.maximum(peak, 1.0)))
    keep(0, picked, scale)
    for index in range(1, chunks):
        keep(index, turn(index), scale)
    factor = peak * norm_factor

    def stick_sums(index, plane, block, first_band):
        lane = pl.ds(index * chunk, chunk)
        row = pl.ds(block * height, height)
        cos_table = left_ref[0, row, lane].reshape(height // PACK, PACK, chunk)
        sin_table = left_ref[1, row, lane].reshape(height // PACK, PACK, chunk)
        parts = []
        for band in range(group):
            at = plane * spots + first_band + band
            real, imag = value_ref[at, :, lane][None], value_ref[at + bands, :, lane][None]
            parts.append((cos_table * real - sin_table * imag).reshape(height, chunk))
            parts.append((sin_table * real + cos_table * imag).reshape(height, chunk))
        return dot(jnp.concatenate(parts, 0), right_ref[pl.ds(index * chunk, chunk), :])

    def group_sums(step):
        first_band, block = step % groups * group, step // groups
        found = []
        for plane in range(own_planes):
            if chunks == 1:
                found.append(stick_sums(0, plane, block, first_band))
            else:
                found.append(
                    lax.fori_loop(
                        0,
                        chunks,
                        lambda at, so_far: so_far + stick_sums(at, plane, block, first_band),
                        jnp.zeros((2 * group * height, 2 * grid_len), jnp.float32),
                    )
                )
        return found

    def add_squares(found, sums):
        result = []
        for place, (with_cos, with_sin, mixed) in enumerate(sums):
            plane, left = place // 2, place % 2 * grid_len
            for band in range(group):
                top = 2 * band * height
                a = found[plane][top : top + height, left : left + half]
                d = found[plane][top : top + height, left + half : left + grid_len]
                top += height
                c = found[plane][top : top + height, left : left + half]
                b = found[plane][top : top + height, left + half : left + grid_len]
                with_cos += a * a + c * c
                with_sin += b * b + d * d
                mixed += c * d - a * b
            result.append((with_cos, with_sin, mixed))
        return result

    def copy_out(place, block):
        where = (place // 2, pl.ds(place % 2 * half + block * height, height))
        return pltpu.make_async_copy(
            held_ref.at[where], out_ref.at[where], sem.at[place * blocks + block]
        )

    def finish(block, sums):
        lane = iota((height, half), 1)
        for place, (with_cos, with_sin, mixed) in enumerate(sums):
            both, mixed = with_cos + with_sin, mixed + mixed
            ahead = jnp.where(lane == 0, with_cos, both + mixed)
            back = jnp.where(lane == 0, with_sin, both - mixed)
            row = pl.ds(place % 2 * half + block * height, height)
            held_ref[place // 2, row, :half] = ahead * factor
            held_ref[place // 2, row, half:] = jnp.take_along_axis(
                back * factor, jnp.where(lane == 0, 0, half - lane), axis=1
            )
            copy_out(place, block).start()

    zero = jnp.zeros((height, half), jnp.float32)
    empty = [(zero, zero, zero)] * (2 * own_planes)
    groups = bands // group
    if blocks * groups > 32:

        def one_block(block, carry):
            def one_group(index, sums):
                step = block * groups + index
                return add_squares(group_sums(step), sums)

            finish(block, lax.fori_loop(0, groups, one_group, empty))
            return carry

        lax.fori_loop(0, blocks, one_block, 0)
    else:
        sums, ahead = empty, group_sums(0)
        for step in range(blocks * groups):
            found = ahead
            if step + 1 < blocks * groups:
                ahead = group_sums(step + 1)
            sums = add_squares(found, sums)
            if (step + 1) % groups == 0:
                finish(step // groups, sums)
                sums = empty
    for place in range(2 * own_planes):
        for block in range(blocks):
            copy_out(place, block).wait()


def shards(coeffs, rotation_matrix, stick_length, stick_column, plane_index, occupation):
    band_count = lax.axis_size("band")
    pw_count = lax.axis_size("pw")
    devices = band_count * pw_count
    in_count, sticks, grid_len = coeffs.shape[1:]
    bands = rotation_matrix.shape[2]
    stick_count = stick_column.shape[0]
    own_planes = plane_index.shape[0] // pw_count
    spots = 2 * bands
    rows = own_planes * spots
    lanes = -(-(rows + bands) // LANES) * LANES
    side = lane_groups(sticks, rows, bands, lanes)
    message_rows = sticks // side
    vmem = pl.BlockSpec(memory_space=pltpu.VMEM)
    hbm = pl.BlockSpec(memory_space=pltpu.HBM)
    table_bytes = 8 * grid_len * stick_count
    message_bytes = 2 * stick_count * lanes

    messages = pl.pallas_call(
        stick_kernel,
        out_shape=jax.ShapeDtypeStruct((devices, message_rows, lanes), jnp.bfloat16),
        in_specs=[hbm] * 5,
        out_specs=hbm,
        scratch_shapes=[
            pltpu.SMEM(stick_length.shape, jnp.int32),
            pltpu.SMEM(plane_index.shape, jnp.int32),
            pltpu.SMEM(occupation.shape, jnp.int32),
            pltpu.VMEM((2, bands, in_count), jnp.bfloat16),
            pltpu.VMEM((2 * in_count * sticks, grid_len), jnp.bfloat16),
            pltpu.VMEM((pw_count, message_rows, lanes), jnp.bfloat16),
            pltpu.SemaphoreType.DMA((max(4 + COEFF_COPIES, band_count),)),
        ],
        compiler_params=room(2 * message_bytes),
        name="stick_values",
    )(
        *(
            pltpu.with_memory_space_constraint(array, pltpu.HBM)
            for array in (
                stick_length,
                plane_index,
                occupation,
                jnp.swapaxes(rotation_matrix, 1, 2),
                coeffs.reshape(2 * in_count * sticks, grid_len),
            )
        )
    )
    arrived = lax.all_to_all(
        messages,
        ("band", "pw"),
        split_axis=0,
        concat_axis=0,
        axis_index_groups=[list(range(devices))[::-1]],
        tiled=True,
    )
    left, right = pl.pallas_call(
        functools.partial(table_kernel, grid_len, min(grid_len, stick_count), sticks, side),
        out_shape=(
            jax.ShapeDtypeStruct((2, grid_len // 2, stick_count), jnp.bfloat16),
            jax.ShapeDtypeStruct((stick_count, 2 * grid_len), jnp.bfloat16),
        ),
        in_specs=[hbm],
        out_specs=(vmem, vmem),
        scratch_shapes=[pltpu.VMEM((1, stick_count), jnp.int32), pltpu.SemaphoreType.DMA],
        compiler_params=room(table_bytes),
        cost_estimate=pl.CostEstimate(
            flops=80 * grid_len * stick_count,
            bytes_accessed=12 * grid_len * stick_count,
            transcendentals=0,
        ),
        name="stick_tables",
    )(pltpu.with_memory_space_constraint(stick_column.reshape(1, stick_count), pltpu.HBM))
    norm_factor = 1.0 / float(bands * stick_count * grid_len)
    blocks = 2 * own_planes * (grid_len // 2 // row_block(grid_len, stick_count))
    return pl.pallas_call(
        functools.partial(plane_kernel, bands, own_planes, norm_factor, sticks),
        out_shape=jax.ShapeDtypeStruct((own_planes, grid_len, grid_len), jnp.float32),
        in_specs=[vmem] * 3,
        out_specs=hbm,
        scratch_shapes=[
            pltpu.VMEM((rows, PACK, stick_count), jnp.bfloat16),
            pltpu.VMEM((own_planes, grid_len, grid_len), jnp.float32),
            pltpu.SemaphoreType.DMA((blocks,)),
        ],
        compiler_params=room(table_bytes, message_bytes),
        name="plane_density",
    )(arrived, left, right)


def solution(mesh):
    return jax.shard_map(
        shards,
        mesh=mesh,
        in_specs=(P(None, None, ("band", "pw"), None), P(), P(), P(), P(), P("band")),
        out_specs=P("pw", None, None),
        check_vma=False,
    )
```

```python
import functools
import math

import jax
import jax.numpy as jnp
from jax import lax
from jax.experimental import pallas as pl
from jax.experimental.pallas import tpu as pltpu
from jax.sharding import PartitionSpec as P

LANES = 128
PACK = 16
P_BLOCK = 16
BAND_GROUP = 8
GROUP_LANES = 256
COEFF_COPIES = 4
MIB = 1024 * 1024


def wrap(value, period):
    if period & (period - 1) == 0:
        return value & (period - 1)
    return lax.rem(value, period)


def cut(value, size):
    if size & (size - 1) == 0:
        return value >> (size.bit_length() - 1)
    return lax.div(value, size)


def cosine(index, period):
    fold = jnp.abs(wrap(index, period) - period // 2) - period // 4
    angle = fold.astype(jnp.float32) * (2.0 * math.pi / period)
    square = angle * angle
    series = -2.39e-08
    for factor in (2.7526e-06, -1.984090e-04, 8.3333315e-03, -1.666666664e-01, 1.0):
        series = series * square + factor
    return angle * series


def sine(index, period):
    return cosine(index + (period - period // 4), period)


def iota(shape, dim):
    return lax.broadcasted_iota(jnp.int32, shape, dim)


def dot_last(left, right):
    return lax.dot_general(
        left, right, (((1,), (1,)), ((), ())), preferred_element_type=jnp.float32
    )


def dot(left, right):
    return jnp.dot(left, right, preferred_element_type=jnp.float32)


def loop(count, body, carry):
    if count > 16:
        return lax.fori_loop(0, count, body, carry)
    for index in range(count):
        carry = body(index, carry)
    return carry


def room(*sizes):
    return pltpu.CompilerParams(vmem_limit_bytes=min(56 * MIB, 16 * MIB + 2 * sum(sizes)))


def row_block(grid_len):
    return math.gcd(grid_len // 2, P_BLOCK)


def lane_groups(sticks, spots, bands, lanes):
    groups = 1
    while 2 * groups * spots + bands <= lanes and sticks % (2 * groups) == 0 and sticks > 4 * groups:
        groups *= 2
    return groups


def spread(scalars, index, shape):
    result = jnp.full(shape, scalars[0])
    for place, scalar in enumerate(scalars[1:], 1):
        result = jnp.where(index == place, scalar, result)
    return result


def stick_kernel(
    length_hbm,
    plane_hbm,
    occupation_hbm,
    rotation_hbm,
    coeff_hbm,
    out_hbm,
    length_ref,
    plane_ref,
    occupation_ref,
    rotation_ref,
    coeff_ref,
    message_ref,
    sems,
):
    piece = coeff_ref.shape[0] // COEFF_COPIES
    pieces = [pl.ds(first * piece, piece) for first in range(COEFF_COPIES)]
    copies = [
        pltpu.make_async_copy(source, target, sems.at[index])
        for index, (source, target) in enumerate(
            (
                (rotation_hbm, rotation_ref),
                (plane_hbm, plane_ref),
                (length_hbm, length_ref),
                (occupation_hbm, occupation_ref),
                *((coeff_hbm.at[rows], coeff_ref.at[rows]) for rows in pieces),
            )
        )
    ]
    for copy in copies:
        copy.start()
    out_count, in_count = rotation_ref.shape[1:]
    grid_len = coeff_ref.shape[1]
    sticks = coeff_ref.shape[0] // (2 * in_count)
    plane_count = plane_ref.shape[0]
    pw_count = lax.axis_size("pw")
    own_planes = plane_count // pw_count
    own_bands = occupation_ref.shape[0]
    row_count = 2 * out_count * sticks
    lanes = message_ref.shape[2]
    band_index = lax.axis_index("band")
    first_stick = (band_index * pw_count + lax.axis_index("pw")) * sticks

    group_lanes = GROUP_LANES // (own_planes * 2 * out_count) * (own_planes * 2 * out_count)
    spots = own_planes * 2 * out_count
    side = lane_groups(sticks, spots, out_count, lanes)
    group_pw = group_lanes // spots

    wide = in_count * sticks
    widen = (cut(iota((in_count, wide), 1), sticks) == iota((in_count, wide), 0)).astype(
        jnp.bfloat16
    )
    same = wrap(iota((sticks, wide), 1), sticks) == iota((sticks, wide), 0)
    copies[0].wait()
    parts = [dot(rotation_ref[part], widen) for part in range(2)]
    rows = {}
    for band in range(out_count):
        real, imag = (
            jnp.where(same, jnp.broadcast_to(part[band : band + 1], (sticks, wide)), 0.0)
            for part in parts
        )
        rows[0, band] = jnp.concatenate([real, -imag], 1)
        rows[1, band] = jnp.concatenate([imag, real], 1)
    rotation = jnp.concatenate([rows[key] for key in sorted(rows)], 0).astype(jnp.bfloat16)

    for copy in copies[1:]:
        copy.wait()
    rotated = dot(rotation, coeff_ref[...])
    lengths = [length_ref[first_stick + place] for place in range(sticks)]
    row_lengths = spread(lengths, iota((sticks, grid_len), 0), (sticks, grid_len))
    live = iota((sticks, grid_len), 1) < row_lengths
    shape = (sticks, lanes)
    occupied = jnp.zeros(shape, jnp.int32)
    for own_band in range(own_bands):
        lane = side * spots + band_index * own_bands + own_band
        occupied = jnp.where(iota(shape, 1) == lane, occupation_ref[own_band], occupied)
    occupied = occupied.astype(jnp.float32)

    shape = (sticks, group_lanes)
    lane = iota(shape, 1)
    lane_plane = lax.div(lane, 2 * out_count)
    real_lane = lax.rem(lane, 2 * out_count) < out_count
    lane_band = lax.rem(lane, out_count)
    half_lengths = spread(lengths, iota(shape, 0), shape) >> 1

    def forms(first_pw):
        kinds = group_pw * own_planes
        planes = [plane_ref[first_pw * own_planes + place] for place in range(kinds)]
        kind = iota((2 * kinds, grid_len), 0)
        planes_down = spread(planes, lax.rem(kind, kinds), kind.shape)
        quarter = jnp.where(kind < kinds, 0, grid_len - grid_len // 4)
        waves = cosine(iota(kind.shape, 1) * planes_down + quarter, grid_len)
        place = iota((2 * kinds, 2 * group_lanes), 1)
        wanted = lax.div(lax.rem(place, group_lanes), 2 * out_count)
        wanted = jnp.where(place < group_lanes, wanted, wanted + kinds)
        widen = (iota(place.shape, 0) == wanted).astype(jnp.bfloat16)
        table = lax.dot_general(
            waves.astype(jnp.bfloat16),
            widen,
            (((0,), (0,)), ((), ())),
            preferred_element_type=jnp.float32,
        )
        lane_planes = spread(planes, lane_plane, shape)
        shift = half_lengths * lane_planes
        return table.astype(jnp.bfloat16), cosine(shift, grid_len), sine(shift, grid_len)

    def pick(sums, part):
        chosen = jnp.zeros(shape, jnp.float32)
        for band in range(out_count):
            top = (part * out_count + band) * sticks
            chosen = jnp.where(lane_band == band, sums[top : top + sticks], chosen)
        return chosen

    def send(first_pw, rotated, form):
        table, phase_cos, phase_sin = form
        sums = dot(rotated, table)
        with_cos, with_sin = sums[:, :group_lanes], sums[:, group_lanes:]
        real = pick(with_cos, 0) - pick(with_sin, 1)
        imag = pick(with_sin, 0) + pick(with_cos, 1)
        values = jnp.where(
            real_lane, real * phase_cos + imag * phase_sin, imag * phase_cos - real * phase_sin
        )
        for place in range(group_pw):
            first = place * spots
            tile = first // lanes * lanes
            part = values[:, tile : tile + lanes]
            message = occupied
            for index in reversed(range(side)):
                shift = (index * spots - (first - tile)) % lanes
                piece = pltpu.roll(part, shift, 1) if shift else part
                if index:
                    piece = pltpu.roll(piece, sticks - index * (sticks // side), 0)
                message = jnp.where(
                    iota((sticks, lanes), 1) < (index + 1) * spots, piece, message
                )
            message_ref[first_pw + place] = message[: sticks // side].astype(message_ref.dtype)

    if group_pw == pw_count:
        form = forms(0)
    rotated = rotated.reshape(row_count // sticks, sticks, grid_len)
    rotated = jnp.where(live[None], rotated, 0.0).reshape(row_count, grid_len)
    rotated = rotated.astype(jnp.bfloat16)
    if group_pw == pw_count:
        send(0, rotated, form)
    else:

        def one_group(index, carry):
            send(index * group_pw, rotated, forms(index * group_pw))
            return carry

        lax.fori_loop(0, pw_count // group_pw, one_group, 0)
    for band in range(1, out_hbm.shape[0] // pw_count):
        message_ref[band * pw_count : (band + 1) * pw_count] = message_ref[:pw_count]
    copy = pltpu.make_async_copy(message_ref, out_hbm, sems.at[0])
    copy.start()
    copy.wait()


def reorder(columns, grid_len, chunk, sticks, side):
    count = columns.shape[1]
    shape = (chunk, chunk)
    to, rows = iota(shape, 1), sticks // side
    index, rest = lax.div(to, chunk // side), lax.rem(to, chunk // side)
    source = lax.div(rest, rows) * sticks + index * rows + lax.rem(rest, rows)
    order = (iota(shape, 0) == source).astype(jnp.bfloat16)
    shape = (8, count)
    columns = jnp.broadcast_to(columns, shape)
    halves = jnp.where(iota(shape, 0) == 0, cut(columns, grid_len), wrap(columns, grid_len))
    halves = halves.astype(jnp.float32).astype(jnp.bfloat16)
    ordered = [
        dot(halves[:, first : first + chunk], order) for first in range(0, count, chunk)
    ]
    ordered = jnp.concatenate(ordered, 1).astype(jnp.int32)
    return ordered[:1] * grid_len + ordered[1:2]


def table_kernel(grid_len, chunk, sticks, side, column_hbm, left_ref, right_ref, column_ref, sem):
    copy = pltpu.make_async_copy(column_hbm, column_ref, sem)
    copy.start()
    copy.wait()
    count = column_ref.shape[1]
    half = grid_len // 2
    columns = column_ref[...]
    if side > 1:
        columns = reorder(columns, grid_len, chunk, sticks, side)
    turns = iota((half, count), 0) * cut(columns, grid_len)
    left_ref[0] = cosine(turns, grid_len).astype(jnp.bfloat16)
    left_ref[1] = sine(turns, grid_len).astype(jnp.bfloat16)
    tall = jnp.transpose(jnp.broadcast_to(columns, (half, count)))
    sign = (1 - 2 * (cut(tall, grid_len) & 1)).astype(jnp.float32)
    tall = wrap(tall, grid_len)
    freq = iota((count, half), 1)
    values = cosine(tall * freq, grid_len)
    right_ref[:, :half] = values.astype(jnp.bfloat16)
    right_ref[:, grid_len : grid_len + half] = (sign * values).astype(jnp.bfloat16)
    turns = jnp.where(freq == 0, tall * half, tall * freq + (grid_len - grid_len // 4))
    values = cosine(turns, grid_len)
    right_ref[:, half:grid_len] = values.astype(jnp.bfloat16)
    right_ref[:, grid_len + half :] = (sign * values).astype(jnp.bfloat16)


def plane_kernel(
    bands,
    own_planes,
    norm_factor,
    sticks,
    message_ref,
    left_ref,
    right_ref,
    out_ref,
    value_ref,
    held_ref,
    sem,
):
    rows, _, count = value_ref.shape
    chunk = min(out_ref.shape[1], count)
    chunks = count // chunk
    grid_len = out_ref.shape[1]
    half = grid_len // 2
    message_rows, lanes = message_ref.shape[1:]
    side = sticks // message_rows
    spots = 2 * bands
    height = row_block(grid_len)
    blocks = half // height
    group = math.gcd(bands, BAND_GROUP)
    shape = (side * rows + bands, lanes)
    select = (iota(shape, 0) == iota(shape, 1)).astype(jnp.bfloat16)

    def turn(index):
        pieces = chunk // sticks
        message = message_ref[pl.ds(index * pieces, pieces)]
        return dot_last(select, message.reshape(pieces * message_rows, lanes))

    def occupations(picked):
        return jnp.max(picked[side * rows :], 1, keepdims=True)

    def keep(index, picked, scale):
        width = chunk // side
        for row in range(rows):
            for place in range(side):
                piece = picked[place * rows + row : place * rows + row + 1]
                piece = piece * scale[row % bands : row % bands + 1]
                value_ref[row, :, pl.ds(index * chunk + place * width, width)] = (
                    jnp.broadcast_to(piece, (PACK, width)).astype(jnp.bfloat16)
                )

    picked = turn(0)
    found = occupations(picked)
    for index in range(1, chunks):
        found = jnp.maximum(found, occupations(turn(index)))
    peak = jnp.max(found, 0, keepdims=True)
    scale = jnp.where(found == peak, 1.0, jnp.sqrt(found / jnp.maximum(peak, 1.0)))
    keep(0, picked, scale)
    for index in range(1, chunks):
        keep(index, turn(index), scale)
    factor = peak * norm_factor

    def stick_sums(index, block, first_band):
        lane = pl.ds(index * chunk, chunk)
        row = pl.ds(block * height, height)
        cos_table = left_ref[0, row, lane].reshape(height // PACK, PACK, chunk)
        sin_table = left_ref[1, row, lane].reshape(height // PACK, PACK, chunk)
        parts = []
        for plane in range(own_planes):
            for band in range(group):
                at = plane * spots + first_band + band
                real, imag = value_ref[at, :, lane][None], value_ref[at + bands, :, lane][None]
                parts.append((cos_table * real - sin_table * imag).reshape(height, chunk))
                parts.append((sin_table * real + cos_table * imag).reshape(height, chunk))
        return dot(jnp.concatenate(parts, 0), right_ref[pl.ds(index * chunk, chunk), :])

    def group_sums(step):
        first_band, block = step % groups * group, step // groups
        if chunks == 1:
            return stick_sums(0, block, first_band)
        return lax.fori_loop(
            0,
            chunks,
            lambda at, so_far: so_far + stick_sums(at, block, first_band),
            jnp.zeros((2 * own_planes * group * height, 2 * grid_len), jnp.float32),
        )

    def add_squares(found, sums):
        result = []
        for place, (with_cos, with_sin, mixed) in enumerate(sums):
            plane, left = place // 2, place % 2 * grid_len
            for band in range(group):
                top = 2 * (plane * group + band) * height
                a = found[top : top + height, left : left + half]
                d = found[top : top + height, left + half : left + grid_len]
                top += height
                c = found[top : top + height, left : left + half]
                b = found[top : top + height, left + half : left + grid_len]
                with_cos += a * a + c * c
                with_sin += b * b + d * d
                mixed += c * d - a * b
            result.append((with_cos, with_sin, mixed))
        return result

    def copy_out(place, block):
        where = (place // 2, pl.ds(place % 2 * half + block * height, height))
        return pltpu.make_async_copy(
            held_ref.at[where], out_ref.at[where], sem.at[place * blocks + block]
        )

    def finish(block, sums):
        lane = iota((height, half), 1)
        for place, (with_cos, with_sin, mixed) in enumerate(sums):
            both, mixed = with_cos + with_sin, mixed + mixed
            ahead = jnp.where(lane == 0, with_cos, both + mixed)
            back = jnp.where(lane == 0, with_sin, both - mixed)
            row = pl.ds(place % 2 * half + block * height, height)
            held_ref[place // 2, row, :half] = ahead * factor
            held_ref[place // 2, row, half:] = jnp.take_along_axis(
                back * factor, jnp.where(lane == 0, 0, half - lane), axis=1
            )
            copy_out(place, block).start()

    zero = jnp.zeros((height, half), jnp.float32)
    empty = [(zero, zero, zero)] * (2 * own_planes)
    groups = bands // group
    if blocks * groups > 16:

        def one_block(block, carry):
            def one_group(index, sums):
                step = block * groups + index
                return add_squares(group_sums(step), sums)

            finish(block, lax.fori_loop(0, groups, one_group, empty))
            return carry

        lax.fori_loop(0, blocks, one_block, 0)
    else:
        sums, ahead = empty, group_sums(0)
        for step in range(blocks * groups):
            found = ahead
            if step + 1 < blocks * groups:
                ahead = group_sums(step + 1)
            sums = add_squares(found, sums)
            if (step + 1) % groups == 0:
                finish(step // groups, sums)
                sums = empty
    for place in range(2 * own_planes):
        for block in range(blocks):
            copy_out(place, block).wait()


def shards(coeffs, rotation_matrix, stick_length, stick_column, plane_index, occupation):
    band_count = lax.axis_size("band")
    pw_count = lax.axis_size("pw")
    devices = band_count * pw_count
    in_count, sticks, grid_len = coeffs.shape[1:]
    bands = rotation_matrix.shape[2]
    stick_count = stick_column.shape[0]
    own_planes = plane_index.shape[0] // pw_count
    spots = 2 * bands
    rows = own_planes * spots
    lanes = -(-(rows + bands) // LANES) * LANES
    side = lane_groups(sticks, rows, bands, lanes)
    message_rows = sticks // side
    vmem = pl.BlockSpec(memory_space=pltpu.VMEM)
    hbm = pl.BlockSpec(memory_space=pltpu.HBM)
    table_bytes = 8 * grid_len * stick_count
    message_bytes = 2 * stick_count * lanes

    messages = pl.pallas_call(
        stick_kernel,
        out_shape=jax.ShapeDtypeStruct((devices, message_rows, lanes), jnp.bfloat16),
        in_specs=[hbm] * 5,
        out_specs=hbm,
        scratch_shapes=[
            pltpu.SMEM(stick_length.shape, jnp.int32),
            pltpu.SMEM(plane_index.shape, jnp.int32),
            pltpu.SMEM(occupation.shape, jnp.int32),
            pltpu.VMEM((2, bands, in_count), jnp.bfloat16),
            pltpu.VMEM((2 * in_count * sticks, grid_len), jnp.bfloat16),
            pltpu.VMEM((devices, message_rows, lanes), jnp.bfloat16),
            pltpu.SemaphoreType.DMA((max(4 + COEFF_COPIES, band_count),)),
        ],
        compiler_params=room(2 * message_bytes),
        name="stick_values",
    )(
        *(
            pltpu.with_memory_space_constraint(array, pltpu.HBM)
            for array in (
                stick_length,
                plane_index,
                occupation,
                jnp.swapaxes(rotation_matrix, 1, 2),
                coeffs.reshape(2 * in_count * sticks, grid_len),
            )
        )
    )
    arrived = lax.all_to_all(messages, ("band", "pw"), split_axis=0, concat_axis=0, tiled=True)
    left, right = pl.pallas_call(
        functools.partial(table_kernel, grid_len, min(grid_len, stick_count), sticks, side),
        out_shape=(
            jax.ShapeDtypeStruct((2, grid_len // 2, stick_count), jnp.bfloat16),
            jax.ShapeDtypeStruct((stick_count, 2 * grid_len), jnp.bfloat16),
        ),
        in_specs=[hbm],
        out_specs=(vmem, vmem),
        scratch_shapes=[pltpu.VMEM((1, stick_count), jnp.int32), pltpu.SemaphoreType.DMA],
        compiler_params=room(table_bytes),
        cost_estimate=pl.CostEstimate(
            flops=80 * grid_len * stick_count,
            bytes_accessed=12 * grid_len * stick_count,
            transcendentals=0,
        ),
        name="stick_tables",
    )(pltpu.with_memory_space_constraint(stick_column.reshape(1, stick_count), pltpu.HBM))
    norm_factor = 1.0 / float(bands * stick_count * grid_len)
    blocks = 2 * own_planes * (grid_len // 2 // row_block(grid_len))
    return pl.pallas_call(
        functools.partial(plane_kernel, bands, own_planes, norm_factor, sticks),
        out_shape=jax.ShapeDtypeStruct((own_planes, grid_len, grid_len), jnp.float32),
        in_specs=[vmem] * 3,
        out_specs=hbm,
        scratch_shapes=[
            pltpu.VMEM((rows, PACK, stick_count), jnp.bfloat16),
            pltpu.VMEM((own_planes, grid_len, grid_len), jnp.float32),
            pltpu.SemaphoreType.DMA((blocks,)),
        ],
        compiler_params=room(table_bytes, message_bytes),
        name="plane_density",
    )(arrived, left, right)


def solution(mesh):
    return jax.shard_map(
        shards,
        mesh=mesh,
        in_specs=(P(None, None, ("band", "pw"), None), P(), P(), P(), P(), P("band")),
        out_specs=P("pw", None, None),
        check_vma=False,
    )
```

```python
import functools
import math

import jax
import jax.numpy as jnp
from jax import lax
from jax.experimental import pallas as pl
from jax.experimental.pallas import tpu as pltpu
from jax.sharding import PartitionSpec as P

LANES = 128
PACK = 16
P_BLOCK = 16
BAND_GROUP = 8
GROUP_LANES = 256
COEFF_COPIES = 4
MIB = 1024 * 1024


def wrap(value, period):
    if period & (period - 1) == 0:
        return value & (period - 1)
    return lax.rem(value, period)


def cut(value, size):
    if size & (size - 1) == 0:
        return value >> (size.bit_length() - 1)
    return lax.div(value, size)


def cosine(index, period):
    fold = jnp.abs(wrap(index, period) - period // 2) - period // 4
    angle = fold.astype(jnp.float32) * (2.0 * math.pi / period)
    square = angle * angle
    series = -2.39e-08
    for factor in (2.7526e-06, -1.984090e-04, 8.3333315e-03, -1.666666664e-01, 1.0):
        series = series * square + factor
    return angle * series


def sine(index, period):
    return cosine(index + (period - period // 4), period)


def iota(shape, dim):
    return lax.broadcasted_iota(jnp.int32, shape, dim)


def dot_last(left, right):
    return lax.dot_general(
        left, right, (((1,), (1,)), ((), ())), preferred_element_type=jnp.float32
    )


def dot(left, right):
    return jnp.dot(left, right, preferred_element_type=jnp.float32)


def loop(count, body, carry):
    if count > 16:
        return lax.fori_loop(0, count, body, carry)
    for index in range(count):
        carry = body(index, carry)
    return carry


def room(*sizes):
    return pltpu.CompilerParams(vmem_limit_bytes=min(56 * MIB, 16 * MIB + 2 * sum(sizes)))


def row_block(grid_len):
    return math.gcd(grid_len // 2, P_BLOCK)


def lane_groups(sticks, spots, bands, lanes):
    groups = 1
    while 2 * groups * spots + bands <= lanes and sticks % (2 * groups) == 0 and sticks > 4 * groups:
        groups *= 2
    return groups


def spread(scalars, index, shape):
    result = jnp.full(shape, scalars[0])
    for place, scalar in enumerate(scalars[1:], 1):
        result = jnp.where(index == place, scalar, result)
    return result


def stick_kernel(
    length_hbm,
    plane_hbm,
    occupation_hbm,
    rotation_hbm,
    coeff_hbm,
    out_hbm,
    length_ref,
    plane_ref,
    occupation_ref,
    rotation_ref,
    coeff_ref,
    message_ref,
    sems,
):
    piece = coeff_ref.shape[0] // COEFF_COPIES
    pieces = [pl.ds(first * piece, piece) for first in range(COEFF_COPIES)]
    copies = [
        pltpu.make_async_copy(source, target, sems.at[index])
        for index, (source, target) in enumerate(
            (
                (rotation_hbm, rotation_ref),
                (plane_hbm, plane_ref),
                (length_hbm, length_ref),
                (occupation_hbm, occupation_ref),
                *((coeff_hbm.at[rows], coeff_ref.at[rows]) for rows in pieces),
            )
        )
    ]
    for copy in copies:
        copy.start()
    out_count, in_count = rotation_ref.shape[1:]
    grid_len = coeff_ref.shape[1]
    sticks = coeff_ref.shape[0] // (2 * in_count)
    plane_count = plane_ref.shape[0]
    pw_count = lax.axis_size("pw")
    own_planes = plane_count // pw_count
    own_bands = occupation_ref.shape[0]
    row_count = 2 * out_count * sticks
    lanes = message_ref.shape[2]
    band_index = lax.axis_index("band")
    first_stick = (band_index * pw_count + lax.axis_index("pw")) * sticks

    group_lanes = GROUP_LANES // (own_planes * 2 * out_count) * (own_planes * 2 * out_count)
    spots = own_planes * 2 * out_count
    side = lane_groups(sticks, spots, out_count, lanes)
    group_pw = group_lanes // spots

    wide = in_count * sticks
    widen = (cut(iota((in_count, wide), 1), sticks) == iota((in_count, wide), 0)).astype(
        jnp.bfloat16
    )
    same = wrap(iota((sticks, wide), 1), sticks) == iota((sticks, wide), 0)
    copies[0].wait()
    parts = [dot(rotation_ref[part], widen) for part in range(2)]
    rows = {}
    for band in range(out_count):
        real, imag = (
            jnp.where(same, jnp.broadcast_to(part[band : band + 1], (sticks, wide)), 0.0)
            for part in parts
        )
        rows[0, band] = jnp.concatenate([real, -imag], 1)
        rows[1, band] = jnp.concatenate([imag, real], 1)
    rotation = jnp.concatenate([rows[key] for key in sorted(rows)], 0).astype(jnp.bfloat16)

    for copy in copies[1:]:
        copy.wait()
    rotated = dot(rotation, coeff_ref[...])
    lengths = [length_ref[first_stick + place] for place in range(sticks)]
    row_lengths = spread(lengths, iota((sticks, grid_len), 0), (sticks, grid_len))
    live = iota((sticks, grid_len), 1) < row_lengths
    shape = (sticks, lanes)
    occupied = jnp.zeros(shape, jnp.int32)
    for own_band in range(own_bands):
        lane = side * spots + band_index * own_bands + own_band
        occupied = jnp.where(iota(shape, 1) == lane, occupation_ref[own_band], occupied)
    occupied = occupied.astype(jnp.float32)

    shape = (sticks, group_lanes)
    lane = iota(shape, 1)
    lane_plane = lax.div(lane, 2 * out_count)
    real_lane = lax.rem(lane, 2 * out_count) < out_count
    lane_band = lax.rem(lane, out_count)
    half_lengths = spread(lengths, iota(shape, 0), shape) >> 1

    def forms(first_pw):
        kinds = group_pw * own_planes
        planes = [plane_ref[first_pw * own_planes + place] for place in range(kinds)]
        kind = iota((2 * kinds, grid_len), 0)
        planes_down = spread(planes, lax.rem(kind, kinds), kind.shape)
        quarter = jnp.where(kind < kinds, 0, grid_len - grid_len // 4)
        waves = cosine(iota(kind.shape, 1) * planes_down + quarter, grid_len)
        place = iota((2 * kinds, 2 * group_lanes), 1)
        wanted = lax.div(lax.rem(place, group_lanes), 2 * out_count)
        wanted = jnp.where(place < group_lanes, wanted, wanted + kinds)
        widen = (iota(place.shape, 0) == wanted).astype(jnp.bfloat16)
        table = lax.dot_general(
            waves.astype(jnp.bfloat16),
            widen,
            (((0,), (0,)), ((), ())),
            preferred_element_type=jnp.float32,
        )
        lane_planes = spread(planes, lane_plane, shape)
        shift = half_lengths * lane_planes
        return table.astype(jnp.bfloat16), cosine(shift, grid_len), sine(shift, grid_len)

    def pick(sums, part):
        chosen = jnp.zeros(shape, jnp.float32)
        for band in range(out_count):
            top = (part * out_count + band) * sticks
            chosen = jnp.where(lane_band == band, sums[top : top + sticks], chosen)
        return chosen

    def send(first_pw, rotated, form):
        table, phase_cos, phase_sin = form
        sums = dot(rotated, table)
        with_cos, with_sin = sums[:, :group_lanes], sums[:, group_lanes:]
        real = pick(with_cos, 0) - pick(with_sin, 1)
        imag = pick(with_sin, 0) + pick(with_cos, 1)
        values = jnp.where(
            real_lane, real * phase_cos + imag * phase_sin, imag * phase_cos - real * phase_sin
        )
        for place in range(group_pw):
            first = place * spots
            tile = first // lanes * lanes
            part = values[:, tile : tile + lanes]
            message = occupied
            for index in reversed(range(side)):
                shift = (index * spots - (first - tile)) % lanes
                piece = pltpu.roll(part, shift, 1) if shift else part
                if index:
                    piece = pltpu.roll(piece, sticks - index * (sticks // side), 0)
                message = jnp.where(
                    iota((sticks, lanes), 1) < (index + 1) * spots, piece, message
                )
            message_ref[wrap(pw_count - first_pw - place, pw_count)] = message[: sticks // side].astype(message_ref.dtype)

    if group_pw == pw_count:
        form = forms(0)
    rotated = rotated.reshape(row_count // sticks, sticks, grid_len)
    rotated = jnp.where(live[None], rotated, 0.0).reshape(row_count, grid_len)
    rotated = rotated.astype(jnp.bfloat16)
    if group_pw == pw_count:
        send(0, rotated, form)
    else:

        def one_group(index, carry):
            send(index * group_pw, rotated, forms(index * group_pw))
            return carry

        lax.fori_loop(0, pw_count // group_pw, one_group, 0)
    for band in range(1, out_hbm.shape[0] // pw_count):
        message_ref[band * pw_count : (band + 1) * pw_count] = message_ref[:pw_count]
    copy = pltpu.make_async_copy(message_ref, out_hbm, sems.at[0])
    copy.start()
    copy.wait()


def reorder(columns, grid_len, chunk, sticks, side):
    count = columns.shape[1]
    shape = (chunk, chunk)
    to, rows = iota(shape, 1), sticks // side
    index, rest = lax.div(to, chunk // side), lax.rem(to, chunk // side)
    device = chunk // sticks - 1 - lax.div(rest, rows)
    source = device * sticks + index * rows + lax.rem(rest, rows)
    order = (iota(shape, 0) == source).astype(jnp.bfloat16)
    shape = (8, count)
    columns = pltpu.roll(jnp.broadcast_to(columns, shape), count - sticks, 1)
    halves = jnp.where(iota(shape, 0) == 0, cut(columns, grid_len), wrap(columns, grid_len))
    halves = halves.astype(jnp.float32).astype(jnp.bfloat16)
    ordered = [
        dot(halves[:, first : first + chunk], order) for first in range(0, count, chunk)[::-1]
    ]
    ordered = jnp.concatenate(ordered, 1).astype(jnp.int32)
    return ordered[:1] * grid_len + ordered[1:2]


def table_kernel(grid_len, chunk, sticks, side, column_hbm, left_ref, right_ref, column_ref, sem):
    copy = pltpu.make_async_copy(column_hbm, column_ref, sem)
    copy.start()
    copy.wait()
    count = column_ref.shape[1]
    half = grid_len // 2
    columns = column_ref[...]
    columns = reorder(columns, grid_len, chunk, sticks, side)
    turns = iota((half, count), 0) * cut(columns, grid_len)
    left_ref[0] = cosine(turns, grid_len).astype(jnp.bfloat16)
    left_ref[1] = sine(turns, grid_len).astype(jnp.bfloat16)
    tall = jnp.transpose(jnp.broadcast_to(columns, (half, count)))
    sign = (1 - 2 * (cut(tall, grid_len) & 1)).astype(jnp.float32)
    tall = wrap(tall, grid_len)
    freq = iota((count, half), 1)
    values = cosine(tall * freq, grid_len)
    right_ref[:, :half] = values.astype(jnp.bfloat16)
    right_ref[:, grid_len : grid_len + half] = (sign * values).astype(jnp.bfloat16)
    turns = jnp.where(freq == 0, tall * half, tall * freq + (grid_len - grid_len // 4))
    values = cosine(turns, grid_len)
    right_ref[:, half:grid_len] = values.astype(jnp.bfloat16)
    right_ref[:, grid_len + half :] = (sign * values).astype(jnp.bfloat16)


def plane_kernel(
    bands,
    own_planes,
    norm_factor,
    sticks,
    message_ref,
    left_ref,
    right_ref,
    out_ref,
    value_ref,
    held_ref,
    sem,
):
    rows, _, count = value_ref.shape
    chunk = min(out_ref.shape[1], count)
    chunks = count // chunk
    grid_len = out_ref.shape[1]
    half = grid_len // 2
    message_rows, lanes = message_ref.shape[1:]
    side = sticks // message_rows
    spots = 2 * bands
    height = row_block(grid_len)
    blocks = half // height
    group = math.gcd(bands, BAND_GROUP)
    shape = (side * rows + bands, lanes)
    select = (iota(shape, 0) == iota(shape, 1)).astype(jnp.bfloat16)

    def turn(index):
        pieces = chunk // sticks
        message = message_ref[pl.ds(index * pieces, pieces)]
        return dot_last(select, message.reshape(pieces * message_rows, lanes))

    def occupations(picked):
        return jnp.max(picked[side * rows :], 1, keepdims=True)

    def keep(index, picked, scale):
        width = chunk // side
        for row in range(rows):
            for place in range(side):
                piece = picked[place * rows + row : place * rows + row + 1]
                piece = piece * scale[row % bands : row % bands + 1]
                value_ref[row, :, pl.ds(index * chunk + place * width, width)] = (
                    jnp.broadcast_to(piece, (PACK, width)).astype(jnp.bfloat16)
                )

    picked = turn(0)
    found = occupations(picked)
    for index in range(1, chunks):
        found = jnp.maximum(found, occupations(turn(index)))
    peak = jnp.max(found, 0, keepdims=True)
    scale = jnp.where(found == peak, 1.0, jnp.sqrt(found / jnp.maximum(peak, 1.0)))
    keep(0, picked, scale)
    for index in range(1, chunks):
        keep(index, turn(index), scale)
    factor = peak * norm_factor

    def stick_sums(index, block, first_band):
        lane = pl.ds(index * chunk, chunk)
        row = pl.ds(block * height, height)
        cos_table = left_ref[0, row, lane].reshape(height // PACK, PACK, chunk)
        sin_table = left_ref[1, row, lane].reshape(height // PACK, PACK, chunk)
        parts = []
        for plane in range(own_planes):
            for band in range(group):
                at = plane * spots + first_band + band
                real, imag = value_ref[at, :, lane][None], value_ref[at + bands, :, lane][None]
                parts.append((cos_table * real - sin_table * imag).reshape(height, chunk))
                parts.append((sin_table * real + cos_table * imag).reshape(height, chunk))
        return dot(jnp.concatenate(parts, 0), right_ref[pl.ds(index * chunk, chunk), :])

    def group_sums(step):
        first_band, block = step % groups * group, step // groups
        if chunks == 1:
            return stick_sums(0, block, first_band)
        return lax.fori_loop(
            0,
            chunks,
            lambda at, so_far: so_far + stick_sums(at, block, first_band),
            jnp.zeros((2 * own_planes * group * height, 2 * grid_len), jnp.float32),
        )

    def add_squares(found, sums):
        result = []
        for place, (with_cos, with_sin, mixed) in enumerate(sums):
            plane, left = place // 2, place % 2 * grid_len
            for band in range(group):
                top = 2 * (plane * group + band) * height
                a = found[top : top + height, left : left + half]
                d = found[top : top + height, left + half : left + grid_len]
                top += height
                c = found[top : top + height, left : left + half]
                b = found[top : top + height, left + half : left + grid_len]
                with_cos += a * a + c * c
                with_sin += b * b + d * d
                mixed += c * d - a * b
            result.append((with_cos, with_sin, mixed))
        return result

    def copy_out(place, block):
        where = (place // 2, pl.ds(place % 2 * half + block * height, height))
        return pltpu.make_async_copy(
            held_ref.at[where], out_ref.at[where], sem.at[place * blocks + block]
        )

    def finish(block, sums):
        lane = iota((height, half), 1)
        for place, (with_cos, with_sin, mixed) in enumerate(sums):
            both, mixed = with_cos + with_sin, mixed + mixed
            ahead = jnp.where(lane == 0, with_cos, both + mixed)
            back = jnp.where(lane == 0, with_sin, both - mixed)
            row = pl.ds(place % 2 * half + block * height, height)
            held_ref[place // 2, row, :half] = ahead * factor
            held_ref[place // 2, row, half:] = jnp.take_along_axis(
                back * factor, jnp.where(lane == 0, 0, half - lane), axis=1
            )
            copy_out(place, block).start()

    zero = jnp.zeros((height, half), jnp.float32)
    empty = [(zero, zero, zero)] * (2 * own_planes)
    groups = bands // group
    if blocks * groups > 16:

        def one_block(block, carry):
            def one_group(index, sums):
                step = block * groups + index
                return add_squares(group_sums(step), sums)

            finish(block, lax.fori_loop(0, groups, one_group, empty))
            return carry

        lax.fori_loop(0, blocks, one_block, 0)
    else:
        sums, ahead = empty, group_sums(0)
        for step in range(blocks * groups):
            found = ahead
            if step + 1 < blocks * groups:
                ahead = group_sums(step + 1)
            sums = add_squares(found, sums)
            if (step + 1) % groups == 0:
                finish(step // groups, sums)
                sums = empty
    for place in range(2 * own_planes):
        for block in range(blocks):
            copy_out(place, block).wait()


def shards(coeffs, rotation_matrix, stick_length, stick_column, plane_index, occupation):
    band_count = lax.axis_size("band")
    pw_count = lax.axis_size("pw")
    devices = band_count * pw_count
    in_count, sticks, grid_len = coeffs.shape[1:]
    bands = rotation_matrix.shape[2]
    stick_count = stick_column.shape[0]
    own_planes = plane_index.shape[0] // pw_count
    spots = 2 * bands
    rows = own_planes * spots
    lanes = -(-(rows + bands) // LANES) * LANES
    side = lane_groups(sticks, rows, bands, lanes)
    message_rows = sticks // side
    vmem = pl.BlockSpec(memory_space=pltpu.VMEM)
    hbm = pl.BlockSpec(memory_space=pltpu.HBM)
    table_bytes = 8 * grid_len * stick_count
    message_bytes = 2 * stick_count * lanes

    messages = pl.pallas_call(
        stick_kernel,
        out_shape=jax.ShapeDtypeStruct((devices, message_rows, lanes), jnp.bfloat16),
        in_specs=[hbm] * 5,
        out_specs=hbm,
        scratch_shapes=[
            pltpu.SMEM(stick_length.shape, jnp.int32),
            pltpu.SMEM(plane_index.shape, jnp.int32),
            pltpu.SMEM(occupation.shape, jnp.int32),
            pltpu.VMEM((2, bands, in_count), jnp.bfloat16),
            pltpu.VMEM((2 * in_count * sticks, grid_len), jnp.bfloat16),
            pltpu.VMEM((devices, message_rows, lanes), jnp.bfloat16),
            pltpu.SemaphoreType.DMA((max(4 + COEFF_COPIES, band_count),)),
        ],
        compiler_params=room(2 * message_bytes),
        name="stick_values",
    )(
        *(
            pltpu.with_memory_space_constraint(array, pltpu.HBM)
            for array in (
                stick_length,
                plane_index,
                occupation,
                jnp.swapaxes(rotation_matrix, 1, 2),
                coeffs.reshape(2 * in_count * sticks, grid_len),
            )
        )
    )
    arrived = lax.all_to_all(
        messages,
        ("band", "pw"),
        split_axis=0,
        concat_axis=0,
        axis_index_groups=[[0, *range(devices - 1, 0, -1)]],
        tiled=True,
    )
    left, right = pl.pallas_call(
        functools.partial(table_kernel, grid_len, min(grid_len, stick_count), sticks, side),
        out_shape=(
            jax.ShapeDtypeStruct((2, grid_len // 2, stick_count), jnp.bfloat16),
            jax.ShapeDtypeStruct((stick_count, 2 * grid_len), jnp.bfloat16),
        ),
        in_specs=[hbm],
        out_specs=(vmem, vmem),
        scratch_shapes=[pltpu.VMEM((1, stick_count), jnp.int32), pltpu.SemaphoreType.DMA],
        compiler_params=room(table_bytes),
        cost_estimate=pl.CostEstimate(
            flops=80 * grid_len * stick_count,
            bytes_accessed=12 * grid_len * stick_count,
            transcendentals=0,
        ),
        name="stick_tables",
    )(pltpu.with_memory_space_constraint(stick_column.reshape(1, stick_count), pltpu.HBM))
    norm_factor = 1.0 / float(bands * stick_count * grid_len)
    blocks = 2 * own_planes * (grid_len // 2 // row_block(grid_len))
    return pl.pallas_call(
        functools.partial(plane_kernel, bands, own_planes, norm_factor, sticks),
        out_shape=jax.ShapeDtypeStruct((own_planes, grid_len, grid_len), jnp.float32),
        in_specs=[vmem] * 3,
        out_specs=hbm,
        scratch_shapes=[
            pltpu.VMEM((rows, PACK, stick_count), jnp.bfloat16),
            pltpu.VMEM((own_planes, grid_len, grid_len), jnp.float32),
            pltpu.SemaphoreType.DMA((blocks,)),
        ],
        compiler_params=room(table_bytes, message_bytes),
        name="plane_density",
    )(arrived, left, right)


def solution(mesh):
    return jax.shard_map(
        shards,
        mesh=mesh,
        in_specs=(P(None, None, ("band", "pw"), None), P(), P(), P(), P(), P("band")),
        out_specs=P("pw", None, None),
        check_vma=False,
    )
```

```python
import functools
import math

import jax
import jax.numpy as jnp
from jax import lax
from jax.experimental import pallas as pl
from jax.experimental.pallas import tpu as pltpu
from jax.sharding import PartitionSpec as P

LANES = 128
PACK = 16
P_BLOCK = 16
BAND_GROUP = 8
GROUP_LANES = 256
COEFF_COPIES = 4
MIB = 1024 * 1024


def wrap(value, period):
    if period & (period - 1) == 0:
        return value & (period - 1)
    return lax.rem(value, period)


def cut(value, size):
    if size & (size - 1) == 0:
        return value >> (size.bit_length() - 1)
    return lax.div(value, size)


def cosine(index, period):
    fold = jnp.abs(wrap(index, period) - period // 2) - period // 4
    angle = fold.astype(jnp.float32) * (2.0 * math.pi / period)
    square = angle * angle
    series = -2.39e-08
    for factor in (2.7526e-06, -1.984090e-04, 8.3333315e-03, -1.666666664e-01, 1.0):
        series = series * square + factor
    return angle * series


def sine(index, period):
    return cosine(index + (period - period // 4), period)


def iota(shape, dim):
    return lax.broadcasted_iota(jnp.int32, shape, dim)


def dot_last(left, right):
    return lax.dot_general(
        left, right, (((1,), (1,)), ((), ())), preferred_element_type=jnp.float32
    )


def dot(left, right):
    return jnp.dot(left, right, preferred_element_type=jnp.float32)


def loop(count, body, carry):
    if count > 16:
        return lax.fori_loop(0, count, body, carry)
    for index in range(count):
        carry = body(index, carry)
    return carry


def room(*sizes):
    return pltpu.CompilerParams(vmem_limit_bytes=min(56 * MIB, 16 * MIB + 2 * sum(sizes)))


def row_block(grid_len):
    return math.gcd(grid_len // 2, P_BLOCK)


def lane_groups(sticks, spots, bands, lanes):
    groups = 1
    while 2 * groups * spots + bands <= lanes and sticks % (2 * groups) == 0 and sticks > 4 * groups:
        groups *= 2
    return groups


def spread(scalars, index, shape):
    result = jnp.full(shape, scalars[0])
    for place, scalar in enumerate(scalars[1:], 1):
        result = jnp.where(index == place, scalar, result)
    return result


def stick_kernel(
    length_hbm,
    plane_hbm,
    occupation_hbm,
    rotation_hbm,
    coeff_hbm,
    out_hbm,
    length_ref,
    plane_ref,
    occupation_ref,
    rotation_ref,
    coeff_ref,
    message_ref,
    sems,
):
    piece = coeff_ref.shape[0] // COEFF_COPIES
    pieces = [pl.ds(first * piece, piece) for first in range(COEFF_COPIES)]
    copies = [
        pltpu.make_async_copy(source, target, sems.at[index])
        for index, (source, target) in enumerate(
            (
                (rotation_hbm, rotation_ref),
                (plane_hbm, plane_ref),
                (length_hbm, length_ref),
                (occupation_hbm, occupation_ref),
                *((coeff_hbm.at[rows], coeff_ref.at[rows]) for rows in pieces),
            )
        )
    ]
    for copy in copies:
        copy.start()
    out_count, in_count = rotation_ref.shape[1:]
    grid_len = coeff_ref.shape[1]
    sticks = coeff_ref.shape[0] // (2 * in_count)
    plane_count = plane_ref.shape[0]
    pw_count = lax.axis_size("pw")
    own_planes = plane_count // pw_count
    own_bands = occupation_ref.shape[0]
    row_count = 2 * out_count * sticks
    lanes = message_ref.shape[2]
    band_index = lax.axis_index("band")
    first_stick = (band_index * pw_count + lax.axis_index("pw")) * sticks

    group_lanes = GROUP_LANES // (own_planes * 2 * out_count) * (own_planes * 2 * out_count)
    spots = own_planes * 2 * out_count
    side = lane_groups(sticks, spots, out_count, lanes)
    group_pw = group_lanes // spots

    wide = in_count * sticks
    widen = (cut(iota((in_count, wide), 1), sticks) == iota((in_count, wide), 0)).astype(
        jnp.bfloat16
    )
    same = wrap(iota((sticks, wide), 1), sticks) == iota((sticks, wide), 0)
    copies[0].wait()
    parts = [dot(rotation_ref[part], widen) for part in range(2)]
    rows = {}
    for band in range(out_count):
        real, imag = (
            jnp.where(same, jnp.broadcast_to(part[band : band + 1], (sticks, wide)), 0.0)
            for part in parts
        )
        rows[0, band] = jnp.concatenate([real, -imag], 1)
        rows[1, band] = jnp.concatenate([imag, real], 1)
    rotation = jnp.concatenate([rows[key] for key in sorted(rows)], 0).astype(jnp.bfloat16)

    for copy in copies[1:]:
        copy.wait()
    rotated = dot(rotation, coeff_ref[...])
    lengths = [length_ref[first_stick + place] for place in range(sticks)]
    row_lengths = spread(lengths, iota((sticks, grid_len), 0), (sticks, grid_len))
    live = iota((sticks, grid_len), 1) < row_lengths
    shape = (sticks, lanes)
    occupied = jnp.zeros(shape, jnp.int32)
    for own_band in range(own_bands):
        lane = side * spots + band_index * own_bands + own_band
        occupied = jnp.where(iota(shape, 1) == lane, occupation_ref[own_band], occupied)
    occupied = occupied.astype(jnp.float32)

    shape = (sticks, group_lanes)
    lane = iota(shape, 1)
    lane_plane = lax.div(lane, 2 * out_count)
    real_lane = lax.rem(lane, 2 * out_count) < out_count
    lane_band = lax.rem(lane, out_count)
    half_lengths = spread(lengths, iota(shape, 0), shape) >> 1

    def forms(first_pw):
        kinds = group_pw * own_planes
        planes = [plane_ref[first_pw * own_planes + place] for place in range(kinds)]
        kind = iota((2 * kinds, grid_len), 0)
        planes_down = spread(planes, lax.rem(kind, kinds), kind.shape)
        quarter = jnp.where(kind < kinds, 0, grid_len - grid_len // 4)
        waves = cosine(iota(kind.shape, 1) * planes_down + quarter, grid_len)
        place = iota((2 * kinds, 2 * group_lanes), 1)
        wanted = lax.div(lax.rem(place, group_lanes), 2 * out_count)
        wanted = jnp.where(place < group_lanes, wanted, wanted + kinds)
        widen = (iota(place.shape, 0) == wanted).astype(jnp.bfloat16)
        table = lax.dot_general(
            waves.astype(jnp.bfloat16),
            widen,
            (((0,), (0,)), ((), ())),
            preferred_element_type=jnp.float32,
        )
        lane_planes = spread(planes, lane_plane, shape)
        shift = half_lengths * lane_planes
        return table.astype(jnp.bfloat16), cosine(shift, grid_len), sine(shift, grid_len)

    def pick(sums, part):
        chosen = jnp.zeros(shape, jnp.float32)
        for band in range(out_count):
            top = (part * out_count + band) * sticks
            chosen = jnp.where(lane_band == band, sums[top : top + sticks], chosen)
        return chosen

    def send(first_pw, rotated, form):
        table, phase_cos, phase_sin = form
        sums = dot(rotated, table)
        with_cos, with_sin = sums[:, :group_lanes], sums[:, group_lanes:]
        real = pick(with_cos, 0) - pick(with_sin, 1)
        imag = pick(with_sin, 0) + pick(with_cos, 1)
        values = jnp.where(
            real_lane, real * phase_cos + imag * phase_sin, imag * phase_cos - real * phase_sin
        )
        for place in range(group_pw):
            first = place * spots
            tile = first // lanes * lanes
            part = values[:, tile : tile + lanes]
            message = occupied
            for index in reversed(range(side)):
                shift = (index * spots - (first - tile)) % lanes
                piece = pltpu.roll(part, shift, 1) if shift else part
                if index:
                    piece = pltpu.roll(piece, sticks - index * (sticks // side), 0)
                message = jnp.where(
                    iota((sticks, lanes), 1) < (index + 1) * spots, piece, message
                )
            message_ref[first_pw + place] = message[: sticks // side].astype(message_ref.dtype)

    if group_pw == pw_count:
        form = forms(0)
    rotated = rotated.reshape(row_count // sticks, sticks, grid_len)
    rotated = jnp.where(live[None], rotated, 0.0).reshape(row_count, grid_len)
    rotated = rotated.astype(jnp.bfloat16)
    if group_pw == pw_count:
        send(0, rotated, form)
    else:

        def one_group(index, carry):
            send(index * group_pw, rotated, forms(index * group_pw))
            return carry

        lax.fori_loop(0, pw_count // group_pw, one_group, 0)
    copies = [
        pltpu.make_async_copy(
            message_ref, out_hbm.at[pl.ds(band * pw_count, pw_count)], sems.at[band]
        )
        for band in range(out_hbm.shape[0] // pw_count)
    ]
    for copy in copies:
        copy.start()
    for copy in copies:
        copy.wait()


def reorder(columns, grid_len, chunk, sticks, side):
    count = columns.shape[1]
    shape = (chunk, chunk)
    to, rows = iota(shape, 1), sticks // side
    index, rest = lax.div(to, chunk // side), lax.rem(to, chunk // side)
    source = lax.div(rest, rows) * sticks + index * rows + lax.rem(rest, rows)
    order = (iota(shape, 0) == source).astype(jnp.bfloat16)
    shape = (8, count)
    columns = jnp.broadcast_to(columns, shape)
    halves = jnp.where(iota(shape, 0) == 0, cut(columns, grid_len), wrap(columns, grid_len))
    halves = halves.astype(jnp.float32).astype(jnp.bfloat16)
    ordered = [
        dot(halves[:, first : first + chunk], order) for first in range(0, count, chunk)
    ]
    ordered = jnp.concatenate(ordered, 1).astype(jnp.int32)
    return ordered[:1] * grid_len + ordered[1:2]


def table_kernel(grid_len, chunk, sticks, side, column_hbm, left_ref, right_ref, column_ref, sem):
    copy = pltpu.make_async_copy(column_hbm, column_ref, sem)
    copy.start()
    copy.wait()
    count = column_ref.shape[1]
    half = grid_len // 2
    columns = column_ref[...]
    if side > 1:
        columns = reorder(columns, grid_len, chunk, sticks, side)
    turns = iota((half, count), 0) * cut(columns, grid_len)
    left_ref[0] = cosine(turns, grid_len).astype(jnp.bfloat16)
    left_ref[1] = sine(turns, grid_len).astype(jnp.bfloat16)
    tall = jnp.transpose(jnp.broadcast_to(columns, (half, count)))
    sign = (1 - 2 * (cut(tall, grid_len) & 1)).astype(jnp.float32)
    tall = wrap(tall, grid_len)
    freq = iota((count, half), 1)
    values = cosine(tall * freq, grid_len)
    right_ref[:, :half] = values.astype(jnp.bfloat16)
    right_ref[:, grid_len : grid_len + half] = (sign * values).astype(jnp.bfloat16)
    turns = jnp.where(freq == 0, tall * half, tall * freq + (grid_len - grid_len // 4))
    values = cosine(turns, grid_len)
    right_ref[:, half:grid_len] = values.astype(jnp.bfloat16)
    right_ref[:, grid_len + half :] = (sign * values).astype(jnp.bfloat16)


def plane_kernel(
    bands,
    own_planes,
    norm_factor,
    sticks,
    message_ref,
    left_ref,
    right_ref,
    out_ref,
    value_ref,
    held_ref,
    sem,
):
    rows, _, count = value_ref.shape
    chunk = min(out_ref.shape[1], count)
    chunks = count // chunk
    grid_len = out_ref.shape[1]
    half = grid_len // 2
    message_rows, lanes = message_ref.shape[1:]
    side = sticks // message_rows
    spots = 2 * bands
    height = row_block(grid_len)
    blocks = half // height
    group = math.gcd(bands, BAND_GROUP)
    shape = (side * rows + bands, lanes)
    select = (iota(shape, 0) == iota(shape, 1)).astype(jnp.bfloat16)

    def turn(index):
        pieces = chunk // sticks
        message = message_ref[pl.ds(index * pieces, pieces)]
        return dot_last(select, message.reshape(pieces * message_rows, lanes))

    def occupations(picked):
        return jnp.max(picked[side * rows :], 1, keepdims=True)

    def keep(index, picked, scale):
        width = chunk // side
        for row in range(rows):
            for place in range(side):
                piece = picked[place * rows + row : place * rows + row + 1]
                piece = piece * scale[row % bands : row % bands + 1]
                value_ref[row, :, pl.ds(index * chunk + place * width, width)] = (
                    jnp.broadcast_to(piece, (PACK, width)).astype(jnp.bfloat16)
                )

    picked = turn(0)
    found = occupations(picked)
    for index in range(1, chunks):
        found = jnp.maximum(found, occupations(turn(index)))
    peak = jnp.max(found, 0, keepdims=True)
    scale = jnp.where(found == peak, 1.0, jnp.sqrt(found / jnp.maximum(peak, 1.0)))
    keep(0, picked, scale)
    for index in range(1, chunks):
        keep(index, turn(index), scale)
    factor = peak * norm_factor

    def stick_sums(index, block, first_band):
        lane = pl.ds(index * chunk, chunk)
        row = pl.ds(block * height, height)
        cos_table = left_ref[0, row, lane].reshape(height // PACK, PACK, chunk)
        sin_table = left_ref[1, row, lane].reshape(height // PACK, PACK, chunk)
        parts = []
        for plane in range(own_planes):
            for band in range(group):
                at = plane * spots + first_band + band
                real, imag = value_ref[at, :, lane][None], value_ref[at + bands, :, lane][None]
                parts.append((cos_table * real - sin_table * imag).reshape(height, chunk))
                parts.append((sin_table * real + cos_table * imag).reshape(height, chunk))
        return dot(jnp.concatenate(parts, 0), right_ref[pl.ds(index * chunk, chunk), :])

    def group_sums(step):
        first_band, block = step % groups * group, step // groups
        if chunks == 1:
            return stick_sums(0, block, first_band)
        return lax.fori_loop(
            0,
            chunks,
            lambda at, so_far: so_far + stick_sums(at, block, first_band),
            jnp.zeros((2 * own_planes * group * height, 2 * grid_len), jnp.float32),
        )

    def add_squares(found, sums):
        result = []
        for place, (with_cos, with_sin, mixed) in enumerate(sums):
            plane, left = place // 2, place % 2 * grid_len
            for band in range(group):
                top = 2 * (plane * group + band) * height
                a = found[top : top + height, left : left + half]
                d = found[top : top + height, left + half : left + grid_len]
                top += height
                c = found[top : top + height, left : left + half]
                b = found[top : top + height, left + half : left + grid_len]
                with_cos += a * a + c * c
                with_sin += b * b + d * d
                mixed += c * d - a * b
            result.append((with_cos, with_sin, mixed))
        return result

    def copy_out(place, block):
        where = (place // 2, pl.ds(place % 2 * half + block * height, height))
        return pltpu.make_async_copy(
            held_ref.at[where], out_ref.at[where], sem.at[place * blocks + block]
        )

    def finish(block, sums):
        lane = iota((height, half), 1)
        for place, (with_cos, with_sin, mixed) in enumerate(sums):
            both, mixed = with_cos + with_sin, mixed + mixed
            ahead = jnp.where(lane == 0, with_cos, both + mixed)
            back = jnp.where(lane == 0, with_sin, both - mixed)
            row = pl.ds(place % 2 * half + block * height, height)
            held_ref[place // 2, row, :half] = ahead * factor
            held_ref[place // 2, row, half:] = jnp.take_along_axis(
                back * factor, jnp.where(lane == 0, 0, half - lane), axis=1
            )
            copy_out(place, block).start()

    zero = jnp.zeros((height, half), jnp.float32)
    empty = [(zero, zero, zero)] * (2 * own_planes)
    groups = bands // group
    if blocks * groups > 16:

        def one_block(block, carry):
            def one_group(index, sums):
                step = block * groups + index
                return add_squares(group_sums(step), sums)

            finish(block, lax.fori_loop(0, groups, one_group, empty))
            return carry

        lax.fori_loop(0, blocks, one_block, 0)
    else:
        sums, ahead = empty, group_sums(0)
        for step in range(blocks * groups):
            found = ahead
            if step + 1 < blocks * groups:
                ahead = group_sums(step + 1)
            sums = add_squares(found, sums)
            if (step + 1) % groups == 0:
                finish(step // groups, sums)
                sums = empty
    for place in range(2 * own_planes):
        for block in range(blocks):
            copy_out(place, block).wait()


def shards(coeffs, rotation_matrix, stick_length, stick_column, plane_index, occupation):
    band_count = lax.axis_size("band")
    pw_count = lax.axis_size("pw")
    devices = band_count * pw_count
    in_count, sticks, grid_len = coeffs.shape[1:]
    bands = rotation_matrix.shape[2]
    stick_count = stick_column.shape[0]
    own_planes = plane_index.shape[0] // pw_count
    spots = 2 * bands
    rows = own_planes * spots
    lanes = -(-(rows + bands) // LANES) * LANES
    side = lane_groups(sticks, rows, bands, lanes)
    message_rows = sticks // side
    vmem = pl.BlockSpec(memory_space=pltpu.VMEM)
    hbm = pl.BlockSpec(memory_space=pltpu.HBM)
    table_bytes = 8 * grid_len * stick_count
    message_bytes = 2 * stick_count * lanes

    messages = pl.pallas_call(
        stick_kernel,
        out_shape=jax.ShapeDtypeStruct((devices, message_rows, lanes), jnp.bfloat16),
        in_specs=[hbm] * 5,
        out_specs=hbm,
        scratch_shapes=[
            pltpu.SMEM(stick_length.shape, jnp.int32),
            pltpu.SMEM(plane_index.shape, jnp.int32),
            pltpu.SMEM(occupation.shape, jnp.int32),
            pltpu.VMEM((2, bands, in_count), jnp.bfloat16),
            pltpu.VMEM((2 * in_count * sticks, grid_len), jnp.bfloat16),
            pltpu.VMEM((pw_count, message_rows, lanes), jnp.bfloat16),
            pltpu.SemaphoreType.DMA((max(4 + COEFF_COPIES, band_count),)),
        ],
        compiler_params=room(2 * message_bytes),
        name="stick_values",
    )(
        *(
            pltpu.with_memory_space_constraint(array, pltpu.HBM)
            for array in (
                stick_length,
                plane_index,
                occupation,
                jnp.swapaxes(rotation_matrix, 1, 2),
                coeffs.reshape(2 * in_count * sticks, grid_len),
            )
        )
    )
    arrived = lax.all_to_all(messages, ("band", "pw"), split_axis=0, concat_axis=0, tiled=True)
    left, right = pl.pallas_call(
        functools.partial(table_kernel, grid_len, min(grid_len, stick_count), sticks, side),
        out_shape=(
            jax.ShapeDtypeStruct((2, grid_len // 2, stick_count), jnp.bfloat16),
            jax.ShapeDtypeStruct((stick_count, 2 * grid_len), jnp.bfloat16),
        ),
        in_specs=[hbm],
        out_specs=(vmem, vmem),
        scratch_shapes=[pltpu.VMEM((1, stick_count), jnp.int32), pltpu.SemaphoreType.DMA],
        compiler_params=room(table_bytes),
        cost_estimate=pl.CostEstimate(
            flops=80 * grid_len * stick_count,
            bytes_accessed=12 * grid_len * stick_count,
            transcendentals=0,
        ),
        name="stick_tables",
    )(pltpu.with_memory_space_constraint(stick_column.reshape(1, stick_count), pltpu.HBM))
    norm_factor = 1.0 / float(bands * stick_count * grid_len)
    blocks = 2 * own_planes * (grid_len // 2 // row_block(grid_len))
    return pl.pallas_call(
        functools.partial(plane_kernel, bands, own_planes, norm_factor, sticks),
        out_shape=jax.ShapeDtypeStruct((own_planes, grid_len, grid_len), jnp.float32),
        in_specs=[vmem] * 3,
        out_specs=hbm,
        scratch_shapes=[
            pltpu.VMEM((rows, PACK, stick_count), jnp.bfloat16),
            pltpu.VMEM((own_planes, grid_len, grid_len), jnp.float32),
            pltpu.SemaphoreType.DMA((blocks,)),
        ],
        compiler_params=room(table_bytes, message_bytes),
        name="plane_density",
    )(arrived, left, right)


def solution(mesh):
    return jax.shard_map(
        shards,
        mesh=mesh,
        in_specs=(P(None, None, ("band", "pw"), None), P(), P(), P(), P(), P("band")),
        out_specs=P("pw", None, None),
        check_vma=False,
    )
```
